256 devices in a mesh: rep: 2 (over y_hi), brick: 128 (over x, y_lo, z, core).
Axes of the slice: x: 4, y: 4 (y_hi: 2, y_lo: 2; y = y_hi * 2 + y_lo), z: 8, core: 2. Of those that a mesh axis runs over, the one named last changes fastest.
Arguments:
- noisy: bfloat16 [2, 128, 32, 256], P(None, 'brick'), may hold values from -6 to 6
- w2_in: bfloat16 [16, 1, 3, 3], replicated, may hold values from -3 to 3
- w2_mid: bfloat16 [16, 16, 3, 3], replicated, may hold values from -0.75 to 0.75
- w2_low: bfloat16 [16, 16, 3, 3], replicated, may hold values from -0.75 to 0.75
- w2_deep: bfloat16 [16, 16, 3, 3], replicated, may hold values from -0.75 to 0.75
- w2_up: bfloat16 [16, 32, 3, 3], replicated, may hold values from -0.5 to 0.5
- w2_out: bfloat16 [1, 16], replicated, may hold values from -2 to 2
- w3_in: bfloat16 [8, 1, 3, 3, 3], replicated, may hold values from -1.75 to 1.75
- w3_mid: bfloat16 [8, 8, 3, 3, 3], replicated, may hold values from -0.625 to 0.625
- w3_low: bfloat16 [8, 8, 3, 3, 3], replicated, may hold values from -0.625 to 0.625
- w3_up: bfloat16 [8, 16, 3, 3, 3], replicated, may hold values from -0.4375 to 0.4375
- w3_out: bfloat16 [8, 8], replicated, may hold values from -3 to 3
Outputs:
- organelle_logits: float32 [128, 8, 4, 32, 128], P('brick', 'rep')
The draws below stay inside these ranges and needn't reach their ends.
All inputs are finite; a program needn't handle non-finite values.
Results may differ from the reference program's by a relative error of at most 0.025.
Values may be sent and summed in bfloat16 or wider, within the bound.
No kernel may reach another device: no remote copies, remote signals or barrier semaphores. Data moves between devices by JAX's collectives and lax.ppermute only.
A program may use at most 64 MiB of HBM per device.

```python
import jax
import jax.numpy as jnp
from jax import lax

C2 = 16
C3 = 8
K = 8
GY = 8
BX = 4
BY = 32
GX = 8
P_SIZE = 128
X = 32
Y = 256
Z = 256
BRICKS = 128


def block_scale(stream_key, dims, shards, least, top_value):
    loudness, own = 1.0, jax.random.fold_in(stream_key, 6)
    for axis_at, parts in shards:
        steps = jnp.exp(jax.random.uniform(jax.random.fold_in(own, axis_at), (parts,), jnp.float32, least / len(shards), top_value / len(shards)))
        loudness = loudness * jnp.repeat(steps, dims[axis_at] // parts).reshape([-1 if axis == axis_at else 1 for axis in range(len(dims))])
    return loudness


def noise(key, extent, spread, limit, pieces=(), kind=jnp.bfloat16):
    drawn = spread * jax.random.normal(key, extent, jnp.float32)
    if pieces:
        drawn = drawn * block_scale(key, extent, pieces, -0.22, 0.18)
    return jnp.clip(drawn, -limit, limit).astype(kind)


def setup_inputs(seed: int = 0) -> dict:
    splits = jax.random.split(jax.random.key(seed), 13)
    noisy = noise(splits[0], (2, P_SIZE, X, Y), 1.0, 6.0, ((1, 128),))
    w2_in = noise(splits[1], (C2, 1, 3, 3), (9 // 2) ** -0.5, 3.0)
    w2_mid = noise(splits[2], (C2, C2, 3, 3), (9 * C2 // 2) ** -0.5, 0.75)
    w2_low = noise(splits[3], (C2, C2, 3, 3), (9 * C2 // 2) ** -0.5, 0.75)
    w2_deep = noise(splits[4], (C2, C2, 3, 3), (9 * C2 // 2) ** -0.5, 0.75)
    w2_up = noise(splits[5], (C2, 2 * C2, 3, 3), (9 * C2) ** -0.5, 0.5)
    w2_out = noise(splits[6], (1, C2), (C2 // 2) ** -0.5, 2.0)
    w3_in = noise(splits[7], (C3, 1, 3, 3, 3), (27 // 2) ** -0.5, 1.75)
    w3_mid = noise(splits[8], (C3, C3, 3, 3, 3), (27 * C3 // 2) ** -0.5, 0.625)
    w3_low = noise(splits[9], (C3, C3, 3, 3, 3), (27 * C3 // 2) ** -0.5, 0.625)
    w3_up = noise(splits[10], (C3, 2 * C3, 3, 3, 3), (27 * C3) ** -0.5, 0.4375)
    w3_out = noise(splits[11], (K, C3), (C3 // 2) ** -0.5, 3.0)
    return dict(noisy=noisy, w2_in=w2_in, w2_mid=w2_mid, w2_low=w2_low, w2_deep=w2_deep, w2_up=w2_up, w2_out=w2_out, w3_in=w3_in, w3_mid=w3_mid, w3_low=w3_low, w3_up=w3_up, w3_out=w3_out)


def conv_plane(x, w):
    return lax.conv_general_dilated(x.astype(jnp.float32), w.astype(jnp.float32), (1, 1), "SAME", dimension_numbers=("NCHW", "OIHW", "NCHW"), precision=lax.Precision.HIGHEST)


def conv_cube(x, w):
    return lax.conv_general_dilated(x.astype(jnp.float32), w.astype(jnp.float32), (1, 1, 1), "SAME", dimension_numbers=("NCDHW", "OIDHW", "NCDHW"), precision=lax.Precision.HIGHEST)


def relu_cast(v):
    return jnp.maximum(v, 0.0).astype(jnp.bfloat16)


def pool_plane(x):
    n, c, a, b = x.shape
    return x.astype(jnp.float32).reshape(n, c, a // 2, 2, b // 2, 2).mean(axis=(3, 5)).astype(jnp.bfloat16)


def pool_cube(x):
    n, c, a, b, d = x.shape
    return x.astype(jnp.float32).reshape(n, c, a // 2, 2, b // 2, 2, d // 2, 2).mean(axis=(3, 5, 7)).astype(jnp.bfloat16)


def denoise(planes, w2_in, w2_mid, w2_low, w2_deep, w2_up, w2_out):
    first = relu_cast(conv_plane(planes, w2_in))
    skip = relu_cast(conv_plane(first, w2_mid))
    low = relu_cast(conv_plane(pool_plane(skip), w2_low))
    deep = relu_cast(conv_plane(low, w2_deep))
    upper = jnp.repeat(jnp.repeat(deep, 2, axis=2), 2, axis=3)
    joined = relu_cast(conv_plane(jnp.concatenate([skip, upper], axis=1), w2_up))
    return jnp.einsum("oc,nchw->nohw", w2_out.astype(jnp.float32), joined.astype(jnp.float32), precision=lax.Precision.HIGHEST).astype(jnp.bfloat16)


def segment(volume, w3_in, w3_mid, w3_low, w3_up, w3_out):
    first = relu_cast(conv_cube(volume, w3_in))
    skip = relu_cast(conv_cube(first, w3_mid))
    low = relu_cast(conv_cube(pool_cube(skip), w3_low))
    upper = jnp.repeat(jnp.repeat(jnp.repeat(low, 2, axis=2), 2, axis=3), 2, axis=4)
    joined = relu_cast(conv_cube(jnp.concatenate([skip, upper], axis=1), w3_up))
    return jnp.einsum("kc,ncxyz->nkxyz", w3_out.astype(jnp.float32), joined.astype(jnp.float32), precision=lax.Precision.HIGHEST).astype(jnp.bfloat16)[0]


def reference(noisy, w2_in, w2_mid, w2_low, w2_deep, w2_up, w2_out, w3_in, w3_mid, w3_low, w3_up, w3_out):
    grouped = jnp.transpose(noisy, (1, 0, 2, 3)).reshape(P_SIZE, 2, 1, X, Y)
    cleaned = lax.map(lambda g: denoise(g, w2_in, w2_mid, w2_low, w2_deep, w2_up, w2_out), grouped)
    volume = jnp.transpose(cleaned[:, :, 0], (2, 3, 1, 0)).reshape(X, Y, Z)
    plain = segment(volume[None, None], w3_in, w3_mid, w3_low, w3_up, w3_out)
    mirrored = segment(volume[::-1][None, None], w3_in, w3_mid, w3_low, w3_up, w3_out)
    mean_logits = (plain.astype(jnp.float32) + mirrored[:, ::-1].astype(jnp.float32)) * 0.5
    blocks = mean_logits.reshape(K, GX, BX, GY, BY, 2, P_SIZE)
    return jnp.transpose(blocks, (1, 3, 5, 0, 2, 4, 6)).reshape(BRICKS, K, BX, BY, P_SIZE)
```

```python
import jax
import jax.numpy as jnp
from jax import lax
from jax.experimental import pallas as pl
from jax.experimental.pallas import tpu as pltpu
from jax.sharding import Mesh
from jax.sharding import PartitionSpec as P

BF = jnp.bfloat16
F32 = jnp.float32
NI, NZ, NC = 8, 8, 2
VMEM_BYTES = 56 * 1024 * 1024


def iota(shape, dim):
    return lax.broadcasted_iota(jnp.int32, shape, dim)


def nn(a, b):
    return lax.dot_general(a, b, (((1,), (0,)), ((), ())), preferred_element_type=F32)


def nt(a, b):
    return lax.dot_general(a, b, (((1,), (1,)), ((), ())), preferred_element_type=F32)


def lane_spread(rows, channels, first, lanes):
    return (iota((rows, lanes), 1) % channels + first == iota((rows, lanes), 0)).astype(
        F32
    ).astype(BF)


def stacked(taps, at, channels):
    return jnp.concatenate([taps[at * channels : (at + 1) * channels]] * (128 // channels), axis=0)


def same_level(ref, lead, at, blocks, taps, channels):
    cells = 128 // channels
    gap = iota((128, 128), 1) // channels - iota((128, 128), 0) // channels
    zero = jnp.zeros((128, 128), F32)
    own = jnp.where(
        gap == 0, taps[1], jnp.where(gap == -1, taps[0], jnp.where(gap == 1, taps[2], zero))
    ).astype(BF)
    if blocks > 1:
        later = jnp.where(gap == 1 - cells, taps[2], zero).astype(BF)
        earlier = jnp.where(gap == cells - 1, taps[0], zero).astype(BF)
    for out in range(blocks):
        for inp in range(blocks):
            if inp == out:
                block = own
            elif inp == out + 1:
                block = later
            elif inp == out - 1:
                block = earlier
            else:
                block = jnp.zeros((128, 128), BF)
            ref[lead + (pl.ds(out * 128, 128), pl.ds(at + inp * 128, 128))] = block


def from_coarse(ref, lead, at, out_blocks, in_blocks, taps, channels):
    cells = 128 // channels
    lane_cell = iota((128, 128), 1) // channels
    row_cell = iota((128, 128), 0) // channels
    zero = jnp.zeros((128, 128), F32)
    for out in range(out_blocks):
        for inp in range(in_blocks):
            total = zero
            for kx in range(3):
                meets = (row_cell + (out * cells + kx - 1)) >> 1 == lane_cell + inp * cells
                total = total + jnp.where(meets, taps[kx], zero)
            ref[lead + (pl.ds(out * 128, 128), pl.ds(at + inp * 128, 128))] = total.astype(BF)


def pool_matrix(channels, half):
    cells = 128 // channels
    lane, row = iota((128, 128), 1), iota((128, 128), 0)
    meets = ((lane // channels + half * cells) >> 1 == row // channels) & (
        lane % channels == row % channels
    )
    return meets.astype(F32).astype(BF)


def rolled(v, steps):
    return pltpu.roll(v, steps % v.shape[0], 0)


def denoise_kernel(
    planes_ref,
    w_in_ref,
    w_mid_ref,
    w_low_ref,
    w_deep_ref,
    w_up_ref,
    w_out_ref,
    out_ref,
    b_in,
    b_mid,
    b_low,
    b_deep,
    b_up,
    b_pool,
    lhs,
    wide,
    coarse,
    half,
    raised,
    vol,
):
    planes = planes_ref.shape[0]
    rows = planes * 256
    low_rows = planes * 128
    w9 = nn(w_in_ref[...], lane_spread(16, 16, 0, 512))
    xi = iota((32, 512), 0)
    xo = iota((32, 512), 1) // 16
    for ky in range(3):
        total = jnp.zeros((32, 512), F32)
        for kx in range(3):
            total = jnp.where(xi == xo + (kx - 1), w9[kx * 3 + ky : kx * 3 + ky + 1], total)
        b_in[ky * 32 : (ky + 1) * 32] = total.astype(BF)
    b_in[96:128] = jnp.zeros((32, 512), BF)
    spread = lane_spread(16, 16, 0, 128)
    for w_ref, b_ref, blocks in ((w_mid_ref, b_mid, 4), (w_low_ref, b_low, 2), (w_deep_ref, b_deep, 2)):
        w = nn(w_ref[...], spread)
        for ky in range(3):
            taps = [stacked(w, kx * 3 + ky, 16) for kx in range(3)]
            same_level(b_ref, (), ky * blocks * 128, blocks, taps, 16)
    w_skip = nn(w_up_ref[...], lane_spread(32, 16, 0, 128))
    w_rise = nn(w_up_ref[...], lane_spread(32, 16, 16, 128))
    for ky in range(3):
        taps = [stacked(w_skip, kx * 3 + ky, 16) for kx in range(3)]
        same_level(b_up, (), ky * 512, 4, taps, 16)
        taps = [stacked(w_rise, kx * 3 + ky, 16) for kx in range(3)]
        from_coarse(b_up, (), 1536 + ky * 256, 4, 2, taps, 16)
    none = jnp.zeros((128, 128), BF)
    for out in range(2):
        for inp in range(4):
            b_pool[out * 128 : (out + 1) * 128, inp * 128 : (inp + 1) * 128] = (
                pool_matrix(16, inp % 2) if inp // 2 == out else none
            )

    def place(ref, at, width, v, length):
        n = v.shape[0]
        row = iota(v.shape, 0) % length
        ref[:n, at : at + width] = jnp.where(row == 0, 0.0, rolled(v, 1)).astype(BF)
        ref[:n, at + width : at + 2 * width] = v.astype(BF)
        ref[:n, at + 2 * width : at + 3 * width] = jnp.where(
            row == length - 1, 0.0, rolled(v, -1)
        ).astype(BF)

    turned = planes_ref[...].astype(F32).reshape(planes * 32, 256).T
    if planes < 4:
        turned = jnp.concatenate([turned, jnp.zeros((256, 128 - planes * 32), F32)], axis=1)
    row = iota((256, 128), 0)
    lane = iota((256, 128), 1)
    before = jnp.where(row == 0, 0.0, rolled(turned, 1))
    after = jnp.where(row == 255, 0.0, rolled(turned, -1))
    for q in range(planes):
        three = jnp.zeros((256, 128), F32)
        for g, v in enumerate((before, turned, after)):
            three = jnp.where(lane // 32 == g, pltpu.roll(v, ((g - q) * 32) % 128, 1), three)
        first = jnp.maximum(nn(three.astype(BF), b_in[...]), 0.0)
        place(lhs.at[q * 256 : (q + 1) * 256], 0, 512, first, 256)
    skip = jnp.maximum(nt(lhs[...], b_mid[...]), 0.0)
    place(wide, 0, 512, skip, 256)
    fine = nt(skip.astype(BF), b_pool[...])
    for c in range(2):
        half[...] = fine[:, c * 128 : (c + 1) * 128]
        coarse[:, c * 128 : (c + 1) * 128] = 0.25 * (
            half[pl.ds(0, low_rows, stride=2), :] + half[pl.ds(1, low_rows, stride=2), :]
        )
    place(lhs.at[:low_rows], 0, 256, coarse[...], 128)
    low = jnp.maximum(nt(lhs[:low_rows, :768], b_low[...]), 0.0)
    place(lhs.at[:low_rows], 768, 256, low, 128)
    deep = jnp.maximum(nt(lhs[:low_rows, 768:1536], b_deep[...]), 0.0)
    for c in range(2):
        part = deep[:, c * 128 : (c + 1) * 128]
        half[pl.ds(0, low_rows, stride=2), :] = part
        half[pl.ds(1, low_rows, stride=2), :] = part
        raised[:, c * 128 : (c + 1) * 128] = half[...]
    place(wide, 1536, 256, raised[...], 256)
    joined = jnp.maximum(nt(wide[...], b_up[...]), 0.0).astype(BF)
    w_row = nn(w_out_ref[...], lane_spread(16, 16, 0, 512))
    to_lane, cell = iota((128, 512), 0), iota((128, 512), 1) // 16
    total = jnp.zeros((256, 128), F32)
    for q in range(planes):
        b_out = jnp.where(to_lane == q * 32 + cell, w_row, 0.0).astype(BF)
        total = total + nt(joined[q * 256 : (q + 1) * 256], b_out)
    vol[0:8] = jnp.zeros((8, 128), F32)
    vol[264:272] = jnp.zeros((8, 128), F32)
    vol[8:264] = total
    for z in range(NZ):
        out_ref[z] = vol[z * 32 : z * 32 + 48].astype(BF)


def segment_kernel(
    v_ref,
    w_in_ref,
    w_mid_ref,
    w_low_ref,
    w_up_ref,
    w_out_ref,
    out_ref,
    b_in,
    b_mid,
    b_low,
    b_up,
    vz,
    vl,
    h1l,
    pool,
    ql,
    rise,
    l4,
):
    rep, at_i, at_z, at_c = (lax.axis_index(name) for name in ("rep", "i", "z", "c"))
    w27 = nn(w_in_ref[...], lane_spread(8, 8, 0, 256))
    xi = iota((32, 256), 0)
    xo = iota((32, 256), 1) // 8
    for ky in range(3):
        for kz in range(3):
            plain = jnp.zeros((32, 256), F32)
            mirror = jnp.zeros((32, 256), F32)
            for kx in range(3):
                tap = (kx * 3 + ky) * 3 + kz
                plain = jnp.where(xi == xo + (kx - 1), w27[tap : tap + 1], plain)
                mirror = jnp.where(xi == (32 - kx) - xo, w27[tap : tap + 1], mirror)
            at = ky * 128 + kz * 32
            b_in[at : at + 32, :256] = plain.astype(BF)
            b_in[at : at + 32, 256:] = mirror.astype(BF)
        b_in[ky * 128 + 96 : ky * 128 + 128] = jnp.zeros((32, 512), BF)
    spread = lane_spread(8, 8, 0, 128)
    w_mid = nn(w_mid_ref[...], spread)
    w_low = nn(w_low_ref[...], spread)
    w_skip = nn(w_up_ref[...], lane_spread(16, 8, 0, 128))
    w_rise = nn(w_up_ref[...], lane_spread(16, 8, 8, 128))
    for ky in range(3):
        for kz in range(3):
            for w, b_ref, at, blocks in (
                (w_mid, b_mid, kz * 256, 2),
                (w_low, b_low, kz * 128, 1),
                (w_skip, b_up, kz * 256, 2),
            ):
                taps = [stacked(w, (kx * 3 + ky) * 3 + kz, 8) for kx in range(3)]
                same_level(b_ref, (ky,), at, blocks, taps, 8)
            taps = [stacked(w_rise, (kx * 3 + ky) * 3 + kz, 8) for kx in range(3)]
            from_coarse(b_up, (ky,), 768 + kz * 128, 2, 1, taps, 8)

    out_lane = iota((128, 512), 1)
    select = (
        (iota((128, 512), 0) == (out_lane // 128) * 32 + out_lane % 32) & (out_lane % 128 < 96)
    ).astype(F32).astype(BF)
    vz[...] = jnp.zeros(vz.shape, F32)
    for src in range(NZ):
        spread_v = nn(v_ref[src], select)
        for q in range(4):
            z_row = 8 + 2 * src + q
            if q >= 2:
                if src >= 5:
                    z_row = 2 * src + (q - 2) - 8
                elif src <= 2:
                    z_row = 24 + 2 * src + (q - 2)
                else:
                    continue
            vz[pl.ds(z_row, 48, stride=32), :] = spread_v[:, q * 128 : (q + 1) * 128]
    v = vz[...]
    lane = iota(v.shape, 1)
    v = jnp.where(lane < 32, rolled(v, 1), jnp.where(lane < 64, v, rolled(v, -1)))
    v = v.astype(BF).reshape(48, 32, 128)
    for ky in range(3):
        vl[:, :, ky * 128 : (ky + 1) * 128] = v[2 + ky : 44 + ky]

    z_base = 128 * at_c + 16 * at_i - 8
    y_base = 32 * at_z

    def inside(y_count, y_first, z_count, z_first, limit_y, limit_z):
        r = iota((y_count * z_count, 128), 0)
        y = r // z_count + y_first
        z = r % z_count + z_first
        return ((y >= 0) & (y < limit_y) & (z >= 0) & (z < limit_z)).astype(F32)

    def masked(v, mask):
        return jnp.maximum(v, 0.0) * jnp.concatenate([mask] * (v.shape[1] // 128), axis=1)

    part = 14
    for step in range(3):
        y0 = step * part
        n = part * 32
        h1 = nn(vl[y0 : y0 + part].reshape(n, 384), b_in[...])
        mask = inside(part, y_base - 5 + y0, 32, z_base, 256, 256)
        for copy in range(2):
            h = masked(h1[:, copy * 256 : (copy + 1) * 256], mask)
            for kz, steps in enumerate((1, 0, -1)):
                moved = rolled(h, steps) if steps else h
                h1l[copy, y0 : y0 + part, :, kz * 256 : (kz + 1) * 256] = moved.astype(BF).reshape(
                    part, 32, 256
                )

    pool_t = jnp.concatenate([pool_matrix(8, 0), pool_matrix(8, 1)], axis=1)
    lane_r = iota((128, 256), 1)
    row_r = iota((128, 256), 0)
    w_out = nn(w_out_ref[...], lane_spread(8, 8, 0, 256)).astype(BF)
    pick = (iota((128, 8), 1) == (iota((128, 8), 0) // 4) % 4 + 4 * rep).astype(F32).astype(BF)
    w_rows = nn(pick, w_out)
    x_row = (row_r // 16) * 4 + row_r % 4
    logits = jnp.zeros((128, 512), F32)
    for copy in range(2):
        part = 20
        n = part * 32
        for step in range(2):
            y0 = step * part
            acc = jnp.zeros((n, 256), F32)
            for ky in range(3):
                acc = acc + nt(h1l[copy, y0 + ky : y0 + ky + part].reshape(n, 768), b_mid[ky])
            h2 = masked(acc, inside(part, y_base - 4 + y0, 32, z_base, 256, 256))
            fine = nt(h2.astype(BF), pool_t).reshape(part // 2, 2, 32, 128)
            pool[y0 * 16 : y0 * 16 + n // 2] = (fine[:, 0] + fine[:, 1]).reshape(n // 2, 128)
            first, last = max(y0, 3), min(y0 + part, 37)
            for kz in range(3):
                moved = rolled(h2, -(7 + kz)).reshape(part, 32, 256)
                l4[copy, first - 3 : last - 3, :, kz * 256 : (kz + 1) * 256] = moved[
                    first - y0 : last - y0, :16
                ].astype(BF)
        q = 0.125 * (pool[pl.ds(0, 320, stride=2), :] + pool[pl.ds(1, 320, stride=2), :])
        for kz, steps in enumerate((1, 0, -1)):
            moved = rolled(q, steps) if steps else q
            ql[:, :, kz * 128 : (kz + 1) * 128] = moved.astype(BF).reshape(20, 16, 128)
        acc = jnp.zeros((288, 128), F32)
        for ky in range(3):
            acc = acc + nt(ql[ky : ky + 18].reshape(288, 384), b_low[ky])
        h3 = masked(
            acc, inside(18, 16 * at_z - 1, 16, 64 * at_c + 8 * at_i - 4, 128, 128)
        )
        rise[pl.ds(0, 288, stride=2), :] = h3
        rise[pl.ds(1, 288, stride=2), :] = h3
        r = rise[...]
        for kz in range(3):
            moved = rolled(r, -(7 + kz)).reshape(18, 32, 128)[:, :16].astype(BF)
            for slot in range(34):
                l4[copy, slot, :, 768 + kz * 128 : 896 + kz * 128] = moved[(slot + 3) // 2 - 1]
        acc = jnp.zeros((512, 256), F32)
        for ky in range(3):
            acc = acc + nt(l4[copy, ky : ky + 32].reshape(512, 1152), b_up[ky])
        h4 = jnp.maximum(acc, 0.0).astype(BF)
        x_lane = lane_r // 8 if copy == 0 else 31 - lane_r // 8
        b_out = jnp.where(x_lane == x_row, w_rows, 0.0).astype(BF)
        logits = logits + nt(b_out, h4)
    out_ref[...] = (0.5 * logits).astype(BF).reshape(NI, 16, 512)


def arrange_kernel(parts_ref, out_ref):
    lane = iota((16, 128), 1) // 16
    for o in range(4):
        parts = [parts_ref[src, :, o * 128 : (o + 1) * 128].astype(F32) for src in range(NI)]
        for y in range(8):
            total = jnp.zeros((16, 128), F32)
            for src in range(NI):
                moved = parts[src]
                if src != y:
                    moved = pltpu.roll(moved, ((src - y) * 16) % 128, 1)
                total = jnp.where(lane == src, moved, total)
            out_ref[pl.ds(o * 8 + y, 16, stride=32), :] = total


def call(kernel, out_shape, scratch, *args):
    return pl.pallas_call(
        kernel,
        out_shape=out_shape,
        in_specs=[pl.BlockSpec(memory_space=pltpu.VMEM)] * len(args),
        out_specs=pl.BlockSpec(memory_space=pltpu.VMEM),
        scratch_shapes=scratch,
        compiler_params=pltpu.CompilerParams(vmem_limit_bytes=VMEM_BYTES),
    )(*args)


def flat2(w):
    return w.transpose(2, 3, 0, 1).reshape(-1, w.shape[1])


def flat3(w):
    return w.transpose(2, 3, 4, 0, 1).reshape(-1, w.shape[1])


def rim_pairs():
    pairs = []

    def index(i, z, c):
        return (i * NZ + z) * NC + c

    for c in range(NC):
        for z in range(NZ):
            for i in range(NI):
                if z >= 5:
                    if i < NI - 1:
                        pairs.append((index(i, z, c), index(i + 1, z, c)))
                    elif c == 0:
                        pairs.append((index(i, z, 0), index(0, z, 1)))
                if z <= 2:
                    if i > 0:
                        pairs.append((index(i, z, c), index(i - 1, z, c)))
                    elif c == 1:
                        pairs.append((index(i, z, 1), index(NI - 1, z, 0)))
    return pairs


def per_device(
    noisy, w2_in, w2_mid, w2_low, w2_deep, w2_up, w2_out, w3_in, w3_mid, w3_low, w3_up, w3_out
):
    second = lax.axis_index("c") == 1
    low_half, high_half = noisy[0, 0], noisy[1, 0]
    sent = jnp.where(second, low_half, high_half)
    got = lax.ppermute(sent, "c", [(0, 1), (1, 0)])
    own = jnp.stack([jnp.where(second, got, low_half), jnp.where(second, high_half, got)])
    rim = lax.ppermute(own, ("i", "z", "c"), rim_pairs())
    planes = jnp.concatenate([own, rim], axis=0)
    count = planes.shape[0]
    vmem = pltpu.VMEM
    volume = call(
        denoise_kernel,
        jax.ShapeDtypeStruct((NZ, 48, 128), BF),
        [
            vmem((128, 512), BF),
            vmem((512, 1536), BF),
            vmem((256, 768), BF),
            vmem((256, 768), BF),
            vmem((512, 2304), BF),
            vmem((256, 512), BF),
            vmem((count * 256, 1536), BF),
            vmem((count * 256, 2304), BF),
            vmem((count * 128, 256), F32),
            vmem((count * 256, 128), F32),
            vmem((count * 256, 256), F32),
            vmem((272, 128), F32),
        ],
        planes,
        w2_in.transpose(2, 3, 1, 0).reshape(9, 16),
        flat2(w2_mid),
        flat2(w2_low),
        flat2(w2_deep),
        flat2(w2_up),
        w2_out,
    )
    window = lax.all_to_all(volume, "z", 0, 0, tiled=True)
    logits = call(
        segment_kernel,
        jax.ShapeDtypeStruct((NI, 16, 512), BF),
        [
            vmem((384, 512), BF),
            vmem((3, 256, 768), BF),
            vmem((3, 128, 384), BF),
            vmem((3, 256, 1152), BF),
            vmem((48 * 32, 128), F32),
            vmem((42, 32, 384), BF),
            vmem((2, 42, 32, 768), BF),
            vmem((640, 128), F32),
            vmem((20, 16, 384), BF),
            vmem((576, 128), F32),
            vmem((2, 34, 16, 1152), BF),
        ],
        window,
        w3_in.transpose(2, 3, 4, 1, 0).reshape(27, 8),
        flat3(w3_mid),
        flat3(w3_low),
        flat3(w3_up),
        w3_out,
    )
    parts = lax.all_to_all(logits, "i", 0, 0, tiled=True)
    out = call(arrange_kernel, jax.ShapeDtypeStruct((512, 128), F32), [], parts)
    return out.reshape(1, 4, 4, 32, 128)


def solution(mesh):
    finer = Mesh(mesh.devices.reshape(2, NI, NZ, NC), ("rep", "i", "z", "c"))
    brick = ("i", "z", "c")
    placed = (P(None, brick, None, None),) + (P(),) * 11
    return jax.shard_map(
        per_device,
        mesh=finer,
        in_specs=placed,
        out_specs=P(brick, "rep", None, None, None),
        check_vma=False,
    )
```

```python
import functools

import jax
import jax.numpy as jnp
from jax import lax
from jax.experimental import pallas as pl
from jax.experimental.pallas import tpu as pltpu
from jax.sharding import Mesh
from jax.sharding import PartitionSpec as P

BF = jnp.bfloat16
F32 = jnp.float32
NI, NZ, NC = 8, 8, 2


def iota(shape, dim):
    return lax.broadcasted_iota(jnp.int32, shape, dim)


def nn(a, b):
    return lax.dot_general(a, b, (((1,), (0,)), ((), ())), preferred_element_type=F32)


def nt(a, b):
    return lax.dot_general(a, b, (((1,), (1,)), ((), ())), preferred_element_type=F32)


def lane_spread(rows, channels, first, lanes):
    return (iota((rows, lanes), 1) % channels + first == iota((rows, lanes), 0)).astype(
        F32
    ).astype(BF)


def stacked(taps, at, channels):
    return jnp.concatenate([taps[at * channels : (at + 1) * channels]] * (128 // channels), axis=0)


def same_level(ref, lead, at, blocks, taps, channels):
    cells = 128 // channels
    gap = iota((128, 128), 1) // channels - iota((128, 128), 0) // channels
    zero = jnp.zeros((128, 128), F32)
    own = jnp.where(
        gap == 0, taps[1], jnp.where(gap == -1, taps[0], jnp.where(gap == 1, taps[2], zero))
    ).astype(BF)
    if blocks > 1:
        later = jnp.where(gap == 1 - cells, taps[2], zero).astype(BF)
        earlier = jnp.where(gap == cells - 1, taps[0], zero).astype(BF)
    for out in range(blocks):
        for inp in range(blocks):
            if inp == out:
                block = own
            elif inp == out + 1:
                block = later
            elif inp == out - 1:
                block = earlier
            else:
                block = jnp.zeros((128, 128), BF)
            ref[lead + (pl.ds(out * 128, 128), pl.ds(at + inp * 128, 128))] = block


def from_coarse(ref, lead, at, out_blocks, in_blocks, taps, channels):
    cells = 128 // channels
    lane_cell = iota((128, 128), 1) // channels
    row_cell = iota((128, 128), 0) // channels
    zero = jnp.zeros((128, 128), F32)
    for out in range(out_blocks):
        for inp in range(in_blocks):
            total = zero
            for kx in range(3):
                meets = (row_cell + (out * cells + kx - 1)) >> 1 == lane_cell + inp * cells
                total = total + jnp.where(meets, taps[kx], zero)
            ref[lead + (pl.ds(out * 128, 128), pl.ds(at + inp * 128, 128))] = total.astype(BF)


def pool_matrix(channels, half):
    cells = 128 // channels
    lane, row = iota((128, 128), 1), iota((128, 128), 0)
    meets = ((lane // channels + half * cells) >> 1 == row // channels) & (
        lane % channels == row % channels
    )
    return meets.astype(F32).astype(BF)


def rolled(v, steps):
    return pltpu.roll(v, steps % v.shape[0], 0)


def plane_weights_kernel(w_ref, b_in, b_mid, b_low, b_deep, b_up, b_pool, b_last):
    w_mid_ref, w_low_ref, w_deep_ref, w_up_ref = (
        w_ref.at[at * 144 : (at + 1) * 144] for at in range(4)
    )
    edge = nn(w_ref[576:640], lane_spread(32, 16, 0, 512))
    w9, w_row = [edge[kx * 16 : kx * 16 + 3] for kx in range(3)], edge[48:49]
    xi = iota((32, 512), 0)
    xo = iota((32, 512), 1) // 16
    for ky in range(3):
        total = jnp.zeros((32, 512), F32)
        for kx in range(3):
            total = jnp.where(xi == xo + (kx - 1), w9[kx][ky : ky + 1], total)
        b_in[ky * 32 : (ky + 1) * 32] = total.astype(BF)
    b_in[96:128] = jnp.zeros((32, 512), BF)
    spread = lane_spread(32, 16, 0, 128)
    for taps_ref, b_ref, blocks in ((w_mid_ref, b_mid, 4), (w_low_ref, b_low, 2), (w_deep_ref, b_deep, 2)):
        w = nn(taps_ref[...], spread)
        for ky in range(3):
            taps = [stacked(w, kx * 3 + ky, 16) for kx in range(3)]
            same_level(b_ref, (), ky * blocks * 128, blocks, taps, 16)
    w_skip = nn(w_up_ref[...], lane_spread(32, 16, 0, 128))
    w_rise = nn(w_up_ref[...], lane_spread(32, 16, 16, 128))
    for ky in range(3):
        taps = [stacked(w_skip, kx * 3 + ky, 16) for kx in range(3)]
        same_level(b_up, (), ky * 512, 4, taps, 16)
        taps = [stacked(w_rise, kx * 3 + ky, 16) for kx in range(3)]
        from_coarse(b_up, (), 1536 + ky * 256, 4, 2, taps, 16)
    none = jnp.zeros((128, 128), BF)
    for out in range(2):
        for inp in range(4):
            b_pool[out * 128 : (out + 1) * 128, inp * 128 : (inp + 1) * 128] = (
                pool_matrix(16, inp % 2) if inp // 2 == out else none
            )
    to_lane, cell = iota((128, 512), 0), iota((128, 512), 1) // 16
    for q in range(4):
        b_last[q] = jnp.where(to_lane == q * 32 + cell, w_row, 0.0).astype(BF)


def denoise_kernel(first_plane, continues, planes_ref, *refs):
    before_ref = refs[0] if continues else None
    refs = refs[continues:]
    b_in, b_mid, b_low, b_deep, b_up, b_pool, b_last, out_ref = refs[:8]
    lhs, wide, coarse, half, raised, vol = refs[8:]
    planes = planes_ref.shape[0]
    low_rows = planes * 128

    def place(ref, at, width, v, length):
        n = v.shape[0]
        row = iota(v.shape, 0) % length
        ref[:n, at : at + width] = jnp.where(row == 0, 0.0, rolled(v, 1)).astype(BF)
        ref[:n, at + width : at + 2 * width] = v.astype(BF)
        ref[:n, at + 2 * width : at + 3 * width] = jnp.where(
            row == length - 1, 0.0, rolled(v, -1)
        ).astype(BF)

    turned = planes_ref[...].astype(F32).reshape(planes * 32, 256).T
    if planes < 4:
        turned = jnp.concatenate([turned, jnp.zeros((256, 128 - planes * 32), F32)], axis=1)
    row = iota((256, 128), 0)
    lane = iota((256, 128), 1)
    before = jnp.where(row == 0, 0.0, rolled(turned, 1))
    after = jnp.where(row == 255, 0.0, rolled(turned, -1))
    for q in range(planes):
        three = jnp.zeros((256, 128), F32)
        for g, v in enumerate((before, turned, after)):
            three = jnp.where(lane // 32 == g, pltpu.roll(v, ((g - q) * 32) % 128, 1), three)
        first = jnp.maximum(nn(three.astype(BF), b_in[...]), 0.0)
        place(lhs.at[q * 256 : (q + 1) * 256], 0, 512, first, 256)
    skip = jnp.maximum(nt(lhs[...], b_mid[...]), 0.0)
    place(wide, 0, 512, skip, 256)
    fine = nt(skip.astype(BF), b_pool[...])
    for c in range(2):
        half[...] = fine[:, c * 128 : (c + 1) * 128]
        coarse[:, c * 128 : (c + 1) * 128] = 0.25 * (
            half[pl.ds(0, low_rows, stride=2), :] + half[pl.ds(1, low_rows, stride=2), :]
        )
    place(lhs.at[:low_rows], 0, 256, coarse[...], 128)
    low = jnp.maximum(nt(lhs[:low_rows, :768], b_low[...]), 0.0)
    place(lhs.at[:low_rows], 768, 256, low, 128)
    deep = jnp.maximum(nt(lhs[:low_rows, 768:1536], b_deep[...]), 0.0)
    for c in range(2):
        part = deep[:, c * 128 : (c + 1) * 128]
        half[pl.ds(0, low_rows, stride=2), :] = part
        half[pl.ds(1, low_rows, stride=2), :] = part
        raised[:, c * 128 : (c + 1) * 128] = half[...]
    place(wide, 1536, 256, raised[...], 256)
    joined = jnp.maximum(nt(wide[...], b_up[...]), 0.0).astype(BF)
    total = jnp.zeros((256, 128), F32)
    for q in range(planes):
        total = total + nt(joined[q * 256 : (q + 1) * 256], b_last[first_plane + q])
    vol[0:8] = jnp.zeros((8, 128), F32)
    vol[264:272] = jnp.zeros((8, 128), F32)
    vol[8:264] = total
    for z in range(NZ):
        window = vol[z * 32 : z * 32 + 48]
        if before_ref is not None:
            window = window + before_ref[z].astype(F32)
        out_ref[z] = window.astype(BF)


def volume_weights_kernel(w_ref, b_rest, b_mid, b_up):
    edge = nn(w_ref[648:800], lane_spread(16, 8, 0, 256))
    spread = lane_spread(16, 8, 0, 128)
    w_mid, w_low, w_skip = (nn(w_ref[at * 216 : (at + 1) * 216], spread) for at in range(3))
    w_rise = nn(w_ref[432:648], lane_spread(16, 8, 8, 128))
    xi = iota((32, 256), 0)
    xo = iota((32, 256), 1) // 8
    for ky in range(3):
        for kz in range(3):
            plain = jnp.zeros((32, 256), F32)
            mirror = jnp.zeros((32, 256), F32)
            for kx in range(3):
                at = (kx * 3 + ky) * 16 + kz
                tap = edge[at : at + 1]
                plain = jnp.where(xi == xo + (kx - 1), tap, plain)
                mirror = jnp.where(xi == (32 - kx) - xo, tap, mirror)
            at = ky * 128 + kz * 32
            b_rest[at : at + 32, :256] = plain.astype(BF)
            b_rest[at : at + 32, 256:512] = mirror.astype(BF)
        b_rest[ky * 128 + 96 : ky * 128 + 128, :512] = jnp.zeros((32, 512), BF)
    for ky in range(3):
        for kz in range(3):
            for w, b_ref, at, blocks in (
                (w_mid, b_mid.at[ky], kz * 256, 2),
                (w_low, b_rest.at[ky * 128 : ky * 128 + 128], 512 + kz * 128, 1),
                (w_skip, b_up.at[ky], kz * 256, 2),
            ):
                taps = [stacked(w, (kx * 3 + ky) * 3 + kz, 8) for kx in range(3)]
                same_level(b_ref, (), at, blocks, taps, 8)
            taps = [stacked(w_rise, (kx * 3 + ky) * 3 + kz, 8) for kx in range(3)]
            from_coarse(b_up, (ky,), 768 + kz * 128, 2, 1, taps, 8)
    w_out = edge[144:152].astype(BF)
    row_r = iota((128, 256), 0)
    cell = iota((128, 256), 1) // 8
    pick = (iota((128, 8), 1) == (iota((128, 8), 0) // 4) % 4 + 4 * lax.axis_index("rep"))
    w_rows = nn(pick.astype(F32).astype(BF), w_out)
    x_row = (row_r // 16) * 4 + row_r % 4
    b_rest[:128, 896:] = jnp.where(cell == x_row, w_rows, 0.0).astype(BF)
    b_rest[128:256, 896:] = jnp.where(31 - cell == x_row, w_rows, 0.0).astype(BF)


def segment_kernel(v_ref, b_rest, b_mid, b_up, out_ref, vz, vl, h1l, pool, ql, rise, l4):
    at_i, at_z, at_c = (lax.axis_index(name) for name in ("i", "z", "c"))
    out_lane = iota((128, 512), 1)
    select = (
        (iota((128, 512), 0) == (out_lane // 128) * 32 + out_lane % 32) & (out_lane % 128 < 96)
    ).astype(F32).astype(BF)
    vz[...] = jnp.zeros(vz.shape, F32)
    for src in range(NZ):
        spread_v = nn(v_ref[src], select)
        for q in range(4):
            z_row = 8 + 2 * src + q
            if q >= 2:
                if src >= 5:
                    z_row = 2 * src + (q - 2) - 8
                elif src <= 2:
                    z_row = 24 + 2 * src + (q - 2)
                else:
                    continue
            vz[pl.ds(z_row, 48, stride=32), :] = spread_v[:, q * 128 : (q + 1) * 128]
    v = vz[...]
    lane = iota(v.shape, 1)
    v = jnp.where(lane < 32, rolled(v, 1), jnp.where(lane < 64, v, rolled(v, -1)))
    v = v.astype(BF).reshape(48, 32, 128)
    for ky in range(3):
        vl[:, :, ky * 128 : (ky + 1) * 128] = v[2 + ky : 44 + ky]

    z_base = 128 * at_c + 16 * at_i - 8
    y_base = 32 * at_z

    def inside(y_count, y_first, z_count, z_first, limit):
        z = iota((z_count, 128), 0) + z_first
        rows = ((z >= 0) & (z < limit)).astype(F32)
        return jnp.concatenate(
            [
                rows * jnp.where((y_first + y >= 0) & (y_first + y < limit), 1.0, 0.0)
                for y in range(y_count)
            ],
            axis=0,
        )

    def masked(v, mask):
        return jnp.maximum(v, 0.0) * jnp.concatenate([mask] * (v.shape[1] // 128), axis=1)

    part = 14
    for step in range(3):
        y0 = step * part
        n = part * 32
        h1 = nn(vl[y0 : y0 + part].reshape(n, 384), b_rest[:, :512])
        mask = inside(part, y_base - 5 + y0, 32, z_base, 256)
        for copy in range(2):
            h = masked(h1[:, copy * 256 : (copy + 1) * 256], mask)
            for kz, steps in enumerate((1, 0, -1)):
                moved = rolled(h, steps) if steps else h
                h1l[copy, y0 : y0 + part, :, kz * 256 : (kz + 1) * 256] = moved.astype(BF).reshape(
                    part, 32, 256
                )

    pool_t = jnp.concatenate([pool_matrix(8, 0), pool_matrix(8, 1)], axis=1)
    logits = jnp.zeros((128, 512), F32)
    for copy in range(2):
        part = 20
        n = part * 32
        for step in range(2):
            y0 = step * part
            acc = jnp.zeros((n, 256), F32)
            for ky in range(3):
                acc = acc + nt(h1l[copy, y0 + ky : y0 + ky + part].reshape(n, 768), b_mid[ky])
            h2 = masked(acc, inside(part, y_base - 4 + y0, 32, z_base, 256))
            fine = nt(h2.astype(BF), pool_t).reshape(part // 2, 2, 32, 128)
            pool[y0 * 16 : y0 * 16 + n // 2] = (fine[:, 0] + fine[:, 1]).reshape(n // 2, 128)
            first, last = max(y0, 3), min(y0 + part, 37)
            for kz in range(3):
                moved = rolled(h2, -(7 + kz)).reshape(part, 32, 256)
                l4[copy, first - 3 : last - 3, :, kz * 256 : (kz + 1) * 256] = moved[
                    first - y0 : last - y0, :16
                ].astype(BF)
        q = 0.125 * (pool[pl.ds(0, 320, stride=2), :] + pool[pl.ds(1, 320, stride=2), :])
        for kz, steps in enumerate((1, 0, -1)):
            moved = rolled(q, steps) if steps else q
            ql[:, :, kz * 128 : (kz + 1) * 128] = moved.astype(BF).reshape(20, 16, 128)
        acc = jnp.zeros((288, 128), F32)
        for ky in range(3):
            acc = acc + nt(ql[ky : ky + 18].reshape(288, 384), b_rest[ky * 128 : ky * 128 + 128, 512:896])
        h3 = masked(
            acc, inside(18, 16 * at_z - 1, 16, 64 * at_c + 8 * at_i - 4, 128)
        )
        rise[pl.ds(0, 288, stride=2), :] = h3
        rise[pl.ds(1, 288, stride=2), :] = h3
        r = rise[...]
        for kz in range(3):
            moved = rolled(r, -(7 + kz)).reshape(18, 32, 128)[:, :16].astype(BF)
            for slot in range(34):
                l4[copy, slot, :, 768 + kz * 128 : 896 + kz * 128] = moved[(slot + 3) // 2 - 1]
        acc = jnp.zeros((512, 256), F32)
        for ky in range(3):
            acc = acc + nt(l4[copy, ky : ky + 32].reshape(512, 1152), b_up[ky])
        h4 = jnp.maximum(acc, 0.0).astype(BF)
        logits = logits + nt(b_rest[copy * 128 : copy * 128 + 128, 896:], h4)
    out_ref[...] = (0.5 * logits).astype(BF).reshape(NI, 16, 512)


def arrange_kernel(parts_ref, out_ref):
    lane = iota((16, 128), 1) // 16
    for o in range(4):
        parts = [parts_ref[src, :, o * 128 : (o + 1) * 128].astype(F32) for src in range(NI)]
        for bit in (1, 2, 4):
            upper = (lane & bit) != 0
            for low in range(NI):
                if low & bit == 0:
                    first, second = parts[low], parts[low | bit]
                    parts[low] = jnp.where(upper, pltpu.roll(second, 16 * bit, 1), first)
                    parts[low | bit] = jnp.where(upper, second, pltpu.roll(first, 128 - 16 * bit, 1))
        for y in range(8):
            out_ref[pl.ds(o * 8 + y, 16, stride=32), :] = parts[y]


def call(kernel, out_shape, scratch, megabytes, *args):
    spec = pl.BlockSpec(memory_space=pltpu.VMEM)
    return pl.pallas_call(
        kernel,
        out_shape=out_shape,
        in_specs=[spec] * len(args),
        out_specs=jax.tree.map(lambda _: spec, out_shape),
        scratch_shapes=scratch,
        compiler_params=pltpu.CompilerParams(vmem_limit_bytes=megabytes * 1024 * 1024),
    )(*args)


def bf(*shape):
    return jax.ShapeDtypeStruct(shape, BF)


def flat2(w):
    return w.transpose(2, 3, 0, 1).reshape(-1, w.shape[1])


def table(rows, width, *weights):
    total, at = None, 0
    for w in weights:
        n = w.shape[0]
        filled = jnp.pad(w, ((at, rows - at - n), (0, width - w.shape[1])))
        total = filled if total is None else total + filled
        at += n
    return total


def flat3(w):
    return w.transpose(2, 3, 4, 0, 1).reshape(-1, w.shape[1])


def rim_pairs():
    pairs = []

    def index(i, z, c):
        return (i * NZ + z) * NC + c

    for c in range(NC):
        for z in range(NZ):
            for i in range(NI):
                if z >= 5:
                    if i < NI - 1:
                        pairs.append((index(i, z, c), index(i + 1, z, c)))
                    elif c == 0:
                        pairs.append((index(i, z, 0), index(0, z, 1)))
                if z <= 2:
                    if i > 0:
                        pairs.append((index(i, z, c), index(i - 1, z, c)))
                    elif c == 1:
                        pairs.append((index(i, z, 1), index(NI - 1, z, 0)))
    return pairs


def denoise(first_plane, planes, before, *weights):
    count = planes.shape[0]
    args = (planes,) if before is None else (planes, before)
    vmem = pltpu.VMEM
    return call(
        functools.partial(denoise_kernel, first_plane, before is not None),
        bf(NZ, 48, 128),
        [
            vmem((count * 256, 1536), BF),
            vmem((count * 256, 2304), BF),
            vmem((count * 128, 256), F32),
            vmem((count * 256, 128), F32),
            vmem((count * 256, 256), F32),
            vmem((272, 128), F32),
        ],
        24,
        *args,
        *weights,
    )


def per_device(
    noisy, w2_in, w2_mid, w2_low, w2_deep, w2_up, w2_out, w3_in, w3_mid, w3_low, w3_up, w3_out
):
    second = lax.axis_index("c") == 1
    low_half, high_half = noisy[0, 0], noisy[1, 0]
    sent = jnp.where(second, low_half, high_half)
    got = lax.ppermute(sent, "c", [(0, 1), (1, 0)])
    w_in = jnp.pad(w2_in.transpose(1, 2, 3, 0)[0], ((0, 0), (0, 13), (0, 0))).reshape(48, 16)
    taps = (flat2(w2_mid), flat2(w2_low), flat2(w2_deep), flat2(w2_up), w_in, w2_out)
    weights = call(
        plane_weights_kernel,
        [
            bf(128, 512),
            bf(512, 1536),
            bf(256, 768),
            bf(256, 768),
            bf(512, 2304),
            bf(256, 512),
            bf(4, 128, 512),
        ],
        [],
        16,
        table(640, 32, *taps),
    )
    own = jnp.stack([jnp.where(second, got, low_half), jnp.where(second, high_half, got)])
    rim = lax.ppermute(own, ("i", "z", "c"), rim_pairs())
    volume = denoise(0, own, None, *weights)
    volume = denoise(2, rim, volume, *weights)
    window = lax.all_to_all(volume, "z", 0, 0, tiled=True)
    w_in = jnp.pad(w3_in.transpose(1, 2, 3, 4, 0)[0], ((0, 0), (0, 0), (0, 13), (0, 0)))
    taps = (flat3(w3_mid), flat3(w3_low), flat3(w3_up), w_in.reshape(144, 8), w3_out)
    volume_weights = call(
        volume_weights_kernel,
        [bf(384, 1152), bf(3, 256, 768), bf(3, 256, 1152)],
        [],
        16,
        table(800, 16, *taps),
    )
    vmem = pltpu.VMEM
    logits = call(
        segment_kernel,
        bf(NI, 16, 512),
        [
            vmem((48 * 32, 128), F32),
            vmem((42, 32, 384), BF),
            vmem((2, 42, 32, 768), BF),
            vmem((640, 128), F32),
            vmem((20, 16, 384), BF),
            vmem((576, 128), F32),
            vmem((2, 34, 16, 1152), BF),
        ],
        24,
        window,
        *volume_weights,
    )
    parts = lax.all_to_all(logits, "i", 0, 0, tiled=True)
    out = call(arrange_kernel, jax.ShapeDtypeStruct((512, 128), F32), [], 4, parts)
    return out.reshape(1, 4, 4, 32, 128)


def solution(mesh):
    finer = Mesh(mesh.devices.reshape(2, NI, NZ, NC), ("rep", "i", "z", "c"))
    brick = ("i", "z", "c")
    placed = (P(None, brick, None, None),) + (P(),) * 11
    return jax.shard_map(
        per_device,
        mesh=finer,
        in_specs=placed,
        out_specs=P(brick, "rep", None, None, None),
        check_vma=False,
    )
```

```python
import functools

import jax
import jax.numpy as jnp
from jax import lax
from jax.experimental import pallas as pl
from jax.experimental.pallas import tpu as pltpu
from jax.sharding import Mesh
from jax.sharding import PartitionSpec as P

BF = jnp.bfloat16
F32 = jnp.float32
NI, NZ, NC = 8, 8, 2


def iota(shape, dim):
    return lax.broadcasted_iota(jnp.int32, shape, dim)


def nn(a, b):
    return lax.dot_general(a, b, (((1,), (0,)), ((), ())), preferred_element_type=F32)


def nt(a, b):
    return lax.dot_general(a, b, (((1,), (1,)), ((), ())), preferred_element_type=F32)


def lane_spread(rows, channels, first, lanes):
    return (iota((rows, lanes), 1) % channels + first == iota((rows, lanes), 0)).astype(
        F32
    ).astype(BF)


def stacked(taps, at, channels):
    return jnp.concatenate([taps[at * channels : (at + 1) * channels]] * (128 // channels), axis=0)


def same_level(ref, lead, at, blocks, taps, channels):
    cells = 128 // channels
    gap = iota((128, 128), 1) // channels - iota((128, 128), 0) // channels
    zero = jnp.zeros((128, 128), F32)
    own = jnp.where(
        gap == 0, taps[1], jnp.where(gap == -1, taps[0], jnp.where(gap == 1, taps[2], zero))
    ).astype(BF)
    if blocks > 1:
        later = jnp.where(gap == 1 - cells, taps[2], zero).astype(BF)
        earlier = jnp.where(gap == cells - 1, taps[0], zero).astype(BF)
    for out in range(blocks):
        for inp in range(blocks):
            if inp == out:
                block = own
            elif inp == out + 1:
                block = later
            elif inp == out - 1:
                block = earlier
            else:
                block = jnp.zeros((128, 128), BF)
            ref[lead + (pl.ds(out * 128, 128), pl.ds(at + inp * 128, 128))] = block


def from_coarse(ref, lead, at, out_blocks, in_blocks, taps, channels):
    cells = 128 // channels
    lane_cell = iota((128, 128), 1) // channels
    row_cell = iota((128, 128), 0) // channels
    zero = jnp.zeros((128, 128), F32)
    for out in range(out_blocks):
        for inp in range(in_blocks):
            total = zero
            for kx in range(3):
                meets = (row_cell + (out * cells + kx - 1)) >> 1 == lane_cell + inp * cells
                total = total + jnp.where(meets, taps[kx], zero)
            ref[lead + (pl.ds(out * 128, 128), pl.ds(at + inp * 128, 128))] = total.astype(BF)


def pool_matrix(channels, half):
    cells = 128 // channels
    lane, row = iota((128, 128), 1), iota((128, 128), 0)
    meets = ((lane // channels + half * cells) >> 1 == row // channels) & (
        lane % channels == row % channels
    )
    return meets.astype(F32).astype(BF)


def rolled(v, steps):
    return pltpu.roll(v, steps % v.shape[0], 0)


def plane_weights_kernel(w_ref, b_in, b_mid, b_low, b_deep, b_up, b_pool, b_last):
    edge = [nn(w_ref[kx, 192:208], lane_spread(32, 16, 0, 512)) for kx in range(3)]
    w_row = edge[0][3:4]
    xi = iota((32, 512), 0)
    xo = iota((32, 512), 1) // 16
    for ky in range(3):
        total = jnp.zeros((32, 512), F32)
        for kx in range(3):
            total = jnp.where(xi == xo + (kx - 1), edge[kx][ky : ky + 1], total)
        b_in[ky * 32 : (ky + 1) * 32] = total.astype(BF)
    b_in[96:128] = jnp.zeros((32, 512), BF)
    spread = lane_spread(32, 16, 0, 128)
    for at, b_ref, blocks in ((0, b_mid, 4), (48, b_low, 2), (96, b_deep, 2)):
        w = [nn(w_ref[kx, at : at + 48], spread) for kx in range(3)]
        for ky in range(3):
            taps = [stacked(w[kx], ky, 16) for kx in range(3)]
            same_level(b_ref, (), ky * blocks * 128, blocks, taps, 16)
    w_skip = [nn(w_ref[kx, 144:192], spread) for kx in range(3)]
    w_rise = [nn(w_ref[kx, 144:192], lane_spread(32, 16, 16, 128)) for kx in range(3)]
    for ky in range(3):
        taps = [stacked(w_skip[kx], ky, 16) for kx in range(3)]
        same_level(b_up, (), ky * 512, 4, taps, 16)
        taps = [stacked(w_rise[kx], ky, 16) for kx in range(3)]
        from_coarse(b_up, (), 1536 + ky * 256, 4, 2, taps, 16)
    none = jnp.zeros((128, 128), BF)
    for out in range(2):
        for inp in range(4):
            b_pool[out * 128 : (out + 1) * 128, inp * 128 : (inp + 1) * 128] = (
                pool_matrix(16, inp % 2) if inp // 2 == out else none
            )
    to_lane, cell = iota((128, 512), 0), iota((128, 512), 1) // 16
    for q in range(4):
        b_last[q] = jnp.where(to_lane == q * 32 + cell, w_row, 0.0).astype(BF)


def denoise_kernel(rim, planes_ref, *refs):
    before_ref = refs[0] if rim else None
    refs = refs[rim:]
    b_in, b_mid, b_low, b_deep, b_up, b_pool, b_last, out_ref = refs[:8]
    lhs, wide, coarse, half, raised, vol = refs[8:]
    planes = 2
    low_rows = planes * 128

    def place(ref, at, width, v, length):
        n = v.shape[0]
        row = iota(v.shape, 0) % length
        ref[:n, at : at + width] = jnp.where(row == 0, 0.0, rolled(v, 1)).astype(BF)
        ref[:n, at + width : at + 2 * width] = v.astype(BF)
        ref[:n, at + 2 * width : at + 3 * width] = jnp.where(
            row == length - 1, 0.0, rolled(v, -1)
        ).astype(BF)

    turned = planes_ref[...].astype(F32).reshape(64, 256)
    turned = jnp.concatenate([turned, jnp.zeros((64, 256), F32)], axis=0).T
    row = iota((256, 128), 0)
    lane = iota((256, 128), 1)
    before = jnp.where(row == 0, 0.0, rolled(turned, 1))
    after = jnp.where(row == 255, 0.0, rolled(turned, -1))
    for q in range(planes):
        three = jnp.zeros((256, 128), F32)
        for g, v in enumerate((before, turned, after)):
            three = jnp.where(lane // 32 == g, pltpu.roll(v, ((g - q) * 32) % 128, 1), three)
        first = jnp.maximum(nn(three.astype(BF), b_in[...]), 0.0)
        place(lhs.at[q * 256 : (q + 1) * 256], 0, 512, first, 256)
    skip = jnp.maximum(nt(lhs[...], b_mid[...]), 0.0)
    place(wide, 0, 512, skip, 256)
    fine = nt(skip.astype(BF), b_pool[...])
    for c in range(2):
        half[...] = fine[:, c * 128 : (c + 1) * 128]
        coarse[:, c * 128 : (c + 1) * 128] = 0.25 * (
            half[pl.ds(0, low_rows, stride=2), :] + half[pl.ds(1, low_rows, stride=2), :]
        )
    place(lhs.at[:low_rows], 0, 256, coarse[...], 128)
    low = jnp.maximum(nt(lhs[:low_rows, :768], b_low[...]), 0.0)
    place(lhs.at[:low_rows], 768, 256, low, 128)
    deep = jnp.maximum(nt(lhs[:low_rows, 768:1536], b_deep[...]), 0.0)
    for c in range(2):
        part = deep[:, c * 128 : (c + 1) * 128]
        half[pl.ds(0, low_rows, stride=2), :] = part
        half[pl.ds(1, low_rows, stride=2), :] = part
        raised[:, c * 128 : (c + 1) * 128] = half[...]
    place(wide, 1536, 256, raised[...], 256)
    joined = jnp.maximum(nt(wide[...], b_up[...]), 0.0).astype(BF)
    total = jnp.zeros((256, 128), F32)
    for q in range(planes):
        total = total + nt(joined[q * 256 : (q + 1) * 256], b_last[2 * rim + q])
    vol[0:8] = jnp.zeros((8, 128), F32)
    vol[264:272] = jnp.zeros((8, 128), F32)
    vol[8:264] = total
    for z in range(NZ):
        window = vol[z * 32 : z * 32 + 48]
        if before_ref is not None:
            window = window + before_ref[z].astype(F32)
        out_ref[z] = window.astype(BF)


def volume_weights_kernel(w_ref, b_rest, b_mid, b_up):
    edge = [nn(w_ref[kxy, 72:88], lane_spread(16, 8, 0, 256)) for kxy in range(9)]
    spread = lane_spread(16, 8, 0, 128)
    w_mid, w_low, w_skip = (
        [nn(w_ref[kxy, at : at + 24], spread) for kxy in range(9)] for at in (0, 24, 48)
    )
    w_rise = [nn(w_ref[kxy, 48:72], lane_spread(16, 8, 8, 128)) for kxy in range(9)]
    xi = iota((32, 256), 0)
    xo = iota((32, 256), 1) // 8
    for ky in range(3):
        for kz in range(3):
            plain = jnp.zeros((32, 256), F32)
            mirror = jnp.zeros((32, 256), F32)
            for kx in range(3):
                tap = edge[kx * 3 + ky][kz : kz + 1]
                plain = jnp.where(xi == xo + (kx - 1), tap, plain)
                mirror = jnp.where(xi == (32 - kx) - xo, tap, mirror)
            at = kz * 32
            b_rest[ky, at : at + 32, :256] = plain.astype(BF)
            b_rest[ky, at : at + 32, 256:512] = mirror.astype(BF)
        b_rest[ky, 96:128, :512] = jnp.zeros((32, 512), BF)
    for ky in range(3):
        for kz in range(3):
            for w, b_ref, at, blocks in (
                (w_mid, b_mid.at[ky], kz * 256, 2),
                (w_low, b_rest.at[ky], 512 + kz * 128, 1),
                (w_skip, b_up.at[ky], kz * 256, 2),
            ):
                taps = [stacked(w[kx * 3 + ky], kz, 8) for kx in range(3)]
                same_level(b_ref, (), at, blocks, taps, 8)
            taps = [stacked(w_rise[kx * 3 + ky], kz, 8) for kx in range(3)]
            from_coarse(b_up, (ky,), 768 + kz * 128, 2, 1, taps, 8)
    w_out = edge[0][8:16].astype(BF)
    row_r = iota((128, 256), 0)
    cell = iota((128, 256), 1) // 8
    pick = (iota((128, 8), 1) == (iota((128, 8), 0) // 4) % 4 + 4 * lax.axis_index("rep"))
    w_rows = nn(pick.astype(F32).astype(BF), w_out)
    x_row = (row_r // 16) * 4 + row_r % 4
    b_rest[0, :, 896:] = jnp.where(cell == x_row, w_rows, 0.0).astype(BF)
    b_rest[1, :, 896:] = jnp.where(31 - cell == x_row, w_rows, 0.0).astype(BF)


def segment_kernel(v_ref, b_rest, b_mid, b_up, out_ref, vz, vl, h1l, pool, ql, rise, l4):
    at_i, at_z, at_c = (lax.axis_index(name) for name in ("i", "z", "c"))
    out_lane = iota((128, 512), 1)
    select = (
        (iota((128, 512), 0) == (out_lane // 128) * 32 + out_lane % 32) & (out_lane % 128 < 96)
    ).astype(F32).astype(BF)
    vz[...] = jnp.zeros(vz.shape, F32)
    for src in range(NZ):
        spread_v = nn(v_ref[src], select)
        for q in range(4):
            z_row = 8 + 2 * src + q
            if q >= 2:
                if src >= 5:
                    z_row = 2 * src + (q - 2) - 8
                elif src <= 2:
                    z_row = 24 + 2 * src + (q - 2)
                else:
                    continue
            vz[pl.ds(z_row, 48, stride=32), :] = spread_v[:, q * 128 : (q + 1) * 128]
    v = vz[...]
    lane = iota(v.shape, 1)
    v = jnp.where(lane < 32, rolled(v, 1), jnp.where(lane < 64, v, rolled(v, -1)))
    v = v.astype(BF).reshape(48, 32, 128)
    for ky in range(3):
        vl[:, :, ky * 128 : (ky + 1) * 128] = v[2 + ky : 44 + ky]

    z_base = 128 * at_c + 16 * at_i - 8
    y_base = 32 * at_z

    def inside(y_count, y_first, z_count, z_first, limit):
        z = iota((z_count, 128), 0) + z_first
        rows = ((z >= 0) & (z < limit)).astype(F32)
        return jnp.concatenate(
            [
                rows * jnp.where((y_first + y >= 0) & (y_first + y < limit), 1.0, 0.0)
                for y in range(y_count)
            ],
            axis=0,
        )

    def masked(v, mask):
        return jnp.maximum(v, 0.0) * jnp.concatenate([mask] * (v.shape[1] // 128), axis=1)

    part = 14
    for step in range(3):
        y0 = step * part
        n = part * 32
        h1 = nn(vl[y0 : y0 + part].reshape(n, 384), b_rest[:, :, :512].reshape(384, 512))
        mask = inside(part, y_base - 5 + y0, 32, z_base, 256)
        for copy in range(2):
            h = masked(h1[:, copy * 256 : (copy + 1) * 256], mask)
            for kz, steps in enumerate((1, 0, -1)):
                moved = rolled(h, steps) if steps else h
                h1l[copy, y0 : y0 + part, :, kz * 256 : (kz + 1) * 256] = moved.astype(BF).reshape(
                    part, 32, 256
                )

    pool_t = jnp.concatenate([pool_matrix(8, 0), pool_matrix(8, 1)], axis=1)
    logits = jnp.zeros((128, 512), F32)
    for copy in range(2):
        part = 20
        n = part * 32
        for step in range(2):
            y0 = step * part
            acc = jnp.zeros((n, 256), F32)
            for ky in range(3):
                acc = acc + nt(h1l[copy, y0 + ky : y0 + ky + part].reshape(n, 768), b_mid[ky])
            h2 = masked(acc, inside(part, y_base - 4 + y0, 32, z_base, 256))
            fine = nt(h2.astype(BF), pool_t).reshape(part // 2, 2, 32, 128)
            pool[y0 * 16 : y0 * 16 + n // 2] = (fine[:, 0] + fine[:, 1]).reshape(n // 2, 128)
            first, last = max(y0, 3), min(y0 + part, 37)
            for kz in range(3):
                moved = rolled(h2, -(7 + kz)).reshape(part, 32, 256)
                l4[copy, first - 3 : last - 3, :, kz * 256 : (kz + 1) * 256] = moved[
                    first - y0 : last - y0, :16
                ].astype(BF)
        q = 0.125 * (pool[pl.ds(0, 320, stride=2), :] + pool[pl.ds(1, 320, stride=2), :])
        for kz, steps in enumerate((1, 0, -1)):
            moved = rolled(q, steps) if steps else q
            ql[:, :, kz * 128 : (kz + 1) * 128] = moved.astype(BF).reshape(20, 16, 128)
        acc = jnp.zeros((288, 128), F32)
        for ky in range(3):
            acc = acc + nt(ql[ky : ky + 18].reshape(288, 384), b_rest[ky, :, 512:896])
        h3 = masked(
            acc, inside(18, 16 * at_z - 1, 16, 64 * at_c + 8 * at_i - 4, 128)
        )
        rise[pl.ds(0, 288, stride=2), :] = h3
        rise[pl.ds(1, 288, stride=2), :] = h3
        r = rise[...]
        for kz in range(3):
            moved = rolled(r, -(7 + kz)).reshape(18, 32, 128)[:, :16].astype(BF)
            for slot in range(34):
                l4[copy, slot, :, 768 + kz * 128 : 896 + kz * 128] = moved[(slot + 3) // 2 - 1]
        acc = jnp.zeros((512, 256), F32)
        for ky in range(3):
            acc = acc + nt(l4[copy, ky : ky + 32].reshape(512, 1152), b_up[ky])
        h4 = jnp.maximum(acc, 0.0).astype(BF)
        logits = logits + nt(b_rest[copy, :, 896:], h4)
    out_ref[...] = (0.5 * logits).astype(BF).reshape(NI, 16, 512)


def arrange_kernel(parts_ref, out_ref):
    lane = iota((16, 128), 1) // 16
    for o in range(4):
        parts = [parts_ref[src, :, o * 128 : (o + 1) * 128].astype(F32) for src in range(NI)]
        for bit in (1, 2, 4):
            upper = (lane & bit) != 0
            for low in range(NI):
                if low & bit == 0:
                    first, second = parts[low], parts[low | bit]
                    parts[low] = jnp.where(upper, pltpu.roll(second, 16 * bit, 1), first)
                    parts[low | bit] = jnp.where(upper, second, pltpu.roll(first, 128 - 16 * bit, 1))
        for y in range(8):
            out_ref[pl.ds(o * 8 + y, 16, stride=32), :] = parts[y]


def call(kernel, out_shape, scratch, megabytes, *args):
    spec = pl.BlockSpec(memory_space=pltpu.VMEM)
    return pl.pallas_call(
        kernel,
        out_shape=out_shape,
        in_specs=[spec] * len(args),
        out_specs=jax.tree.map(lambda _: spec, out_shape),
        scratch_shapes=scratch,
        compiler_params=pltpu.CompilerParams(vmem_limit_bytes=megabytes * 1024 * 1024),
    )(*args)


def bf(*shape):
    return jax.ShapeDtypeStruct(shape, BF)


def table(lead, rows, width, *weights):
    total = 0
    for at, w in weights:
        size = w.shape
        total = total + jnp.pad(
            w, ((0, lead - size[0]), (at, rows - at - size[1]), (0, width - size[2]))
        )
    return total


def taps2(w):
    return w.transpose(2, 3, 0, 1).reshape(3, -1, w.shape[1])


def taps3(w):
    return w.transpose(2, 3, 4, 0, 1).reshape(9, -1, w.shape[1])


def rim_pairs():
    def index(i, z, c):
        return (i * NZ + z) * NC + c

    pairs = []
    for z in range(NZ):
        if z >= NZ - 3:
            step, edge, wrapped = 1, NI - 1, 0
        elif z <= 2:
            step, edge, wrapped = -1, 0, 1
        else:
            continue
        for i in range(NI):
            for c in range(NC):
                if i != edge:
                    pairs.append((index(i, z, c), index(i + step, z, c)))
                elif c == wrapped:
                    pairs.append((index(i, z, c), index((i + step) % NI, z, 1 - c)))
    return pairs


def denoise(rim, planes, before, weights):
    args = (planes, before) if rim else (planes,)
    count = 2
    vmem = pltpu.VMEM
    return call(
        functools.partial(denoise_kernel, rim),
        bf(NZ, 48, 128),
        [
            vmem((count * 256, 1536), BF),
            vmem((count * 256, 2304), BF),
            vmem((count * 128, 256), F32),
            vmem((count * 256, 128), F32),
            vmem((count * 256, 256), F32),
            vmem((272, 128), F32),
        ],
        24,
        *args,
        *weights,
    )


def per_device(
    noisy, w2_in, w2_mid, w2_low, w2_deep, w2_up, w2_out, w3_in, w3_mid, w3_low, w3_up, w3_out
):
    near = noisy.reshape(2, 32, 256)
    far = lax.ppermute(near, "c", [(0, 1), (1, 0)])
    kernels = ((0, w2_mid), (48, w2_low), (96, w2_deep), (144, w2_up))
    taps = [(at, taps2(w)) for at, w in kernels]
    taps += [(192, w2_in.transpose(1, 2, 3, 0)[0]), (195, w2_out[None])]
    weights = call(
        plane_weights_kernel,
        [
            bf(128, 512),
            bf(512, 1536),
            bf(256, 768),
            bf(256, 768),
            bf(512, 2304),
            bf(256, 512),
            bf(4, 128, 512),
        ],
        [],
        16,
        table(3, 208, 32, *taps),
    )
    second = lax.axis_index("c") == 1
    own = jnp.stack([jnp.where(second, far[1], near[0]), jnp.where(second, near[1], far[0])])
    rim = lax.ppermute(own, ("i", "z", "c"), rim_pairs())
    volume = denoise(0, own, None, weights)
    volume = denoise(1, rim, volume, weights)
    taps = [(at, taps3(w)) for at, w in ((0, w3_mid), (24, w3_low), (48, w3_up))]
    taps += [(72, w3_in.transpose(1, 2, 3, 4, 0).reshape(9, 3, 8)), (80, w3_out[None])]
    bands = call(volume_weights_kernel, [bf(3, 128, 1152), bf(3, 256, 768), bf(3, 256, 1152)], [], 16, table(9, 88, 16, *taps))
    volume, bands = lax.optimization_barrier((volume, bands))
    window = lax.all_to_all(volume, "z", 0, 0, tiled=True)
    vmem = pltpu.VMEM
    logits = call(
        segment_kernel,
        bf(NI, 16, 512),
        [
            vmem((48 * 32, 128), F32),
            vmem((42, 32, 384), BF),
            vmem((2, 42, 32, 768), BF),
            vmem((640, 128), F32),
            vmem((20, 16, 384), BF),
            vmem((576, 128), F32),
            vmem((2, 34, 16, 1152), BF),
        ],
        24,
        window,
        *bands,
    )
    parts = lax.all_to_all(logits, "i", 0, 0, tiled=True)
    out = call(arrange_kernel, jax.ShapeDtypeStruct((512, 128), F32), [], 4, parts)
    return out.reshape(1, 4, 4, 32, 128)


def solution(mesh):
    finer = Mesh(mesh.devices.reshape(2, NI, NZ, NC), ("rep", "i", "z", "c"))
    brick = ("i", "z", "c")
    placed = (P(None, brick, None, None),) + (P(),) * 11
    return jax.shard_map(
        per_device,
        mesh=finer,
        in_specs=placed,
        out_specs=P(brick, "rep", None, None, None),
        check_vma=False,
    )
```

```python
import functools

import jax
import jax.numpy as jnp
from jax import lax
from jax.experimental import pallas as pl
from jax.experimental.pallas import tpu as pltpu
from jax.sharding import Mesh
from jax.sharding import PartitionSpec as P

BF = jnp.bfloat16
F32 = jnp.float32
NI, NZ, NC = 8, 8, 2


def iota(shape, dim):
    return lax.broadcasted_iota(jnp.int32, shape, dim)


def nn(a, b):
    return lax.dot_general(a, b, (((1,), (0,)), ((), ())), preferred_element_type=F32)


def nt(a, b):
    return lax.dot_general(a, b, (((1,), (1,)), ((), ())), preferred_element_type=F32)


def lane_spread(rows, channels, first, lanes):
    return (iota((rows, lanes), 1) % channels + first == iota((rows, lanes), 0)).astype(
        F32
    ).astype(BF)


def stacked(taps, at, channels):
    return jnp.concatenate([taps[at * channels : (at + 1) * channels]] * (128 // channels), axis=0)


def band_parts(taps, channels):
    cells = 128 // channels
    gap = iota((128, 128), 1) // channels - iota((128, 128), 0) // channels
    zero = jnp.zeros((128, 128), F32)
    own = jnp.where(
        gap == 0, taps[1], jnp.where(gap == -1, taps[0], jnp.where(gap == 1, taps[2], zero))
    )
    later = jnp.where(gap == 1 - cells, taps[2], zero)
    earlier = jnp.where(gap == cells - 1, taps[0], zero)
    return [part.astype(BF) for part in (own, later, earlier)]


def same_level(ref, at, blocks, taps, channels):
    own, later, earlier = band_parts(taps, channels)
    for out in range(blocks):
        for inp in range(blocks):
            if inp == out:
                block = own
            elif inp == out + 1:
                block = later
            elif inp == out - 1:
                block = earlier
            else:
                block = jnp.zeros((128, 128), BF)
            ref[out * 128 : (out + 1) * 128, at + inp * 128 : at + (inp + 1) * 128] = block


def two_blocks(ref, ky):
    parts = [ref[ky, :, at * 128 : (at + 1) * 128] for at in range(9)]
    rows = [[], []]
    for own, later, earlier in (parts[0:3], parts[3:6], parts[6:9]):
        rows[0] += [own, later]
        rows[1] += [earlier, own]
    return jnp.concatenate([jnp.concatenate(row, axis=1) for row in rows], axis=0)


def from_coarse(ref, lead, at, out_blocks, in_blocks, taps, channels):
    cells = 128 // channels
    lane_cell = iota((128, 128), 1) // channels
    row_cell = iota((128, 128), 0) // channels
    zero = jnp.zeros((128, 128), F32)
    for out in range(out_blocks):
        for inp in range(in_blocks):
            total = zero
            for kx in range(3):
                meets = (row_cell + (out * cells + kx - 1)) >> 1 == lane_cell + inp * cells
                total = total + jnp.where(meets, taps[kx], zero)
            ref[lead + (pl.ds(out * 128, 128), pl.ds(at + inp * 128, 128))] = total.astype(BF)


def pool_matrix(channels, half):
    cells = 128 // channels
    lane, row = iota((128, 128), 1), iota((128, 128), 0)
    meets = ((lane // channels + half * cells) >> 1 == row // channels) & (
        lane % channels == row % channels
    )
    return meets.astype(F32).astype(BF)


def rolled(v, steps):
    return pltpu.roll(v, steps % v.shape[0], 0)


def plane_weights_kernel(w_ref, b_in, b_mid, b_low, b_deep, b_up, b_pool, b_last):
    edge = [nn(w_ref[kx, 192:208], lane_spread(32, 16, 0, 512)) for kx in range(3)]
    w_row = edge[0][3:4]
    xi = iota((32, 512), 0)
    xo = iota((32, 512), 1) // 16
    for ky in range(3):
        total = jnp.zeros((32, 512), F32)
        for kx in range(3):
            total = jnp.where(xi == xo + (kx - 1), edge[kx][ky : ky + 1], total)
        b_in[ky * 32 : (ky + 1) * 32] = total.astype(BF)
    b_in[96:128] = jnp.zeros((32, 512), BF)
    spread = lane_spread(32, 16, 0, 128)
    for at, b_ref, blocks in ((0, b_mid, 4), (48, b_low, 2), (96, b_deep, 2)):
        w = [nn(w_ref[kx, at : at + 48], spread) for kx in range(3)]
        for ky in range(3):
            taps = [stacked(w[kx], ky, 16) for kx in range(3)]
            same_level(b_ref, ky * blocks * 128, blocks, taps, 16)
    w_skip = [nn(w_ref[kx, 144:192], spread) for kx in range(3)]
    w_rise = [nn(w_ref[kx, 144:192], lane_spread(32, 16, 16, 128)) for kx in range(3)]
    for ky in range(3):
        taps = [stacked(w_skip[kx], ky, 16) for kx in range(3)]
        same_level(b_up, ky * 512, 4, taps, 16)
        taps = [stacked(w_rise[kx], ky, 16) for kx in range(3)]
        from_coarse(b_up, (), 1536 + ky * 256, 4, 2, taps, 16)
    none = jnp.zeros((128, 128), BF)
    for out in range(2):
        for inp in range(4):
            b_pool[out * 128 : (out + 1) * 128, inp * 128 : (inp + 1) * 128] = (
                pool_matrix(16, inp % 2) if inp // 2 == out else none
            )
    to_lane, cell = iota((128, 512), 0), iota((128, 512), 1) // 16
    for q in range(4):
        b_last[q] = jnp.where(to_lane == q * 32 + cell, w_row, 0.0).astype(BF)


def denoise_kernel(rim, planes_ref, *refs):
    before_ref = refs[0] if rim else None
    refs = refs[rim:]
    b_in, b_mid, b_low, b_deep, b_up, b_pool, b_last, out_ref = refs[:8]
    lhs, wide, coarse, half, raised, vol = refs[8:]
    planes = 2
    low_rows = planes * 128

    def place(ref, at, width, v, length):
        n = v.shape[0]
        row = iota(v.shape, 0) % length
        ref[:n, at : at + width] = jnp.where(row == 0, 0.0, rolled(v, 1)).astype(BF)
        ref[:n, at + width : at + 2 * width] = v.astype(BF)
        ref[:n, at + 2 * width : at + 3 * width] = jnp.where(
            row == length - 1, 0.0, rolled(v, -1)
        ).astype(BF)

    turned = planes_ref[...].astype(F32).reshape(64, 256)
    turned = jnp.concatenate([turned, jnp.zeros((64, 256), F32)], axis=0).T
    row = iota((256, 128), 0)
    lane = iota((256, 128), 1)
    before = jnp.where(row == 0, 0.0, rolled(turned, 1))
    after = jnp.where(row == 255, 0.0, rolled(turned, -1))
    for q in range(planes):
        three = jnp.zeros((256, 128), F32)
        for g, v in enumerate((before, turned, after)):
            three = jnp.where(lane // 32 == g, pltpu.roll(v, ((g - q) * 32) % 128, 1), three)
        first = jnp.maximum(nn(three.astype(BF), b_in[...]), 0.0)
        place(lhs.at[q * 256 : (q + 1) * 256], 0, 512, first, 256)
    skip = jnp.maximum(nt(lhs[...], b_mid[...]), 0.0)
    place(wide, 0, 512, skip, 256)
    fine = nt(skip.astype(BF), b_pool[...])
    for c in range(2):
        half[...] = fine[:, c * 128 : (c + 1) * 128]
        coarse[:, c * 128 : (c + 1) * 128] = 0.25 * (
            half[pl.ds(0, low_rows, stride=2), :] + half[pl.ds(1, low_rows, stride=2), :]
        )
    place(lhs.at[:low_rows], 0, 256, coarse[...], 128)
    low = jnp.maximum(nt(lhs[:low_rows, :768], b_low[...]), 0.0)
    place(lhs.at[:low_rows], 768, 256, low, 128)
    deep = jnp.maximum(nt(lhs[:low_rows, 768:1536], b_deep[...]), 0.0)
    for c in range(2):
        part = deep[:, c * 128 : (c + 1) * 128]
        half[pl.ds(0, low_rows, stride=2), :] = part
        half[pl.ds(1, low_rows, stride=2), :] = part
        raised[:, c * 128 : (c + 1) * 128] = half[...]
    place(wide, 1536, 256, raised[...], 256)
    joined = jnp.maximum(nt(wide[...], b_up[...]), 0.0).astype(BF)
    total = jnp.zeros((256, 128), F32)
    for q in range(planes):
        total = total + nt(joined[q * 256 : (q + 1) * 256], b_last[2 * rim + q])
    vol[0:8] = jnp.zeros((8, 128), F32)
    vol[264:272] = jnp.zeros((8, 128), F32)
    vol[8:264] = total
    for z in range(NZ):
        window = vol[z * 32 : z * 32 + 48]
        if before_ref is not None:
            window = window + before_ref[z].astype(F32)
        out_ref[z] = window.astype(BF)


def volume_weights_kernel(w_ref, b_rest, b_mid, b_skip, b_rise):
    edge = [nn(w_ref[kxy, 72:88], lane_spread(16, 8, 0, 256)) for kxy in range(9)]
    spread = lane_spread(16, 8, 0, 128)
    w_mid, w_low, w_skip = (
        [nn(w_ref[kxy, at : at + 24], spread) for kxy in range(9)] for at in (0, 24, 48)
    )
    w_rise = [nn(w_ref[kxy, 48:72], lane_spread(16, 8, 8, 128)) for kxy in range(9)]
    xi = iota((32, 256), 0)
    xo = iota((32, 256), 1) // 8
    for ky in range(3):
        for kz in range(3):
            plain = jnp.zeros((32, 256), F32)
            mirror = jnp.zeros((32, 256), F32)
            for kx in range(3):
                tap = edge[kx * 3 + ky][kz : kz + 1]
                plain = jnp.where(xi == xo + (kx - 1), tap, plain)
                mirror = jnp.where(xi == (32 - kx) - xo, tap, mirror)
            at = kz * 32
            b_rest[ky, at : at + 32, :256] = plain.astype(BF)
            b_rest[ky, at : at + 32, 256:512] = mirror.astype(BF)
        b_rest[ky, 96:128, :512] = jnp.zeros((32, 512), BF)
    for ky in range(3):
        for kz in range(3):
            for w, b_ref in ((w_mid, b_mid), (w_skip, b_skip)):
                taps = [stacked(w[kx * 3 + ky], kz, 8) for kx in range(3)]
                for side, part in enumerate(band_parts(taps, 8)):
                    at = (kz * 3 + side) * 128
                    b_ref[ky, :, at : at + 128] = part
            taps = [stacked(w_low[kx * 3 + ky], kz, 8) for kx in range(3)]
            same_level(b_rest.at[ky], 512 + kz * 128, 1, taps, 8)
            taps = [stacked(w_rise[kx * 3 + ky], kz, 8) for kx in range(3)]
            from_coarse(b_rise, (ky,), kz * 128, 2, 1, taps, 8)
    w_out = edge[0][8:16].astype(BF)
    row_r = iota((128, 256), 0)
    cell = iota((128, 256), 1) // 8
    pick = (iota((128, 8), 1) == (iota((128, 8), 0) // 4) % 4 + 4 * lax.axis_index("rep"))
    w_rows = nn(pick.astype(F32).astype(BF), w_out)
    x_row = (row_r // 16) * 4 + row_r % 4
    b_rest[0, :, 896:] = jnp.where(cell == x_row, w_rows, 0.0).astype(BF)
    b_rest[1, :, 896:] = jnp.where(31 - cell == x_row, w_rows, 0.0).astype(BF)


def segment_kernel(v_ref, b_rest, b_mid, b_skip, b_rise, out_ref, vz, vl, h1l, pool, ql, rise, l4):
    at_i, at_z, at_c = (lax.axis_index(name) for name in ("i", "z", "c"))
    out_lane = iota((128, 512), 1)
    select = (
        (iota((128, 512), 0) == (out_lane // 128) * 32 + out_lane % 32) & (out_lane % 128 < 96)
    ).astype(F32).astype(BF)
    vz[...] = jnp.zeros(vz.shape, F32)
    for src in range(NZ):
        spread_v = nn(v_ref[src], select)
        for q in range(4):
            z_row = 8 + 2 * src + q
            if q >= 2:
                if src >= 5:
                    z_row = 2 * src + (q - 2) - 8
                elif src <= 2:
                    z_row = 24 + 2 * src + (q - 2)
                else:
                    continue
            vz[pl.ds(z_row, 48, stride=32), :] = spread_v[:, q * 128 : (q + 1) * 128]
    v = vz[...]
    lane = iota(v.shape, 1)
    v = jnp.where(lane < 32, rolled(v, 1), jnp.where(lane < 64, v, rolled(v, -1)))
    v = v.astype(BF).reshape(48, 32, 128)
    for ky in range(3):
        vl[:, :, ky * 128 : (ky + 1) * 128] = v[2 + ky : 44 + ky]

    z_base = 128 * at_c + 16 * at_i - 8
    y_base = 32 * at_z

    def inside(y_count, y_first, z_count, z_first, limit):
        z = iota((z_count, 128), 0) + z_first
        rows = ((z >= 0) & (z < limit)).astype(F32)
        return jnp.concatenate(
            [
                rows * jnp.where((y_first + y >= 0) & (y_first + y < limit), 1.0, 0.0)
                for y in range(y_count)
            ],
            axis=0,
        )

    def masked(v, mask):
        return jnp.maximum(v, 0.0) * jnp.concatenate([mask] * (v.shape[1] // 128), axis=1)

    part = 14
    for step in range(3):
        y0 = step * part
        n = part * 32
        h1 = nn(vl[y0 : y0 + part].reshape(n, 384), b_rest[:, :, :512].reshape(384, 512))
        mask = inside(part, y_base - 5 + y0, 32, z_base, 256)
        for copy in range(2):
            h = masked(h1[:, copy * 256 : (copy + 1) * 256], mask)
            for kz, steps in enumerate((1, 0, -1)):
                moved = rolled(h, steps) if steps else h
                h1l[copy, y0 : y0 + part, :, kz * 256 : (kz + 1) * 256] = moved.astype(BF).reshape(
                    part, 32, 256
                )

    pool_t = jnp.concatenate([pool_matrix(8, 0), pool_matrix(8, 1)], axis=1)
    logits = jnp.zeros((128, 512), F32)
    for copy in range(2):
        part = 20
        n = part * 32
        for step in range(2):
            y0 = step * part
            acc = jnp.zeros((n, 256), F32)
            for ky in range(3):
                acc = acc + nt(
                    h1l[copy, y0 + ky : y0 + ky + part].reshape(n, 768), two_blocks(b_mid, ky)
                )
            h2 = masked(acc, inside(part, y_base - 4 + y0, 32, z_base, 256))
            fine = nt(h2.astype(BF), pool_t).reshape(part // 2, 2, 32, 128)
            pool[y0 * 16 : y0 * 16 + n // 2] = (fine[:, 0] + fine[:, 1]).reshape(n // 2, 128)
            first, last = max(y0, 3), min(y0 + part, 37)
            for kz in range(3):
                moved = rolled(h2, -(7 + kz)).reshape(part, 32, 256)
                l4[copy, first - 3 : last - 3, :, kz * 256 : (kz + 1) * 256] = moved[
                    first - y0 : last - y0, :16
                ].astype(BF)
        q = 0.125 * (pool[pl.ds(0, 320, stride=2), :] + pool[pl.ds(1, 320, stride=2), :])
        for kz, steps in enumerate((1, 0, -1)):
            moved = rolled(q, steps) if steps else q
            ql[:, :, kz * 128 : (kz + 1) * 128] = moved.astype(BF).reshape(20, 16, 128)
        acc = jnp.zeros((288, 128), F32)
        for ky in range(3):
            acc = acc + nt(ql[ky : ky + 18].reshape(288, 384), b_rest[ky, :, 512:896])
        h3 = masked(
            acc, inside(18, 16 * at_z - 1, 16, 64 * at_c + 8 * at_i - 4, 128)
        )
        rise[pl.ds(0, 288, stride=2), :] = h3
        rise[pl.ds(1, 288, stride=2), :] = h3
        r = rise[...]
        for kz in range(3):
            moved = rolled(r, -(7 + kz)).reshape(18, 32, 128)[:, :16].astype(BF)
            for slot in range(34):
                l4[copy, slot, :, 768 + kz * 128 : 896 + kz * 128] = moved[(slot + 3) // 2 - 1]
        acc = jnp.zeros((512, 256), F32)
        for ky in range(3):
            bands = jnp.concatenate([two_blocks(b_skip, ky), b_rise[ky]], axis=1)
            acc = acc + nt(l4[copy, ky : ky + 32].reshape(512, 1152), bands)
        h4 = jnp.maximum(acc, 0.0).astype(BF)
        logits = logits + nt(b_rest[copy, :, 896:], h4)
    out_ref[...] = (0.5 * logits).astype(BF).reshape(NI, 16, 512)


def arrange_kernel(parts_ref, out_ref):
    lane = iota((16, 128), 1) // 16
    for o in range(4):
        parts = [parts_ref[src, :, o * 128 : (o + 1) * 128].astype(F32) for src in range(NI)]
        for bit in (1, 2, 4):
            upper = (lane & bit) != 0
            for low in range(NI):
                if low & bit == 0:
                    first, second = parts[low], parts[low | bit]
                    parts[low] = jnp.where(upper, pltpu.roll(second, 16 * bit, 1), first)
                    parts[low | bit] = jnp.where(upper, second, pltpu.roll(first, 128 - 16 * bit, 1))
        for y in range(8):
            out_ref[pl.ds(o * 8 + y, 16, stride=32), :] = parts[y]


def call(kernel, out_shape, scratch, megabytes, *args):
    spec = pl.BlockSpec(memory_space=pltpu.VMEM)
    return pl.pallas_call(
        kernel,
        out_shape=out_shape,
        in_specs=[spec] * len(args),
        out_specs=jax.tree.map(lambda _: spec, out_shape),
        scratch_shapes=scratch,
        compiler_params=pltpu.CompilerParams(vmem_limit_bytes=megabytes * 1024 * 1024),
    )(*args)


def bf(*shape):
    return jax.ShapeDtypeStruct(shape, BF)


def table(lead, rows, width, *weights):
    total = 0
    for at, w in weights:
        size = w.shape
        total = total + jnp.pad(
            w, ((0, lead - size[0]), (at, rows - at - size[1]), (0, width - size[2]))
        )
    return total


def taps2(w):
    return w.transpose(2, 3, 0, 1).reshape(3, -1, w.shape[1])


def taps3(w):
    return w.transpose(2, 3, 4, 0, 1).reshape(9, -1, w.shape[1])


def rim_pairs():
    def index(i, z, c):
        return (i * NZ + z) * NC + c

    pairs = []
    for z in range(NZ):
        if z >= NZ - 3:
            step, edge, wrapped = 1, NI - 1, 0
        elif z <= 2:
            step, edge, wrapped = -1, 0, 1
        else:
            continue
        for i in range(NI):
            for c in range(NC):
                if i != edge:
                    pairs.append((index(i, z, c), index(i + step, z, c)))
                elif c == wrapped:
                    pairs.append((index(i, z, c), index((i + step) % NI, z, 1 - c)))
    return pairs


def denoise(rim, planes, before, weights):
    args = (planes, before) if rim else (planes,)
    count = 2
    vmem = pltpu.VMEM
    return call(
        functools.partial(denoise_kernel, rim),
        bf(NZ, 48, 128),
        [
            vmem((count * 256, 1536), BF),
            vmem((count * 256, 2304), BF),
            vmem((count * 128, 256), F32),
            vmem((count * 256, 128), F32),
            vmem((count * 256, 256), F32),
            vmem((272, 128), F32),
        ],
        24,
        *args,
        *weights,
    )


def per_device(
    noisy, w2_in, w2_mid, w2_low, w2_deep, w2_up, w2_out, w3_in, w3_mid, w3_low, w3_up, w3_out
):
    near = noisy.reshape(2, 32, 256)
    far = lax.ppermute(near, "c", [(0, 1), (1, 0)])
    kernels = ((0, w2_mid), (48, w2_low), (96, w2_deep), (144, w2_up))
    taps = [(at, taps2(w)) for at, w in kernels]
    taps += [(192, w2_in.transpose(1, 2, 3, 0)[0]), (195, w2_out[None])]
    weights = call(
        plane_weights_kernel,
        [
            bf(128, 512),
            bf(512, 1536),
            bf(256, 768),
            bf(256, 768),
            bf(512, 2304),
            bf(256, 512),
            bf(4, 128, 512),
        ],
        [],
        16,
        table(3, 208, 32, *taps),
    )
    second = lax.axis_index("c") == 1
    own = jnp.stack([jnp.where(second, far[1], near[0]), jnp.where(second, near[1], far[0])])
    rim = lax.ppermute(own, ("i", "z", "c"), rim_pairs())
    volume = denoise(0, own, None, weights)
    volume = denoise(1, rim, volume, weights)
    taps = [(at, taps3(w)) for at, w in ((0, w3_mid), (24, w3_low), (48, w3_up))]
    taps += [(72, w3_in.transpose(1, 2, 3, 4, 0).reshape(9, 3, 8)), (80, w3_out[None])]
    bands = call(volume_weights_kernel, [bf(3, 128, 1152), bf(3, 128, 1152), bf(3, 128, 1152), bf(3, 256, 384)], [], 16, table(9, 88, 16, *taps))
    window = lax.all_to_all(volume, "z", 0, 0, tiled=True)
    vmem = pltpu.VMEM
    logits = call(
        segment_kernel,
        bf(NI, 16, 512),
        [
            vmem((48 * 32, 128), F32),
            vmem((42, 32, 384), BF),
            vmem((2, 42, 32, 768), BF),
            vmem((640, 128), F32),
            vmem((20, 16, 384), BF),
            vmem((576, 128), F32),
            vmem((2, 34, 16, 1152), BF),
        ],
        24,
        window,
        *bands,
    )
    parts = lax.all_to_all(logits, "i", 0, 0, tiled=True)
    out = call(arrange_kernel, jax.ShapeDtypeStruct((512, 128), F32), [], 4, parts)
    return out.reshape(1, 4, 4, 32, 128)


def solution(mesh):
    finer = Mesh(mesh.devices.reshape(2, NI, NZ, NC), ("rep", "i", "z", "c"))
    brick = ("i", "z", "c")
    placed = (P(None, brick, None, None),) + (P(),) * 11
    return jax.shard_map(
        per_device,
        mesh=finer,
        in_specs=placed,
        out_specs=P(brick, "rep", None, None, None),
        check_vma=False,
    )
```

```python
import functools

import jax
import jax.numpy as jnp
from jax import lax
from jax.experimental import pallas as pl
from jax.experimental.pallas import tpu as pltpu
from jax.sharding import Mesh
from jax.sharding import PartitionSpec as P

BF = jnp.bfloat16
F32 = jnp.float32
NI, NZ, NC = 8, 8, 2


def iota(shape, dim):
    return lax.broadcasted_iota(jnp.int32, shape, dim)


def nn(a, b):
    return lax.dot_general(a, b, (((1,), (0,)), ((), ())), preferred_element_type=F32)


def nt(a, b):
    return lax.dot_general(a, b, (((1,), (1,)), ((), ())), preferred_element_type=F32)


def lane_spread(rows, channels, first, lanes):
    return (iota((rows, lanes), 1) % channels + first == iota((rows, lanes), 0)).astype(
        F32
    ).astype(BF)


def stacked(taps, at, channels):
    return jnp.concatenate([taps[at * channels : (at + 1) * channels]] * (128 // channels), axis=0)


def band_parts(taps, channels):
    cells = 128 // channels
    gap = iota((128, 128), 1) // channels - iota((128, 128), 0) // channels
    zero = jnp.zeros((128, 128), F32)
    own = jnp.where(
        gap == 0, taps[1], jnp.where(gap == -1, taps[0], jnp.where(gap == 1, taps[2], zero))
    )
    later = jnp.where(gap == 1 - cells, taps[2], zero)
    earlier = jnp.where(gap == cells - 1, taps[0], zero)
    return [part.astype(BF) for part in (own, later, earlier)]


def same_level(ref, at, blocks, taps, channels):
    own, later, earlier = band_parts(taps, channels)
    for out in range(blocks):
        for inp in range(blocks):
            if inp == out:
                block = own
            elif inp == out + 1:
                block = later
            elif inp == out - 1:
                block = earlier
            else:
                block = jnp.zeros((128, 128), BF)
            ref[out * 128 : (out + 1) * 128, at + inp * 128 : at + (inp + 1) * 128] = block


def two_blocks(ref, ky):
    parts = [ref[ky, :, at * 128 : (at + 1) * 128] for at in range(9)]
    rows = [[], []]
    for own, later, earlier in (parts[0:3], parts[3:6], parts[6:9]):
        rows[0] += [own, later]
        rows[1] += [earlier, own]
    return jnp.concatenate([jnp.concatenate(row, axis=1) for row in rows], axis=0)


def from_coarse(ref, lead, at, out_blocks, in_blocks, taps, channels):
    cells = 128 // channels
    lane_cell = iota((128, 128), 1) // channels
    row_cell = iota((128, 128), 0) // channels
    zero = jnp.zeros((128, 128), F32)
    for out in range(out_blocks):
        for inp in range(in_blocks):
            total = zero
            for kx in range(3):
                meets = (row_cell + (out * cells + kx - 1)) >> 1 == lane_cell + inp * cells
                total = total + jnp.where(meets, taps[kx], zero)
            ref[lead + (pl.ds(out * 128, 128), pl.ds(at + inp * 128, 128))] = total.astype(BF)


def pool_matrix(channels, half):
    cells = 128 // channels
    lane, row = iota((128, 128), 1), iota((128, 128), 0)
    meets = ((lane // channels + half * cells) >> 1 == row // channels) & (
        lane % channels == row % channels
    )
    return meets.astype(F32).astype(BF)


def rolled(v, steps):
    return pltpu.roll(v, steps % v.shape[0], 0)


def edge_rows(w, first):
    group = iota((16, 128), 1) // 16
    total = jnp.zeros((16, 128), F32)
    for ky in range(3):
        total = jnp.where(group == first + ky, w[ky * 16 : ky * 16 + 16], total)
    return total


def plane_weights_kernel(w_ref, b_in, b_mid, b_low, b_deep, b_up, b_pool, b_last):
    edge = [nn(w_ref[kx, 192:208], lane_spread(32, 16, 0, 512)) for kx in range(3)]
    w_row = edge[0][3:4]
    xi = iota((32, 512), 0)
    xo = iota((32, 512), 1) // 16
    group = iota((32, 128), 1) // 16
    cell = jnp.where(group % 4 == 3, -9, jnp.where(group < 4, 16, 15))
    for ky in range(3):
        total = jnp.zeros((32, 512), F32)
        extra = jnp.zeros((32, 128), F32)
        for kx in range(3):
            tap = edge[kx][ky : ky + 1]
            total = jnp.where(xi == xo + (kx - 1), tap, total)
            extra = jnp.where(xi[:, :128] == cell + (kx - 1), tap[:, :128], extra)
        b_in[ky * 32 : (ky + 1) * 32, :512] = total.astype(BF)
        b_in[ky * 32 : (ky + 1) * 32, 512:] = extra.astype(BF)
    b_in[96:128] = jnp.zeros((32, 640), BF)
    spread = lane_spread(32, 16, 0, 128)
    w_mid, w_low, w_deep, w_skip = (
        [nn(w_ref[kx, at : at + 48], spread) for kx in range(3)] for at in (0, 48, 96, 144)
    )
    w_rise = [nn(w_ref[kx, 144:192], lane_spread(32, 16, 16, 128)) for kx in range(3)]
    for ky in range(3):
        for w, b_ref in ((w_mid, b_mid), (w_low, b_low), (w_deep, b_deep), (w_skip, b_up)):
            same_level(b_ref, ky * 256, 2, [stacked(w[kx], ky, 16) for kx in range(3)], 16)
        taps = [stacked(w_rise[kx], ky, 16) for kx in range(3)]
        from_coarse(b_up, (), 768 + ky * 128, 2, 1, taps, 16)
    b_mid[:, 768:] = jnp.zeros((256, 256), BF)
    b_mid[240:256, 768:896] = edge_rows(w_mid[2], 0).astype(BF)
    b_mid[0:16, 896:1024] = edge_rows(w_mid[0], 4).astype(BF)
    b_up[:, 1152:] = jnp.zeros((256, 256), BF)
    b_up[240:256, 1152:1280] = (edge_rows(w_skip[2], 0) + edge_rows(w_rise[2], 4)).astype(BF)
    b_up[0:16, 1280:1408] = (edge_rows(w_skip[0], 0) + edge_rows(w_rise[0], 4)).astype(BF)
    none = jnp.zeros((128, 128), BF)
    for out in range(2):
        for inp in range(4):
            b_pool[out * 128 : (out + 1) * 128, inp * 128 : (inp + 1) * 128] = (
                pool_matrix(16, inp % 2) if inp // 2 == out else none
            )
    o = iota((256, 512), 0)
    group = o % 128 // 16
    place = 128 - o // 128 * 16 + o % 16
    place = jnp.where(group < 4, place, place + 256)
    picks = (iota((256, 512), 1) == place) & (group % 4 < 3)
    b_pool[256:512] = picks.astype(F32).astype(BF)
    to_lane, cell = iota((128, 512), 0), iota((128, 512), 1) // 16
    for q in range(4):
        b_last[q] = jnp.where(to_lane == q * 32 + cell, w_row, 0.0).astype(BF)


def denoise_kernel(rim, planes_ref, *refs):
    before_ref = refs[0] if rim else None
    refs = refs[rim:]
    b_in, b_mid, b_low, b_deep, b_up, b_pool, b_last, out_ref = refs[:8]
    lhs, wide, coarse, half, raised, vol = refs[8:]
    planes = 2
    low_rows = planes * 128

    def place(ref, at, width, v, length):
        n = v.shape[0]
        row = iota(v.shape, 0) % length
        ref[:n, at : at + width] = jnp.where(row == 0, 0.0, rolled(v, 1)).astype(BF)
        ref[:n, at + width : at + 2 * width] = v.astype(BF)
        ref[:n, at + 2 * width : at + 3 * width] = jnp.where(
            row == length - 1, 0.0, rolled(v, -1)
        ).astype(BF)

    turned = planes_ref[...].astype(F32).reshape(64, 256)
    turned = jnp.concatenate([turned, jnp.zeros((64, 256), F32)], axis=0).T
    row = iota((256, 128), 0)
    lane = iota((256, 128), 1)
    before = jnp.where(row == 0, 0.0, rolled(turned, 1))
    after = jnp.where(row == 255, 0.0, rolled(turned, -1))
    def taps_apart(v, length):
        r, group = iota(v.shape, 0) % length, iota(v.shape, 1) // 16 % 4
        down = jnp.where(r == 0, 0.0, rolled(v, 1))
        up = jnp.where(r == length - 1, 0.0, rolled(v, -1))
        return jnp.where(group == 0, down, jnp.where(group == 1, v, up)).astype(BF)

    def lanes(ref, *pieces):
        return jnp.concatenate([ref[:, at : at + size] for at, size in pieces], axis=1)

    for q in range(planes):
        three = jnp.zeros((256, 128), F32)
        for g, v in enumerate((before, turned, after)):
            three = jnp.where(lane // 32 == g, pltpu.roll(v, ((g - q) * 32) % 128, 1), three)
        first = jnp.maximum(nn(three.astype(BF), b_in[...]), 0.0)
        rows_q = slice(q * 256, (q + 1) * 256)
        place(lhs.at[rows_q], 0, 512, first[:, :512], 256)
        lhs[rows_q, 1536:] = taps_apart(first[:, 512:], 256)
    halves = []
    for x in range(2):
        cells = [(ky * 512 + x * 256, 256) for ky in range(3)]
        bands = lanes(b_mid, (0, 768), (768 + x * 128, 128))
        halves.append(jnp.maximum(nt(lanes(lhs, *cells, (1536, 128)), bands), 0.0))
    skip = jnp.concatenate(halves, axis=1)
    place(wide, 0, 512, skip, 256)
    fine = nt(skip.astype(BF), b_pool[:256])
    for c in range(2):
        half[...] = fine[:, c * 128 : (c + 1) * 128]
        coarse[:, c * 128 : (c + 1) * 128] = 0.25 * (
            half[pl.ds(0, low_rows, stride=2), :] + half[pl.ds(1, low_rows, stride=2), :]
        )
    place(lhs.at[:low_rows], 0, 256, coarse[...], 128)
    low = jnp.maximum(nt(lhs[:low_rows, :768], b_low[...]), 0.0)
    place(lhs.at[:low_rows], 768, 256, low, 128)
    deep = jnp.maximum(nt(lhs[:low_rows, 768:1536], b_deep[...]), 0.0)
    for c in range(2):
        part = deep[:, c * 128 : (c + 1) * 128]
        half[pl.ds(0, low_rows, stride=2), :] = part
        half[pl.ds(1, low_rows, stride=2), :] = part
        raised[:, c * 128 : (c + 1) * 128] = half[...]
    place(wide, 1536, 256, raised[...], 256)
    wide[:, 2304:] = taps_apart(nt(lanes(wide, (640, 256), (1792, 256)), b_pool[256:]), 256)
    halves = []
    for x in range(2):
        cells = [(ky * 512 + x * 256, 256) for ky in range(3)]
        cells += [(1536 + ky * 256 + x * 128, 128) for ky in range(3)]
        bands = lanes(b_up, (0, 1152), (1152 + x * 128, 128))
        halves.append(jnp.maximum(nt(lanes(wide, *cells, (2304 + x * 128, 128)), bands), 0.0))
    joined = jnp.concatenate(halves, axis=1).astype(BF)
    total = jnp.zeros((256, 128), F32)
    for q in range(planes):
        total = total + nt(joined[q * 256 : (q + 1) * 256], b_last[2 * rim + q])
    vol[0:8] = jnp.zeros((8, 128), F32)
    vol[264:272] = jnp.zeros((8, 128), F32)
    vol[8:264] = total
    for z in range(NZ):
        window = vol[z * 32 : z * 32 + 48]
        if before_ref is not None:
            window = window + before_ref[z].astype(F32)
        out_ref[z] = window.astype(BF)


def volume_weights_kernel(w_ref, b_rest, b_mid, b_skip, b_rise):
    edge = [nn(w_ref[kxy, 72:88], lane_spread(16, 8, 0, 256)) for kxy in range(9)]
    spread = lane_spread(16, 8, 0, 128)
    w_mid, w_low, w_skip = (
        [nn(w_ref[kxy, at : at + 24], spread) for kxy in range(9)] for at in (0, 24, 48)
    )
    w_rise = [nn(w_ref[kxy, 48:72], lane_spread(16, 8, 8, 128)) for kxy in range(9)]
    xi = iota((32, 256), 0)
    xo = iota((32, 256), 1) // 8
    for ky in range(3):
        for kz in range(3):
            plain = jnp.zeros((32, 256), F32)
            mirror = jnp.zeros((32, 256), F32)
            for kx in range(3):
                tap = edge[kx * 3 + ky][kz : kz + 1]
                plain = jnp.where(xi == xo + (kx - 1), tap, plain)
                mirror = jnp.where(xi == (32 - kx) - xo, tap, mirror)
            at = kz * 32
            b_rest[ky, at : at + 32, :256] = plain.astype(BF)
            b_rest[ky, at : at + 32, 256:512] = mirror.astype(BF)
        b_rest[ky, 96:128, :512] = jnp.zeros((32, 512), BF)
    for ky in range(3):
        for kz in range(3):
            for w, b_ref in ((w_mid, b_mid), (w_skip, b_skip)):
                taps = [stacked(w[kx * 3 + ky], kz, 8) for kx in range(3)]
                for side, part in enumerate(band_parts(taps, 8)):
                    at = (kz * 3 + side) * 128
                    b_ref[ky, :, at : at + 128] = part
            taps = [stacked(w_low[kx * 3 + ky], kz, 8) for kx in range(3)]
            same_level(b_rest.at[ky], 512 + kz * 128, 1, taps, 8)
            taps = [stacked(w_rise[kx * 3 + ky], kz, 8) for kx in range(3)]
            from_coarse(b_rise, (ky,), kz * 128, 2, 1, taps, 8)
    w_out = edge[0][8:16].astype(BF)
    row_r = iota((128, 256), 0)
    cell = iota((128, 256), 1) // 8
    pick = (iota((128, 8), 1) == (iota((128, 8), 0) // 4) % 4 + 4 * lax.axis_index("rep"))
    w_rows = nn(pick.astype(F32).astype(BF), w_out)
    x_row = (row_r // 16) * 4 + row_r % 4
    b_rest[0, :, 896:] = jnp.where(cell == x_row, w_rows, 0.0).astype(BF)
    b_rest[1, :, 896:] = jnp.where(31 - cell == x_row, w_rows, 0.0).astype(BF)


def segment_kernel(v_ref, b_rest, b_mid, b_skip, b_rise, out_ref, vz, vl, h1l, pool, ql, rise, l4):
    at_i, at_z, at_c = (lax.axis_index(name) for name in ("i", "z", "c"))
    out_lane = iota((128, 512), 1)
    select = (
        (iota((128, 512), 0) == (out_lane // 128) * 32 + out_lane % 32) & (out_lane % 128 < 96)
    ).astype(F32).astype(BF)
    vz[...] = jnp.zeros(vz.shape, F32)
    for src in range(NZ):
        spread_v = nn(v_ref[src], select)
        for q in range(4):
            z_row = 8 + 2 * src + q
            if q >= 2:
                if src >= 5:
                    z_row = 2 * src + (q - 2) - 8
                elif src <= 2:
                    z_row = 24 + 2 * src + (q - 2)
                else:
                    continue
            vz[pl.ds(z_row, 48, stride=32), :] = spread_v[:, q * 128 : (q + 1) * 128]
    v = vz[...]
    lane = iota(v.shape, 1)
    v = jnp.where(lane < 32, rolled(v, 1), jnp.where(lane < 64, v, rolled(v, -1)))
    v = v.astype(BF).reshape(48, 32, 128)
    for ky in range(3):
        vl[:, :, ky * 128 : (ky + 1) * 128] = v[2 + ky : 44 + ky]

    z_base = 128 * at_c + 16 * at_i - 8
    y_base = 32 * at_z

    def inside(y_count, y_first, z_count, z_first, limit):
        z = iota((z_count, 128), 0) + z_first
        rows = ((z >= 0) & (z < limit)).astype(F32)
        return jnp.concatenate(
            [
                rows * jnp.where((y_first + y >= 0) & (y_first + y < limit), 1.0, 0.0)
                for y in range(y_count)
            ],
            axis=0,
        )

    def masked(v, mask):
        return jnp.maximum(v, 0.0) * jnp.concatenate([mask] * (v.shape[1] // 128), axis=1)

    part = 14
    for step in range(3):
        y0 = step * part
        n = part * 32
        h1 = nn(vl[y0 : y0 + part].reshape(n, 384), b_rest[:, :, :512].reshape(384, 512))
        mask = inside(part, y_base - 5 + y0, 32, z_base, 256)
        for copy in range(2):
            h = masked(h1[:, copy * 256 : (copy + 1) * 256], mask)
            for kz, steps in enumerate((1, 0, -1)):
                moved = rolled(h, steps) if steps else h
                h1l[copy, y0 : y0 + part, :, kz * 256 : (kz + 1) * 256] = moved.astype(BF).reshape(
                    part, 32, 256
                )

    pool_t = jnp.concatenate([pool_matrix(8, 0), pool_matrix(8, 1)], axis=1)
    logits = jnp.zeros((128, 512), F32)
    for copy in range(2):
        part = 20
        n = part * 32
        for step in range(2):
            y0 = step * part
            acc = jnp.zeros((n, 256), F32)
            for ky in range(3):
                acc = acc + nt(
                    h1l[copy, y0 + ky : y0 + ky + part].reshape(n, 768), two_blocks(b_mid, ky)
                )
            h2 = masked(acc, inside(part, y_base - 4 + y0, 32, z_base, 256))
            fine = nt(h2.astype(BF), pool_t).reshape(part // 2, 2, 32, 128)
            pool[y0 * 16 : y0 * 16 + n // 2] = (fine[:, 0] + fine[:, 1]).reshape(n // 2, 128)
            first, last = max(y0, 3), min(y0 + part, 37)
            for kz in range(3):
                moved = rolled(h2, -(7 + kz)).reshape(part, 32, 256)
                l4[copy, first - 3 : last - 3, :, kz * 256 : (kz + 1) * 256] = moved[
                    first - y0 : last - y0, :16
                ].astype(BF)
        q = 0.125 * (pool[pl.ds(0, 320, stride=2), :] + pool[pl.ds(1, 320, stride=2), :])
        for kz, steps in enumerate((1, 0, -1)):
            moved = rolled(q, steps) if steps else q
            ql[:, :, kz * 128 : (kz + 1) * 128] = moved.astype(BF).reshape(20, 16, 128)
        acc = jnp.zeros((288, 128), F32)
        for ky in range(3):
            acc = acc + nt(ql[ky : ky + 18].reshape(288, 384), b_rest[ky, :, 512:896])
        h3 = masked(
            acc, inside(18, 16 * at_z - 1, 16, 64 * at_c + 8 * at_i - 4, 128)
        )
        rise[pl.ds(0, 288, stride=2), :] = h3
        rise[pl.ds(1, 288, stride=2), :] = h3
        r = rise[...]
        for kz in range(3):
            moved = rolled(r, -(7 + kz)).reshape(18, 32, 128)[:, :16].astype(BF)
            for slot in range(34):
                l4[copy, slot, :, 768 + kz * 128 : 896 + kz * 128] = moved[(slot + 3) // 2 - 1]
        acc = jnp.zeros((512, 256), F32)
        for ky in range(3):
            bands = jnp.concatenate([two_blocks(b_skip, ky), b_rise[ky]], axis=1)
            acc = acc + nt(l4[copy, ky : ky + 32].reshape(512, 1152), bands)
        h4 = jnp.maximum(acc, 0.0).astype(BF)
        logits = logits + nt(b_rest[copy, :, 896:], h4)
    out_ref[...] = (0.5 * logits).astype(BF).reshape(NI, 16, 512)


def arrange_kernel(parts_ref, out_ref):
    lane = iota((16, 128), 1) // 16
    for o in range(4):
        parts = [parts_ref[src, :, o * 128 : (o + 1) * 128].astype(F32) for src in range(NI)]
        for bit in (1, 2, 4):
            upper = (lane & bit) != 0
            for low in range(NI):
                if low & bit == 0:
                    first, second = parts[low], parts[low | bit]
                    parts[low] = jnp.where(upper, pltpu.roll(second, 16 * bit, 1), first)
                    parts[low | bit] = jnp.where(upper, second, pltpu.roll(first, 128 - 16 * bit, 1))
        for y in range(8):
            out_ref[pl.ds(o * 8 + y, 16, stride=32), :] = parts[y]


def call(kernel, out_shape, scratch, megabytes, *args):
    spec = pl.BlockSpec(memory_space=pltpu.VMEM)
    return pl.pallas_call(
        kernel,
        out_shape=out_shape,
        in_specs=[spec] * len(args),
        out_specs=jax.tree.map(lambda _: spec, out_shape),
        scratch_shapes=scratch,
        compiler_params=pltpu.CompilerParams(vmem_limit_bytes=megabytes * 1024 * 1024),
    )(*args)


def bf(*shape):
    return jax.ShapeDtypeStruct(shape, BF)


def table(lead, rows, width, *weights):
    total = 0
    for at, w in weights:
        size = w.shape
        total = total + jnp.pad(
            w, ((0, lead - size[0]), (at, rows - at - size[1]), (0, width - size[2]))
        )
    return total


def taps2(w):
    return w.transpose(2, 3, 0, 1).reshape(3, -1, w.shape[1])


def taps3(w):
    return w.transpose(2, 3, 4, 0, 1).reshape(9, -1, w.shape[1])


def rim_pairs():
    def index(i, z, c):
        return (i * NZ + z) * NC + c

    pairs = []
    for z in range(NZ):
        if z >= NZ - 3:
            step, edge, wrapped = 1, NI - 1, 0
        elif z <= 2:
            step, edge, wrapped = -1, 0, 1
        else:
            continue
        for i in range(NI):
            for c in range(NC):
                if i != edge:
                    pairs.append((index(i, z, c), index(i + step, z, c)))
                elif c == wrapped:
                    pairs.append((index(i, z, c), index((i + step) % NI, z, 1 - c)))
    return pairs


def denoise(rim, planes, before, weights):
    args = (planes, before) if rim else (planes,)
    count = 2
    vmem = pltpu.VMEM
    return call(
        functools.partial(denoise_kernel, rim),
        bf(NZ, 48, 128),
        [
            vmem((count * 256, 1664), BF),
            vmem((count * 256, 2560), BF),
            vmem((count * 128, 256), F32),
            vmem((count * 256, 128), F32),
            vmem((count * 256, 256), F32),
            vmem((272, 128), F32),
        ],
        24,
        *args,
        *weights,
    )


def per_device(
    noisy, w2_in, w2_mid, w2_low, w2_deep, w2_up, w2_out, w3_in, w3_mid, w3_low, w3_up, w3_out
):
    near = noisy.reshape(2, 32, 256)
    far = lax.ppermute(near, "c", [(0, 1), (1, 0)])
    kernels = ((0, w2_mid), (48, w2_low), (96, w2_deep), (144, w2_up))
    taps = [(at, taps2(w)) for at, w in kernels]
    taps += [(192, w2_in.transpose(1, 2, 3, 0)[0]), (195, w2_out[None])]
    weights = call(
        plane_weights_kernel,
        [
            bf(128, 640),
            bf(256, 1024),
            bf(256, 768),
            bf(256, 768),
            bf(256, 1408),
            bf(512, 512),
            bf(4, 128, 512),
        ],
        [],
        16,
        table(3, 208, 32, *taps),
    )
    second = lax.axis_index("c") == 1
    own = jnp.stack([jnp.where(second, far[1], near[0]), jnp.where(second, near[1], far[0])])
    rim = lax.ppermute(own, ("i", "z", "c"), rim_pairs())
    volume = denoise(0, own, None, weights)
    volume = denoise(1, rim, volume, weights)
    taps = [(at, taps3(w)) for at, w in ((0, w3_mid), (24, w3_low), (48, w3_up))]
    taps += [(72, w3_in.transpose(1, 2, 3, 4, 0).reshape(9, 3, 8)), (80, w3_out[None])]
    bands = call(volume_weights_kernel, [bf(3, 128, 1152), bf(3, 128, 1152), bf(3, 128, 1152), bf(3, 256, 384)], [], 16, table(9, 88, 16, *taps))
    window = lax.all_to_all(volume, "z", 0, 0, tiled=True)
    vmem = pltpu.VMEM
    logits = call(
        segment_kernel,
        bf(NI, 16, 512),
        [
            vmem((48 * 32, 128), F32),
            vmem((42, 32, 384), BF),
            vmem((2, 42, 32, 768), BF),
            vmem((640, 128), F32),
            vmem((20, 16, 384), BF),
            vmem((576, 128), F32),
            vmem((2, 34, 16, 1152), BF),
        ],
        24,
        window,
        *bands,
    )
    parts = lax.all_to_all(logits, "i", 0, 0, tiled=True)
    out = call(arrange_kernel, jax.ShapeDtypeStruct((512, 128), F32), [], 4, parts)
    return out.reshape(1, 4, 4, 32, 128)


def solution(mesh):
    finer = Mesh(mesh.devices.reshape(2, NI, NZ, NC), ("rep", "i", "z", "c"))
    brick = ("i", "z", "c")
    placed = (P(None, brick, None, None),) + (P(),) * 11
    return jax.shard_map(
        per_device,
        mesh=finer,
        in_specs=placed,
        out_specs=P(brick, "rep", None, None, None),
        check_vma=False,
    )
```

```python
import functools

import jax
import jax.numpy as jnp
from jax import lax
from jax.experimental import pallas as pl
from jax.experimental.pallas import tpu as pltpu
from jax.sharding import Mesh
from jax.sharding import PartitionSpec as P

BF = jnp.bfloat16
F32 = jnp.float32
NI, NZ, NC = 8, 8, 2


def iota(shape, dim):
    return lax.broadcasted_iota(jnp.int32, shape, dim)


def nn(a, b):
    return lax.dot_general(a, b, (((1,), (0,)), ((), ())), preferred_element_type=F32)


def nt(a, b):
    return lax.dot_general(a, b, (((1,), (1,)), ((), ())), preferred_element_type=F32)


def lane_spread(rows, channels, first, lanes):
    return (iota((rows, lanes), 1) % channels + first == iota((rows, lanes), 0)).astype(
        F32
    ).astype(BF)


def stacked(taps, at, channels):
    return jnp.concatenate([taps[at * channels : (at + 1) * channels]] * (128 // channels), axis=0)


def band_parts(taps, channels):
    cells = 128 // channels
    gap = iota((128, 128), 1) // channels - iota((128, 128), 0) // channels
    zero = jnp.zeros((128, 128), F32)
    own = jnp.where(
        gap == 0, taps[1], jnp.where(gap == -1, taps[0], jnp.where(gap == 1, taps[2], zero))
    )
    later = jnp.where(gap == 1 - cells, taps[2], zero)
    earlier = jnp.where(gap == cells - 1, taps[0], zero)
    return [part.astype(BF) for part in (own, later, earlier)]


def same_level(ref, at, blocks, taps, channels):
    own, later, earlier = band_parts(taps, channels)
    for out in range(blocks):
        for inp in range(blocks):
            if inp == out:
                block = own
            elif inp == out + 1:
                block = later
            elif inp == out - 1:
                block = earlier
            else:
                block = jnp.zeros((128, 128), BF)
            ref[out * 128 : (out + 1) * 128, at + inp * 128 : at + (inp + 1) * 128] = block


def two_blocks(ref, ky):
    parts = [ref[ky, :, at * 128 : (at + 1) * 128] for at in range(9)]
    rows = [[], []]
    for own, later, earlier in (parts[0:3], parts[3:6], parts[6:9]):
        rows[0] += [own, later]
        rows[1] += [earlier, own]
    return jnp.concatenate([jnp.concatenate(row, axis=1) for row in rows], axis=0)


def from_coarse(ref, lead, at, out_blocks, in_blocks, taps, channels):
    cells = 128 // channels
    lane_cell = iota((128, 128), 1) // channels
    row_cell = iota((128, 128), 0) // channels
    zero = jnp.zeros((128, 128), F32)
    for out in range(out_blocks):
        for inp in range(in_blocks):
            total = zero
            for kx in range(3):
                meets = (row_cell + (out * cells + kx - 1)) >> 1 == lane_cell + inp * cells
                total = total + jnp.where(meets, taps[kx], zero)
            ref[lead + (pl.ds(out * 128, 128), pl.ds(at + inp * 128, 128))] = total.astype(BF)


def pool_matrix(channels, half):
    cells = 128 // channels
    lane, row = iota((128, 128), 1), iota((128, 128), 0)
    meets = ((lane // channels + half * cells) >> 1 == row // channels) & (
        lane % channels == row % channels
    )
    return meets.astype(F32).astype(BF)


def rolled(v, steps):
    return pltpu.roll(v, steps % v.shape[0], 0)


def edge_rows(w, first):
    group = iota((16, 128), 1) // 16
    total = jnp.zeros((16, 128), F32)
    for ky in range(3):
        total = jnp.where(group == first + ky, w[ky * 16 : ky * 16 + 16], total)
    return total


def plane_weights_kernel(w_ref, b_in, b_mid, b_low, b_deep, b_up, b_pool, b_last):
    edge = [nn(w_ref[kx, 192:208], lane_spread(32, 16, 0, 512)) for kx in range(3)]
    w_row = edge[0][3:4]
    xi = iota((32, 512), 0)
    xo = iota((32, 512), 1) // 16
    group = iota((32, 128), 1) // 16
    cell = jnp.where(group % 4 == 3, -9, jnp.where(group < 4, 16, 15))
    for ky in range(3):
        total = jnp.zeros((32, 512), F32)
        extra = jnp.zeros((32, 128), F32)
        for kx in range(3):
            tap = edge[kx][ky : ky + 1]
            total = jnp.where(xi == xo + (kx - 1), tap, total)
            extra = jnp.where(xi[:, :128] == cell + (kx - 1), tap[:, :128], extra)
        b_in[ky * 32 : (ky + 1) * 32, :512] = total.astype(BF)
        b_in[ky * 32 : (ky + 1) * 32, 512:] = extra.astype(BF)
    b_in[96:128] = jnp.zeros((32, 640), BF)
    spread = lane_spread(32, 16, 0, 128)
    w_mid, w_low, w_deep, w_skip = (
        [nn(w_ref[kx, at : at + 48], spread) for kx in range(3)] for at in (0, 48, 96, 144)
    )
    w_rise = [nn(w_ref[kx, 144:192], lane_spread(32, 16, 16, 128)) for kx in range(3)]
    for ky in range(3):
        for w, b_ref in ((w_mid, b_mid), (w_low, b_low), (w_deep, b_deep), (w_skip, b_up)):
            same_level(b_ref, ky * 256, 2, [stacked(w[kx], ky, 16) for kx in range(3)], 16)
        taps = [stacked(w_rise[kx], ky, 16) for kx in range(3)]
        from_coarse(b_up, (), 768 + ky * 128, 2, 1, taps, 16)
    b_mid[:, 768:] = jnp.zeros((256, 256), BF)
    b_mid[240:256, 768:896] = edge_rows(w_mid[2], 0).astype(BF)
    b_mid[0:16, 896:1024] = edge_rows(w_mid[0], 4).astype(BF)
    b_up[:, 1152:] = jnp.zeros((256, 256), BF)
    b_up[240:256, 1152:1280] = (edge_rows(w_skip[2], 0) + edge_rows(w_rise[2], 4)).astype(BF)
    b_up[0:16, 1280:1408] = (edge_rows(w_skip[0], 0) + edge_rows(w_rise[0], 4)).astype(BF)
    none = jnp.zeros((128, 128), BF)
    for out in range(2):
        for inp in range(4):
            b_pool[out * 128 : (out + 1) * 128, inp * 128 : (inp + 1) * 128] = (
                pool_matrix(16, inp % 2) if inp // 2 == out else none
            )
    o = iota((256, 512), 0)
    group = o % 128 // 16
    place = 128 - o // 128 * 16 + o % 16
    place = jnp.where(group < 4, place, place + 256)
    picks = (iota((256, 512), 1) == place) & (group % 4 < 3)
    b_pool[256:512] = picks.astype(F32).astype(BF)
    to_lane, cell = iota((128, 512), 0), iota((128, 512), 1) // 16
    for q in range(4):
        b_last[q] = jnp.where(to_lane == q * 32 + cell, w_row, 0.0).astype(BF)


def denoise_kernel(rim, planes_ref, *refs):
    before_ref = refs[0] if rim else None
    refs = refs[rim:]
    b_in, b_mid, b_low, b_deep, b_up, b_pool, b_last, out_ref = refs[:8]
    lhs, wide, coarse, half, raised, vol = refs[8:]
    planes = 2
    low_rows = planes * 128

    def place(ref, at, width, v, length):
        n = v.shape[0]
        row = iota(v.shape, 0) % length
        ref[:n, at : at + width] = jnp.where(row == 0, 0.0, rolled(v, 1)).astype(BF)
        ref[:n, at + width : at + 2 * width] = v.astype(BF)
        ref[:n, at + 2 * width : at + 3 * width] = jnp.where(
            row == length - 1, 0.0, rolled(v, -1)
        ).astype(BF)

    turned = planes_ref[...].astype(F32).reshape(64, 256)
    turned = jnp.concatenate([turned, jnp.zeros((64, 256), F32)], axis=0).T
    row = iota((256, 128), 0)
    lane = iota((256, 128), 1)
    before = jnp.where(row == 0, 0.0, rolled(turned, 1))
    after = jnp.where(row == 255, 0.0, rolled(turned, -1))
    def taps_apart(v, length):
        r, group = iota(v.shape, 0) % length, iota(v.shape, 1) // 16 % 4
        down = jnp.where(r == 0, 0.0, rolled(v, 1))
        up = jnp.where(r == length - 1, 0.0, rolled(v, -1))
        return jnp.where(group == 0, down, jnp.where(group == 1, v, up)).astype(BF)

    def lanes(ref, *pieces):
        return jnp.concatenate([ref[:, at : at + size] for at, size in pieces], axis=1)

    for q in range(planes):
        three = jnp.zeros((256, 128), F32)
        for g, v in enumerate((before, turned, after)):
            three = jnp.where(lane // 32 == g, pltpu.roll(v, ((g - q) * 32) % 128, 1), three)
        first = jnp.maximum(nn(three.astype(BF), b_in[...]), 0.0)
        rows_q = slice(q * 256, (q + 1) * 256)
        place(lhs.at[rows_q], 0, 512, first[:, :512], 256)
        lhs[rows_q, 1536:] = taps_apart(first[:, 512:], 256)
    halves = []
    for x in range(2):
        cells = [(ky * 512 + x * 256, 256) for ky in range(3)]
        bands = lanes(b_mid, (0, 768), (768 + x * 128, 128))
        halves.append(jnp.maximum(nt(lanes(lhs, *cells, (1536, 128)), bands), 0.0))
    skip = jnp.concatenate(halves, axis=1)
    place(wide, 0, 512, skip, 256)
    fine = nt(skip.astype(BF), b_pool[:256])
    for c in range(2):
        half[...] = fine[:, c * 128 : (c + 1) * 128]
        coarse[:, c * 128 : (c + 1) * 128] = 0.25 * (
            half[pl.ds(0, low_rows, stride=2), :] + half[pl.ds(1, low_rows, stride=2), :]
        )
    place(lhs.at[:low_rows], 0, 256, coarse[...], 128)
    low = jnp.maximum(nt(lhs[:low_rows, :768], b_low[...]), 0.0)
    place(lhs.at[:low_rows], 768, 256, low, 128)
    deep = jnp.maximum(nt(lhs[:low_rows, 768:1536], b_deep[...]), 0.0)
    for c in range(2):
        part = deep[:, c * 128 : (c + 1) * 128]
        half[pl.ds(0, low_rows, stride=2), :] = part
        half[pl.ds(1, low_rows, stride=2), :] = part
        raised[:, c * 128 : (c + 1) * 128] = half[...]
    place(wide, 1536, 256, raised[...], 256)
    wide[:, 2304:] = taps_apart(nt(lanes(wide, (640, 256), (1792, 256)), b_pool[256:]), 256)
    halves = []
    for x in range(2):
        cells = [(ky * 512 + x * 256, 256) for ky in range(3)]
        cells += [(1536 + ky * 256 + x * 128, 128) for ky in range(3)]
        bands = lanes(b_up, (0, 1152), (1152 + x * 128, 128))
        halves.append(jnp.maximum(nt(lanes(wide, *cells, (2304 + x * 128, 128)), bands), 0.0))
    joined = jnp.concatenate(halves, axis=1).astype(BF)
    total = jnp.zeros((256, 128), F32)
    for q in range(planes):
        total = total + nt(joined[q * 256 : (q + 1) * 256], b_last[2 * rim + q])
    vol[0:8] = jnp.zeros((8, 128), F32)
    vol[264:272] = jnp.zeros((8, 128), F32)
    vol[8:264] = total
    for z in range(NZ):
        window = vol[z * 32 : z * 32 + 48]
        if before_ref is not None:
            window = window + before_ref[z].astype(F32)
        out_ref[z] = window.astype(BF)


def volume_weights_kernel(w_ref, b_rest, b_mid, b_skip, b_rise):
    edge = [nn(w_ref[kxy, 72:88], lane_spread(16, 8, 0, 256)) for kxy in range(9)]
    spread = lane_spread(16, 8, 0, 128)
    w_mid, w_low, w_skip = (
        [nn(w_ref[kxy, at : at + 24], spread) for kxy in range(9)] for at in (0, 24, 48)
    )
    w_rise = [nn(w_ref[kxy, 48:72], lane_spread(16, 8, 8, 128)) for kxy in range(9)]
    xi = iota((32, 256), 0)
    xo = iota((32, 256), 1) // 8
    for ky in range(3):
        for kz in range(3):
            plain = jnp.zeros((32, 256), F32)
            mirror = jnp.zeros((32, 256), F32)
            for kx in range(3):
                tap = edge[kx * 3 + ky][kz : kz + 1]
                plain = jnp.where(xi == xo + (kx - 1), tap, plain)
                mirror = jnp.where(xi == (32 - kx) - xo, tap, mirror)
            at = kz * 32
            b_rest[ky, at : at + 32, :256] = plain.astype(BF)
            b_rest[ky, at : at + 32, 256:512] = mirror.astype(BF)
        b_rest[ky, 96:128, :512] = jnp.zeros((32, 512), BF)
    for ky in range(3):
        for kz in range(3):
            for w, b_ref in ((w_mid, b_mid), (w_skip, b_skip)):
                taps = [stacked(w[kx * 3 + ky], kz, 8) for kx in range(3)]
                for side, part in enumerate(band_parts(taps, 8)):
                    at = (kz * 3 + side) * 128
                    b_ref[ky, :, at : at + 128] = part
            taps = [stacked(w_low[kx * 3 + ky], kz, 8) for kx in range(3)]
            same_level(b_rest.at[ky], 512 + kz * 128, 1, taps, 8)
            taps = [stacked(w_rise[kx * 3 + ky], kz, 8) for kx in range(3)]
            from_coarse(b_rise, (ky,), kz * 128, 2, 1, taps, 8)
    w_out = edge[0][8:16].astype(BF)
    row_r = iota((128, 256), 0)
    cell = iota((128, 256), 1) // 8
    pick = (iota((128, 8), 1) == (iota((128, 8), 0) // 4) % 4 + 4 * lax.axis_index("rep"))
    w_rows = nn(pick.astype(F32).astype(BF), w_out)
    x_row = (row_r // 16) * 4 + row_r % 4
    b_rest[0, :, 896:] = jnp.where(cell == x_row, w_rows, 0.0).astype(BF)
    b_rest[1, :, 896:] = jnp.where(31 - cell == x_row, w_rows, 0.0).astype(BF)


def segment_kernel(v_ref, b_rest, b_mid, b_skip, b_rise, out_ref, vz, vl, h1l, pool, ql, rise, l4):
    at_i, at_z, at_c = (lax.axis_index(name) for name in ("i", "z", "c"))
    out_lane = iota((128, 512), 1)
    select = (
        (iota((128, 512), 0) == (out_lane // 128) * 32 + out_lane % 32) & (out_lane % 128 < 96)
    ).astype(F32).astype(BF)
    vz[...] = jnp.zeros(vz.shape, F32)
    for src in range(NZ):
        spread_v = nn(v_ref[src], select)
        for q in range(4):
            z_row = 8 + 2 * src + q
            if q >= 2:
                if src >= 5:
                    z_row = 2 * src + (q - 2) - 8
                elif src <= 2:
                    z_row = 24 + 2 * src + (q - 2)
                else:
                    continue
            vz[pl.ds(z_row, 48, stride=32), :] = spread_v[:, q * 128 : (q + 1) * 128]
    v = vz[...]
    lane = iota(v.shape, 1)
    v = jnp.where(lane < 32, rolled(v, 1), jnp.where(lane < 64, v, rolled(v, -1)))
    v = v.astype(BF).reshape(48, 32, 128)
    for ky in range(3):
        vl[:, :, ky * 128 : (ky + 1) * 128] = v[2 + ky : 44 + ky]

    z_base = 128 * at_c + 16 * at_i - 8
    y_base = 32 * at_z

    def inside(y_count, y_first, z_count, z_first, limit):
        z = iota((z_count, 128), 0) + z_first
        rows = ((z >= 0) & (z < limit)).astype(F32)
        return jnp.concatenate(
            [
                rows * jnp.where((y_first + y >= 0) & (y_first + y < limit), 1.0, 0.0)
                for y in range(y_count)
            ],
            axis=0,
        )

    def masked(v, mask):
        return jnp.maximum(v, 0.0) * jnp.concatenate([mask] * (v.shape[1] // 128), axis=1)

    part = 14
    for step in range(3):
        y0 = step * part
        n = part * 32
        h1 = nn(vl[y0 : y0 + part].reshape(n, 384), b_rest[:, :, :512].reshape(384, 512))
        mask = inside(part, y_base - 5 + y0, 32, z_base, 256)
        for copy in range(2):
            h = masked(h1[:, copy * 256 : (copy + 1) * 256], mask)
            for kz in range(3):
                moved = rolled(h, -(3 + kz)).reshape(part, 32, 256)[:, :24].reshape(part * 24, 256)
                rows = slice(y0 * 24, (y0 + part) * 24)
                h1l[copy, rows, kz * 256 : (kz + 1) * 256] = moved.astype(BF)

    pool_t = jnp.concatenate([pool_matrix(8, 0), pool_matrix(8, 1)], axis=1)
    logits = jnp.zeros((128, 512), F32)
    for copy in range(2):
        part = 20
        n = part * 24
        for step in range(2):
            y0 = step * part
            acc = jnp.zeros((n, 256), F32)
            for ky in range(3):
                first = (y0 + ky) * 24
                acc = acc + nt(h1l[copy, first : first + n], two_blocks(b_mid, ky))
            h2 = masked(acc, inside(part, y_base - 4 + y0, 24, z_base + 4, 256))
            fine = nt(h2.astype(BF), pool_t).reshape(part // 2, 2, 24, 128)
            filled = [fine[:, 0] + fine[:, 1], jnp.zeros((part // 2, 8, 128), F32)]
            pool[y0 * 16 : (y0 + part) * 16] = jnp.concatenate(filled, axis=1).reshape(
                part * 16, 128
            )
            first, last = max(y0, 3), min(y0 + part, 37)
            for kz in range(3):
                moved = rolled(h2, -(3 + kz)).reshape(part, 24, 256)
                l4[copy, first - 3 : last - 3, :, kz * 256 : (kz + 1) * 256] = moved[
                    first - y0 : last - y0, :16
                ].astype(BF)
        q = 0.125 * (pool[pl.ds(0, 320, stride=2), :] + pool[pl.ds(1, 320, stride=2), :])
        for kz, steps in enumerate((1, 0, -1)):
            moved = rolled(q, steps) if steps else q
            ql[:, :, kz * 128 : (kz + 1) * 128] = moved.astype(BF).reshape(20, 16, 128)
        acc = jnp.zeros((288, 128), F32)
        for ky in range(3):
            acc = acc + nt(ql[ky : ky + 18].reshape(288, 384), b_rest[ky, :, 512:896])
        h3 = masked(
            acc, inside(18, 16 * at_z - 1, 16, 64 * at_c + 8 * at_i - 2, 128)
        )
        rise[pl.ds(0, 288, stride=2), :] = h3
        rise[pl.ds(1, 288, stride=2), :] = h3
        r = rise[...]
        for kz in range(3):
            moved = rolled(r, -(3 + kz)).reshape(18, 32, 128)[:, :16].astype(BF)
            for slot in range(34):
                l4[copy, slot, :, 768 + kz * 128 : 896 + kz * 128] = moved[(slot + 3) // 2 - 1]
        acc = jnp.zeros((512, 256), F32)
        for ky in range(3):
            bands = jnp.concatenate([two_blocks(b_skip, ky), b_rise[ky]], axis=1)
            acc = acc + nt(l4[copy, ky : ky + 32].reshape(512, 1152), bands)
        h4 = jnp.maximum(acc, 0.0).astype(BF)
        logits = logits + nt(b_rest[copy, :, 896:], h4)
    out_ref[...] = (0.5 * logits).astype(BF).reshape(NI, 16, 512)


def arrange_kernel(parts_ref, out_ref):
    lane = iota((16, 128), 1) // 16
    for o in range(4):
        parts = [parts_ref[src, :, o * 128 : (o + 1) * 128].astype(F32) for src in range(NI)]
        for bit in (1, 2, 4):
            upper = (lane & bit) != 0
            for low in range(NI):
                if low & bit == 0:
                    first, second = parts[low], parts[low | bit]
                    parts[low] = jnp.where(upper, pltpu.roll(second, 16 * bit, 1), first)
                    parts[low | bit] = jnp.where(upper, second, pltpu.roll(first, 128 - 16 * bit, 1))
        for y in range(8):
            out_ref[pl.ds(o * 8 + y, 16, stride=32), :] = parts[y]


def call(kernel, out_shape, scratch, megabytes, *args):
    spec = pl.BlockSpec(memory_space=pltpu.VMEM)
    return pl.pallas_call(
        kernel,
        out_shape=out_shape,
        in_specs=[spec] * len(args),
        out_specs=jax.tree.map(lambda _: spec, out_shape),
        scratch_shapes=scratch,
        compiler_params=pltpu.CompilerParams(vmem_limit_bytes=megabytes * 1024 * 1024),
    )(*args)


def bf(*shape):
    return jax.ShapeDtypeStruct(shape, BF)


def table(lead, rows, width, *weights):
    total = 0
    for at, w in weights:
        size = w.shape
        total = total + jnp.pad(
            w, ((0, lead - size[0]), (at, rows - at - size[1]), (0, width - size[2]))
        )
    return total


def taps2(w):
    return w.transpose(2, 3, 0, 1).reshape(3, -1, w.shape[1])


def taps3(w):
    return w.transpose(2, 3, 4, 0, 1).reshape(9, -1, w.shape[1])


def rim_pairs():
    def index(i, z, c):
        return (i * NZ + z) * NC + c

    pairs = []
    for z in range(NZ):
        if z >= NZ - 3:
            step, edge, wrapped = 1, NI - 1, 0
        elif z <= 2:
            step, edge, wrapped = -1, 0, 1
        else:
            continue
        for i in range(NI):
            for c in range(NC):
                if i != edge:
                    pairs.append((index(i, z, c), index(i + step, z, c)))
                elif c == wrapped:
                    pairs.append((index(i, z, c), index((i + step) % NI, z, 1 - c)))
    return pairs


def denoise(rim, planes, before, weights):
    args = (planes, before) if rim else (planes,)
    count = 2
    vmem = pltpu.VMEM
    return call(
        functools.partial(denoise_kernel, rim),
        bf(NZ, 48, 128),
        [
            vmem((count * 256, 1664), BF),
            vmem((count * 256, 2560), BF),
            vmem((count * 128, 256), F32),
            vmem((count * 256, 128), F32),
            vmem((count * 256, 256), F32),
            vmem((272, 128), F32),
        ],
        24,
        *args,
        *weights,
    )


def per_device(
    noisy, w2_in, w2_mid, w2_low, w2_deep, w2_up, w2_out, w3_in, w3_mid, w3_low, w3_up, w3_out
):
    near = noisy.reshape(2, 32, 256)
    far = lax.ppermute(near, "c", [(0, 1), (1, 0)])
    kernels = ((0, w2_mid), (48, w2_low), (96, w2_deep), (144, w2_up))
    taps = [(at, taps2(w)) for at, w in kernels]
    taps += [(192, w2_in.transpose(1, 2, 3, 0)[0]), (195, w2_out[None])]
    weights = call(
        plane_weights_kernel,
        [
            bf(128, 640),
            bf(256, 1024),
            bf(256, 768),
            bf(256, 768),
            bf(256, 1408),
            bf(512, 512),
            bf(4, 128, 512),
        ],
        [],
        16,
        table(3, 208, 32, *taps),
    )
    far, weights = lax.optimization_barrier((far, weights))
    second = lax.axis_index("c") == 1
    own = jnp.stack([jnp.where(second, far[1], near[0]), jnp.where(second, near[1], far[0])])
    rim = lax.ppermute(own, ("i", "z", "c"), rim_pairs())
    volume = denoise(0, own, None, weights)
    volume = denoise(1, rim, volume, weights)
    taps = [(at, taps3(w)) for at, w in ((0, w3_mid), (24, w3_low), (48, w3_up))]
    taps += [(72, w3_in.transpose(1, 2, 3, 4, 0).reshape(9, 3, 8)), (80, w3_out[None])]
    bands = call(volume_weights_kernel, [bf(3, 128, 1152), bf(3, 128, 1152), bf(3, 128, 1152), bf(3, 256, 384)], [], 16, table(9, 88, 16, *taps))
    window = lax.all_to_all(volume, "z", 0, 0, tiled=True)
    vmem = pltpu.VMEM
    logits = call(
        segment_kernel,
        bf(NI, 16, 512),
        [
            vmem((48 * 32, 128), F32),
            vmem((42, 32, 384), BF),
            vmem((2, 42 * 24, 768), BF),
            vmem((640, 128), F32),
            vmem((20, 16, 384), BF),
            vmem((576, 128), F32),
            vmem((2, 34, 16, 1152), BF),
        ],
        24,
        window,
        *bands,
    )
    parts = lax.all_to_all(logits, "i", 0, 0, tiled=True)
    out = call(arrange_kernel, jax.ShapeDtypeStruct((512, 128), F32), [], 4, parts)
    return out.reshape(1, 4, 4, 32, 128)


def solution(mesh):
    finer = Mesh(mesh.devices.reshape(2, NI, NZ, NC), ("rep", "i", "z", "c"))
    brick = ("i", "z", "c")
    placed = (P(None, brick, None, None),) + (P(),) * 11
    return jax.shard_map(
        per_device,
        mesh=finer,
        in_specs=placed,
        out_specs=P(brick, "rep", None, None, None),
        check_vma=False,
    )
```

```python
import functools

import jax
import jax.numpy as jnp
from jax import lax
from jax.experimental import pallas as pl
from jax.experimental.pallas import tpu as pltpu
from jax.sharding import Mesh
from jax.sharding import PartitionSpec as P

BF = jnp.bfloat16
F32 = jnp.float32
NI, NZ, NC = 8, 8, 2


def iota(shape, dim):
    return lax.broadcasted_iota(jnp.int32, shape, dim)


def nn(a, b):
    return lax.dot_general(a, b, (((1,), (0,)), ((), ())), preferred_element_type=F32)


def nt(a, b):
    return lax.dot_general(a, b, (((1,), (1,)), ((), ())), preferred_element_type=F32)


def lane_spread(rows, channels, first, lanes):
    return (iota((rows, lanes), 1) % channels + first == iota((rows, lanes), 0)).astype(
        F32
    ).astype(BF)


def stacked(taps, at, channels):
    return jnp.concatenate([taps[at * channels : (at + 1) * channels]] * (128 // channels), axis=0)


def band_parts(taps, channels):
    cells = 128 // channels
    gap = iota((128, 128), 1) // channels - iota((128, 128), 0) // channels
    zero = jnp.zeros((128, 128), F32)
    own = jnp.where(
        gap == 0, taps[1], jnp.where(gap == -1, taps[0], jnp.where(gap == 1, taps[2], zero))
    )
    later = jnp.where(gap == 1 - cells, taps[2], zero)
    earlier = jnp.where(gap == cells - 1, taps[0], zero)
    return [part.astype(BF) for part in (own, later, earlier)]


def same_level(ref, at, blocks, taps, channels):
    own, later, earlier = band_parts(taps, channels)
    for out in range(blocks):
        for inp in range(blocks):
            if inp == out:
                block = own
            elif inp == out + 1:
                block = later
            elif inp == out - 1:
                block = earlier
            else:
                block = jnp.zeros((128, 128), BF)
            ref[out * 128 : (out + 1) * 128, at + inp * 128 : at + (inp + 1) * 128] = block


def two_blocks(ref, ky):
    parts = [ref[ky, :, at * 128 : (at + 1) * 128] for at in range(9)]
    rows = [[], []]
    for own, later, earlier in (parts[0:3], parts[3:6], parts[6:9]):
        rows[0] += [own, later]
        rows[1] += [earlier, own]
    return jnp.concatenate([jnp.concatenate(row, axis=1) for row in rows], axis=0)


def from_coarse(ref, lead, at, out_blocks, in_blocks, taps, channels):
    cells = 128 // channels
    lane_cell = iota((128, 128), 1) // channels
    row_cell = iota((128, 128), 0) // channels
    zero = jnp.zeros((128, 128), F32)
    for out in range(out_blocks):
        for inp in range(in_blocks):
            total = zero
            for kx in range(3):
                meets = (row_cell + (out * cells + kx - 1)) >> 1 == lane_cell + inp * cells
                total = total + jnp.where(meets, taps[kx], zero)
            ref[lead + (pl.ds(out * 128, 128), pl.ds(at + inp * 128, 128))] = total.astype(BF)


def pool_matrix(channels, half):
    cells = 128 // channels
    lane, row = iota((128, 128), 1), iota((128, 128), 0)
    meets = ((lane // channels + half * cells) >> 1 == row // channels) & (
        lane % channels == row % channels
    )
    return meets.astype(F32).astype(BF)


def rolled(v, steps):
    return pltpu.roll(v, steps % v.shape[0], 0)


def edge_rows(w, first):
    group = iota((16, 128), 1) // 16
    total = jnp.zeros((16, 128), F32)
    for ky in range(3):
        total = jnp.where(group == first + ky, w[ky * 16 : ky * 16 + 16], total)
    return total


def plane_weights_kernel(w_ref, b_in, b_mid, b_low, b_deep, b_up, b_pool, b_last):
    edge = [nn(w_ref[kx, 192:208], lane_spread(32, 16, 0, 512)) for kx in range(3)]
    w_row = edge[0][3:4]
    xi = iota((32, 512), 0)
    xo = iota((32, 512), 1) // 16
    group = iota((32, 128), 1) // 16
    cell = jnp.where(group % 4 == 3, -9, jnp.where(group < 4, 16, 15))
    for ky in range(3):
        total = jnp.zeros((32, 512), F32)
        extra = jnp.zeros((32, 128), F32)
        for kx in range(3):
            tap = edge[kx][ky : ky + 1]
            total = jnp.where(xi == xo + (kx - 1), tap, total)
            extra = jnp.where(xi[:, :128] == cell + (kx - 1), tap[:, :128], extra)
        b_in[ky * 32 : (ky + 1) * 32, :512] = total.astype(BF)
        b_in[ky * 32 : (ky + 1) * 32, 512:] = extra.astype(BF)
    b_in[96:128] = jnp.zeros((32, 640), BF)
    spread = lane_spread(32, 16, 0, 128)
    w_mid, w_low, w_deep, w_skip = (
        [nn(w_ref[kx, at : at + 48], spread) for kx in range(3)] for at in (0, 48, 96, 144)
    )
    w_rise = [nn(w_ref[kx, 144:192], lane_spread(32, 16, 16, 128)) for kx in range(3)]
    for ky in range(3):
        for w, b_ref in ((w_mid, b_mid), (w_low, b_low), (w_deep, b_deep), (w_skip, b_up)):
            same_level(b_ref, ky * 256, 2, [stacked(w[kx], ky, 16) for kx in range(3)], 16)
        taps = [stacked(w_rise[kx], ky, 16) for kx in range(3)]
        from_coarse(b_up, (), 768 + ky * 128, 2, 1, taps, 16)
    b_mid[:, 768:] = jnp.zeros((256, 256), BF)
    b_mid[240:256, 768:896] = edge_rows(w_mid[2], 0).astype(BF)
    b_mid[0:16, 896:1024] = edge_rows(w_mid[0], 4).astype(BF)
    b_up[:, 1152:] = jnp.zeros((256, 256), BF)
    b_up[240:256, 1152:1280] = (edge_rows(w_skip[2], 0) + edge_rows(w_rise[2], 4)).astype(BF)
    b_up[0:16, 1280:1408] = (edge_rows(w_skip[0], 0) + edge_rows(w_rise[0], 4)).astype(BF)
    none = jnp.zeros((128, 128), BF)
    for out in range(2):
        for inp in range(4):
            b_pool[out * 128 : (out + 1) * 128, inp * 128 : (inp + 1) * 128] = (
                pool_matrix(16, inp % 2) if inp // 2 == out else none
            )
    o = iota((256, 512), 0)
    group = o % 128 // 16
    place = 128 - o // 128 * 16 + o % 16
    place = jnp.where(group < 4, place, place + 256)
    picks = (iota((256, 512), 1) == place) & (group % 4 < 3)
    b_pool[256:512] = picks.astype(F32).astype(BF)
    to_lane, cell = iota((128, 512), 0), iota((128, 512), 1) // 16
    for q in range(4):
        b_last[q] = jnp.where(to_lane == q * 32 + cell, w_row, 0.0).astype(BF)


def denoise_kernel(rim, planes_ref, *refs):
    before_ref = refs[0] if rim else None
    refs = refs[rim:]
    b_in, b_mid, b_low, b_deep, b_up, b_pool, b_last, out_ref = refs[:8]
    lhs, wide, coarse, half, raised, vol = refs[8:]
    planes = 2
    low_rows = planes * 128

    def place(ref, at, width, v, length):
        n = v.shape[0]
        row = iota(v.shape, 0) % length
        ref[:n, at : at + width] = jnp.where(row == 0, 0.0, rolled(v, 1)).astype(BF)
        ref[:n, at + width : at + 2 * width] = v.astype(BF)
        ref[:n, at + 2 * width : at + 3 * width] = jnp.where(
            row == length - 1, 0.0, rolled(v, -1)
        ).astype(BF)

    turned = planes_ref[...].astype(F32).reshape(64, 256)
    turned = jnp.concatenate([turned, jnp.zeros((64, 256), F32)], axis=0).T
    row = iota((256, 128), 0)
    lane = iota((256, 128), 1)
    before = jnp.where(row == 0, 0.0, rolled(turned, 1))
    after = jnp.where(row == 255, 0.0, rolled(turned, -1))
    def taps_apart(v, length):
        r, group = iota(v.shape, 0) % length, iota(v.shape, 1) // 16 % 4
        down = jnp.where(r == 0, 0.0, rolled(v, 1))
        up = jnp.where(r == length - 1, 0.0, rolled(v, -1))
        return jnp.where(group == 0, down, jnp.where(group == 1, v, up)).astype(BF)

    def lanes(ref, *pieces):
        return jnp.concatenate([ref[:, at : at + size] for at, size in pieces], axis=1)

    for q in range(planes):
        three = jnp.zeros((256, 128), F32)
        for g, v in enumerate((before, turned, after)):
            three = jnp.where(lane // 32 == g, pltpu.roll(v, ((g - q) * 32) % 128, 1), three)
        first = jnp.maximum(nn(three.astype(BF), b_in[...]), 0.0)
        rows_q = slice(q * 256, (q + 1) * 256)
        place(lhs.at[rows_q], 0, 512, first[:, :512], 256)
        lhs[rows_q, 1536:] = taps_apart(first[:, 512:], 256)
    halves = []
    for x in range(2):
        cells = [(ky * 512 + x * 256, 256) for ky in range(3)]
        bands = lanes(b_mid, (0, 768), (768 + x * 128, 128))
        halves.append(jnp.maximum(nt(lanes(lhs, *cells, (1536, 128)), bands), 0.0))
    skip = jnp.concatenate(halves, axis=1)
    place(wide, 0, 512, skip, 256)
    fine = nt(skip.astype(BF), b_pool[:256])
    for c in range(2):
        half[...] = fine[:, c * 128 : (c + 1) * 128]
        coarse[:, c * 128 : (c + 1) * 128] = 0.25 * (
            half[pl.ds(0, low_rows, stride=2), :] + half[pl.ds(1, low_rows, stride=2), :]
        )
    place(lhs.at[:low_rows], 0, 256, coarse[...], 128)
    low = jnp.maximum(nt(lhs[:low_rows, :768], b_low[...]), 0.0)
    place(lhs.at[:low_rows], 768, 256, low, 128)
    deep = jnp.maximum(nt(lhs[:low_rows, 768:1536], b_deep[...]), 0.0)
    for c in range(2):
        part = deep[:, c * 128 : (c + 1) * 128]
        half[pl.ds(0, low_rows, stride=2), :] = part
        half[pl.ds(1, low_rows, stride=2), :] = part
        raised[:, c * 128 : (c + 1) * 128] = half[...]
    place(wide, 1536, 256, raised[...], 256)
    wide[:, 2304:] = taps_apart(nt(lanes(wide, (640, 256), (1792, 256)), b_pool[256:]), 256)
    halves = []
    for x in range(2):
        cells = [(ky * 512 + x * 256, 256) for ky in range(3)]
        cells += [(1536 + ky * 256 + x * 128, 128) for ky in range(3)]
        bands = lanes(b_up, (0, 1152), (1152 + x * 128, 128))
        halves.append(jnp.maximum(nt(lanes(wide, *cells, (2304 + x * 128, 128)), bands), 0.0))
    joined = jnp.concatenate(halves, axis=1).astype(BF)
    total = jnp.zeros((256, 128), F32)
    for q in range(planes):
        total = total + nt(joined[q * 256 : (q + 1) * 256], b_last[2 * rim + q])
    vol[0:8] = jnp.zeros((8, 128), F32)
    vol[264:272] = jnp.zeros((8, 128), F32)
    vol[8:264] = total
    for z in range(NZ):
        window = vol[z * 32 : z * 32 + 48]
        if before_ref is not None:
            window = window + before_ref[z].astype(F32)
        out_ref[z] = window.astype(BF)


def volume_weights_kernel(w_ref, b_rest, b_mid, b_skip, b_rise):
    edge = [nn(w_ref[kxy, 72:88], lane_spread(16, 8, 0, 256)) for kxy in range(9)]
    spread = lane_spread(16, 8, 0, 128)
    w_mid, w_low, w_skip = (
        [nn(w_ref[kxy, at : at + 24], spread) for kxy in range(9)] for at in (0, 24, 48)
    )
    w_rise = [nn(w_ref[kxy, 48:72], lane_spread(16, 8, 8, 128)) for kxy in range(9)]
    xi = iota((32, 256), 0)
    xo = iota((32, 256), 1) // 8
    for ky in range(3):
        for kz in range(3):
            plain = jnp.zeros((32, 256), F32)
            mirror = jnp.zeros((32, 256), F32)
            for kx in range(3):
                tap = edge[kx * 3 + ky][kz : kz + 1]
                plain = jnp.where(xi == xo + (kx - 1), tap, plain)
                mirror = jnp.where(xi == (32 - kx) - xo, tap, mirror)
            at = kz * 32
            b_rest[ky, at : at + 32, :256] = plain.astype(BF)
            b_rest[ky, at : at + 32, 256:512] = mirror.astype(BF)
        b_rest[ky, 96:128, :512] = jnp.zeros((32, 512), BF)
    for ky in range(3):
        for kz in range(3):
            for w, b_ref in ((w_mid, b_mid), (w_skip, b_skip)):
                taps = [stacked(w[kx * 3 + ky], kz, 8) for kx in range(3)]
                for side, part in enumerate(band_parts(taps, 8)):
                    at = (kz * 3 + side) * 128
                    b_ref[ky, :, at : at + 128] = part
            taps = [stacked(w_low[kx * 3 + ky], kz, 8) for kx in range(3)]
            same_level(b_rest.at[ky], 512 + kz * 128, 1, taps, 8)
            taps = [stacked(w_rise[kx * 3 + ky], kz, 8) for kx in range(3)]
            from_coarse(b_rise, (ky,), kz * 128, 2, 1, taps, 8)
    w_out = edge[0][8:16].astype(BF)
    row_r = iota((128, 256), 0)
    cell = iota((128, 256), 1) // 8
    pick = (iota((128, 8), 1) == (iota((128, 8), 0) // 4) % 4 + 4 * lax.axis_index("rep"))
    w_rows = nn(pick.astype(F32).astype(BF), w_out)
    x_row = (row_r // 16) * 4 + row_r % 4
    b_rest[0, :, 896:] = jnp.where(cell == x_row, w_rows, 0.0).astype(BF)
    b_rest[1, :, 896:] = jnp.where(31 - cell == x_row, w_rows, 0.0).astype(BF)


def segment_kernel(v_ref, b_rest, b_mid, b_skip, b_rise, out_ref, vz, vl, h1l, pool, ql, rise, l4):
    at_i, at_z, at_c = (lax.axis_index(name) for name in ("i", "z", "c"))
    out_lane = iota((128, 512), 1)
    select = (
        (iota((128, 512), 0) == (out_lane // 128) * 32 + out_lane % 32) & (out_lane % 128 < 96)
    ).astype(F32).astype(BF)
    vz[...] = jnp.zeros(vz.shape, F32)
    for src in range(NZ):
        spread_v = nn(v_ref[src], select)
        for q in range(4):
            z_row = 8 + 2 * src + q
            if q >= 2:
                if src >= 5:
                    z_row = 2 * src + (q - 2) - 8
                elif src <= 2:
                    z_row = 24 + 2 * src + (q - 2)
                else:
                    continue
            vz[pl.ds(z_row, 48, stride=32), :] = spread_v[:, q * 128 : (q + 1) * 128]
    v = vz[...]
    lane = iota(v.shape, 1)
    v = jnp.where(lane < 32, rolled(v, 1), jnp.where(lane < 64, v, rolled(v, -1)))
    v = v.astype(BF).reshape(48, 32, 128)
    for ky in range(3):
        vl[:, :, ky * 128 : (ky + 1) * 128] = v[2 + ky : 44 + ky]

    z_base = 128 * at_c + 16 * at_i - 8
    y_base = 32 * at_z

    def inside(y_count, y_first, z_count, z_first, limit):
        z = iota((z_count, 128), 0) + z_first
        rows = ((z >= 0) & (z < limit)).astype(F32)
        return jnp.concatenate(
            [
                rows * jnp.where((y_first + y >= 0) & (y_first + y < limit), 1.0, 0.0)
                for y in range(y_count)
            ],
            axis=0,
        )

    def masked(v, mask):
        return jnp.maximum(v, 0.0) * jnp.concatenate([mask] * (v.shape[1] // 128), axis=1)

    part = 14
    for step in range(3):
        y0 = step * part
        n = part * 32
        h1 = nn(vl[y0 : y0 + part].reshape(n, 384), b_rest[:, :, :512].reshape(384, 512))
        mask = inside(part, y_base - 5 + y0, 32, z_base, 256)
        for copy in range(2):
            h = masked(h1[:, copy * 256 : (copy + 1) * 256], mask)
            for kz in range(3):
                moved = rolled(h, -(3 + kz)).reshape(part, 32, 256)[:, :24].reshape(part * 24, 256)
                rows = slice(y0 * 24, (y0 + part) * 24)
                h1l[copy, rows, kz * 256 : (kz + 1) * 256] = moved.astype(BF)

    pool_t = jnp.concatenate([pool_matrix(8, 0), pool_matrix(8, 1)], axis=1)
    logits = jnp.zeros((128, 512), F32)
    for copy in range(2):
        rows = jnp.concatenate([h1l[copy, ky * 24 : ky * 24 + 960] for ky in range(3)], axis=1)
        bands = jnp.concatenate([two_blocks(b_mid, ky) for ky in range(3)], axis=1)
        h2 = masked(nt(rows, bands), inside(40, y_base - 4, 24, z_base + 4, 256))
        fine = nt(h2.astype(BF), pool_t).reshape(20, 2, 24, 128)
        filled = [fine[:, 0] + fine[:, 1], jnp.zeros((20, 8, 128), F32)]
        pool[...] = jnp.concatenate(filled, axis=1).reshape(640, 128)
        for kz in range(3):
            moved = rolled(h2, -(3 + kz)).reshape(40, 24, 256)
            l4[copy, :, :, kz * 256 : (kz + 1) * 256] = moved[3:37, :16].astype(BF)
        q = 0.125 * (pool[pl.ds(0, 320, stride=2), :] + pool[pl.ds(1, 320, stride=2), :])
        for kz, steps in enumerate((1, 0, -1)):
            moved = rolled(q, steps) if steps else q
            ql[:, :, kz * 128 : (kz + 1) * 128] = moved.astype(BF).reshape(20, 16, 128)
        acc = jnp.zeros((288, 128), F32)
        for ky in range(3):
            acc = acc + nt(ql[ky : ky + 18].reshape(288, 384), b_rest[ky, :, 512:896])
        h3 = masked(
            acc, inside(18, 16 * at_z - 1, 16, 64 * at_c + 8 * at_i - 2, 128)
        )
        rise[pl.ds(0, 288, stride=2), :] = h3
        rise[pl.ds(1, 288, stride=2), :] = h3
        r = rise[...]
        for kz in range(3):
            moved = rolled(r, -(3 + kz)).reshape(18, 32, 128)[:, :16].astype(BF)
            for slot in range(34):
                l4[copy, slot, :, 768 + kz * 128 : 896 + kz * 128] = moved[(slot + 3) // 2 - 1]
        at_rows = [slice(ky, ky + 32) for ky in range(3)]
        rows = [l4[copy, at, :, :768].reshape(512, 768) for at in at_rows]
        rows += [l4[copy, at, :, 768:].reshape(512, 384) for at in at_rows]
        bands = [two_blocks(b_skip, ky) for ky in range(3)] + [b_rise[ky] for ky in range(3)]
        h4 = nt(jnp.concatenate(rows, axis=1), jnp.concatenate(bands, axis=1))
        h4 = jnp.maximum(h4, 0.0).astype(BF)
        logits = logits + nt(b_rest[copy, :, 896:], h4)
    out_ref[...] = (0.5 * logits).astype(BF).reshape(NI, 16, 512)


def arrange_kernel(parts_ref, out_ref):
    lane = iota((16, 128), 1) // 16
    for o in range(4):
        parts = [parts_ref[src, :, o * 128 : (o + 1) * 128].astype(F32) for src in range(NI)]
        for bit in (1, 2, 4):
            upper = (lane & bit) != 0
            for low in range(NI):
                if low & bit == 0:
                    first, second = parts[low], parts[low | bit]
                    parts[low] = jnp.where(upper, pltpu.roll(second, 16 * bit, 1), first)
                    parts[low | bit] = jnp.where(upper, second, pltpu.roll(first, 128 - 16 * bit, 1))
        for y in range(8):
            out_ref[pl.ds(o * 8 + y, 16, stride=32), :] = parts[y]


def call(kernel, out_shape, scratch, megabytes, *args):
    spec = pl.BlockSpec(memory_space=pltpu.VMEM)
    return pl.pallas_call(
        kernel,
        out_shape=out_shape,
        in_specs=[spec] * len(args),
        out_specs=jax.tree.map(lambda _: spec, out_shape),
        scratch_shapes=scratch,
        compiler_params=pltpu.CompilerParams(vmem_limit_bytes=megabytes * 1024 * 1024),
    )(*args)


def bf(*shape):
    return jax.ShapeDtypeStruct(shape, BF)


def table(lead, rows, width, *weights):
    total = 0
    for at, w in weights:
        size = w.shape
        total = total + jnp.pad(
            w, ((0, lead - size[0]), (at, rows - at - size[1]), (0, width - size[2]))
        )
    return total


def taps2(w):
    return w.transpose(2, 3, 0, 1).reshape(3, -1, w.shape[1])


def taps3(w):
    return w.transpose(2, 3, 4, 0, 1).reshape(9, -1, w.shape[1])


def rim_pairs():
    def index(i, z, c):
        return (i * NZ + z) * NC + c

    pairs = []
    for z in range(NZ):
        if z >= NZ - 3:
            step, edge, wrapped = 1, NI - 1, 0
        elif z <= 2:
            step, edge, wrapped = -1, 0, 1
        else:
            continue
        for i in range(NI):
            for c in range(NC):
                if i != edge:
                    pairs.append((index(i, z, c), index(i + step, z, c)))
                elif c == wrapped:
                    pairs.append((index(i, z, c), index((i + step) % NI, z, 1 - c)))
    return pairs


def denoise(rim, planes, before, weights):
    args = (planes, before) if rim else (planes,)
    count = 2
    vmem = pltpu.VMEM
    return call(
        functools.partial(denoise_kernel, rim),
        bf(NZ, 48, 128),
        [
            vmem((count * 256, 1664), BF),
            vmem((count * 256, 2560), BF),
            vmem((count * 128, 256), F32),
            vmem((count * 256, 128), F32),
            vmem((count * 256, 256), F32),
            vmem((272, 128), F32),
        ],
        24,
        *args,
        *weights,
    )


def per_device(
    noisy, w2_in, w2_mid, w2_low, w2_deep, w2_up, w2_out, w3_in, w3_mid, w3_low, w3_up, w3_out
):
    near = noisy.reshape(2, 32, 256)
    far = lax.ppermute(near, "c", [(0, 1), (1, 0)])
    kernels = ((0, w2_mid), (48, w2_low), (96, w2_deep), (144, w2_up))
    taps = [(at, taps2(w)) for at, w in kernels]
    taps += [(192, w2_in.transpose(1, 2, 3, 0)[0]), (195, w2_out[None])]
    weights = call(
        plane_weights_kernel,
        [
            bf(128, 640),
            bf(256, 1024),
            bf(256, 768),
            bf(256, 768),
            bf(256, 1408),
            bf(512, 512),
            bf(4, 128, 512),
        ],
        [],
        16,
        table(3, 208, 32, *taps),
    )
    far, weights = lax.optimization_barrier((far, weights))
    second = lax.axis_index("c") == 1
    own = jnp.stack([jnp.where(second, far[1], near[0]), jnp.where(second, near[1], far[0])])
    rim = lax.ppermute(own, ("i", "z", "c"), rim_pairs())
    volume = denoise(0, own, None, weights)
    volume = denoise(1, rim, volume, weights)
    taps = [(at, taps3(w)) for at, w in ((0, w3_mid), (24, w3_low), (48, w3_up))]
    taps += [(72, w3_in.transpose(1, 2, 3, 4, 0).reshape(9, 3, 8)), (80, w3_out[None])]
    bands = call(volume_weights_kernel, [bf(3, 128, 1152), bf(3, 128, 1152), bf(3, 128, 1152), bf(3, 256, 384)], [], 16, table(9, 88, 16, *taps))
    window = lax.all_to_all(volume, "z", 0, 0, tiled=True)
    vmem = pltpu.VMEM
    logits = call(
        segment_kernel,
        bf(NI, 16, 512),
        [
            vmem((48 * 32, 128), F32),
            vmem((42, 32, 384), BF),
            vmem((2, 42 * 24, 768), BF),
            vmem((640, 128), F32),
            vmem((20, 16, 384), BF),
            vmem((576, 128), F32),
            vmem((2, 34, 16, 1152), BF),
        ],
        24,
        window,
        *bands,
    )
    parts = lax.all_to_all(logits, "i", 0, 0, tiled=True)
    out = call(arrange_kernel, jax.ShapeDtypeStruct((512, 128), F32), [], 4, parts)
    return out.reshape(1, 4, 4, 32, 128)


def solution(mesh):
    finer = Mesh(mesh.devices.reshape(2, NI, NZ, NC), ("rep", "i", "z", "c"))
    brick = ("i", "z", "c")
    placed = (P(None, brick, None, None),) + (P(),) * 11
    return jax.shard_map(
        per_device,
        mesh=finer,
        in_specs=placed,
        out_specs=P(brick, "rep", None, None, None),
        check_vma=False,
    )
```

```python
import functools

import jax
import jax.numpy as jnp
from jax import lax
from jax.experimental import pallas as pl
from jax.experimental.pallas import tpu as pltpu
from jax.sharding import Mesh
from jax.sharding import PartitionSpec as P

BF = jnp.bfloat16
F32 = jnp.float32
NI, NZ, NC = 8, 8, 2


def iota(shape, dim):
    return lax.broadcasted_iota(jnp.int32, shape, dim)


def nn(a, b):
    return lax.dot_general(a, b, (((1,), (0,)), ((), ())), preferred_element_type=F32)


def nt(a, b):
    return lax.dot_general(a, b, (((1,), (1,)), ((), ())), preferred_element_type=F32)


def lane_spread(rows, channels, first, lanes):
    return (iota((rows, lanes), 1) % channels + first == iota((rows, lanes), 0)).astype(
        F32
    ).astype(BF)


def stacked(taps, at, channels):
    return jnp.concatenate([taps[at * channels : (at + 1) * channels]] * (128 // channels), axis=0)


def band_parts(taps, channels):
    cells = 128 // channels
    gap = iota((128, 128), 1) // channels - iota((128, 128), 0) // channels
    zero = jnp.zeros((128, 128), F32)
    own = jnp.where(
        gap == 0, taps[1], jnp.where(gap == -1, taps[0], jnp.where(gap == 1, taps[2], zero))
    )
    later = jnp.where(gap == 1 - cells, taps[2], zero)
    earlier = jnp.where(gap == cells - 1, taps[0], zero)
    return [part.astype(BF) for part in (own, later, earlier)]


def same_level(ref, at, blocks, taps, channels):
    own, later, earlier = band_parts(taps, channels)
    for out in range(blocks):
        for inp in range(blocks):
            if inp == out:
                block = own
            elif inp == out + 1:
                block = later
            elif inp == out - 1:
                block = earlier
            else:
                block = jnp.zeros((128, 128), BF)
            ref[out * 128 : (out + 1) * 128, at + inp * 128 : at + (inp + 1) * 128] = block


def two_blocks(ref, ky):
    parts = [ref[ky, :, at * 128 : (at + 1) * 128] for at in range(9)]
    rows = [[], []]
    for own, later, earlier in (parts[0:3], parts[3:6], parts[6:9]):
        rows[0] += [own, later]
        rows[1] += [earlier, own]
    return jnp.concatenate([jnp.concatenate(row, axis=1) for row in rows], axis=0)


def from_coarse(ref, lead, at, out_blocks, in_blocks, taps, channels):
    cells = 128 // channels
    lane_cell = iota((128, 128), 1) // channels
    row_cell = iota((128, 128), 0) // channels
    zero = jnp.zeros((128, 128), F32)
    for out in range(out_blocks):
        for inp in range(in_blocks):
            total = zero
            for kx in range(3):
                meets = (row_cell + (out * cells + kx - 1)) >> 1 == lane_cell + inp * cells
                total = total + jnp.where(meets, taps[kx], zero)
            ref[lead + (pl.ds(out * 128, 128), pl.ds(at + inp * 128, 128))] = total.astype(BF)


def pool_matrix(channels, half):
    cells = 128 // channels
    lane, row = iota((128, 128), 1), iota((128, 128), 0)
    meets = ((lane // channels + half * cells) >> 1 == row // channels) & (
        lane % channels == row % channels
    )
    return meets.astype(F32).astype(BF)


def rolled(v, steps):
    return pltpu.roll(v, steps % v.shape[0], 0)


def edge_rows(w, first):
    group = iota((16, 128), 1) // 16
    total = jnp.zeros((16, 128), F32)
    for ky in range(3):
        total = jnp.where(group == first + ky, w[ky * 16 : ky * 16 + 16], total)
    return total


def plane_weights_kernel(w_ref, b_in, b_mid, b_low, b_deep, b_up, b_pool, b_last):
    edge = [nn(w_ref[kx, 192:208], lane_spread(32, 16, 0, 512)) for kx in range(3)]
    w_row = edge[0][3:4]
    xi = iota((32, 512), 0)
    xo = iota((32, 512), 1) // 16
    group = iota((32, 128), 1) // 16
    cell = jnp.where(group % 4 == 3, -9, jnp.where(group < 4, 16, 15))
    for ky in range(3):
        total = jnp.zeros((32, 512), F32)
        extra = jnp.zeros((32, 128), F32)
        for kx in range(3):
            tap = edge[kx][ky : ky + 1]
            total = jnp.where(xi == xo + (kx - 1), tap, total)
            extra = jnp.where(xi[:, :128] == cell + (kx - 1), tap[:, :128], extra)
        b_in[ky * 32 : (ky + 1) * 32, :512] = total.astype(BF)
        b_in[ky * 32 : (ky + 1) * 32, 512:] = extra.astype(BF)
    b_in[96:128] = jnp.zeros((32, 640), BF)
    spread = lane_spread(32, 16, 0, 128)
    w_mid, w_low, w_deep, w_skip = (
        [nn(w_ref[kx, at : at + 48], spread) for kx in range(3)] for at in (0, 48, 96, 144)
    )
    w_rise = [nn(w_ref[kx, 144:192], lane_spread(32, 16, 16, 128)) for kx in range(3)]
    for ky in range(3):
        for w, b_ref in ((w_mid, b_mid), (w_low, b_low), (w_deep, b_deep), (w_skip, b_up)):
            same_level(b_ref, ky * 256, 2, [stacked(w[kx], ky, 16) for kx in range(3)], 16)
        taps = [stacked(w_rise[kx], ky, 16) for kx in range(3)]
        from_coarse(b_up, (), 768 + ky * 128, 2, 1, taps, 16)
    b_mid[:, 768:] = jnp.zeros((256, 128), BF)
    b_mid[240:256, 768:] = edge_rows(w_mid[2], 0).astype(BF)
    b_mid[0:16, 768:] = edge_rows(w_mid[0], 4).astype(BF)
    b_up[:, 1152:] = jnp.zeros((256, 256), BF)
    b_up[240:256, 1152:1280] = (edge_rows(w_skip[2], 0) + edge_rows(w_rise[2], 4)).astype(BF)
    b_up[0:16, 1280:1408] = (edge_rows(w_skip[0], 0) + edge_rows(w_rise[0], 4)).astype(BF)
    none = jnp.zeros((128, 128), BF)
    for out in range(2):
        for inp in range(4):
            b_pool[out * 128 : (out + 1) * 128, inp * 128 : (inp + 1) * 128] = (
                pool_matrix(16, inp % 2) if inp // 2 == out else none
            )
    o = iota((256, 512), 0)
    group = o % 128 // 16
    place = 128 - o // 128 * 16 + o % 16
    place = jnp.where(group < 4, place, place + 256)
    picks = (iota((256, 512), 1) == place) & (group % 4 < 3)
    b_pool[256:512] = picks.astype(F32).astype(BF)
    to_lane, cell = iota((128, 512), 0), iota((128, 512), 1) // 16
    for q in range(4):
        b_last[q] = jnp.where(to_lane == q * 32 + cell, w_row, 0.0).astype(BF)


def denoise_kernel(rim, planes_ref, *refs):
    before_ref = refs[0] if rim else None
    refs = refs[rim:]
    b_in, b_mid, b_low, b_deep, b_up, b_pool, b_last, out_ref = refs[:8]
    lhs, wide, coarse, half, raised, vol = refs[8:]
    planes = 2
    low_rows = planes * 128

    def place(ref, at, width, v, length):
        n = v.shape[0]
        row = iota(v.shape, 0) % length
        ref[:n, at : at + width] = jnp.where(row == 0, 0.0, rolled(v, 1)).astype(BF)
        ref[:n, at + width : at + 2 * width] = v.astype(BF)
        ref[:n, at + 2 * width : at + 3 * width] = jnp.where(
            row == length - 1, 0.0, rolled(v, -1)
        ).astype(BF)

    turned = planes_ref[...].astype(F32).reshape(64, 256)
    turned = jnp.concatenate([turned, jnp.zeros((64, 256), F32)], axis=0).T
    row = iota((256, 128), 0)
    lane = iota((256, 128), 1)
    before = jnp.where(row == 0, 0.0, rolled(turned, 1))
    after = jnp.where(row == 255, 0.0, rolled(turned, -1))
    def taps_apart(v, length):
        r, group = iota(v.shape, 0) % length, iota(v.shape, 1) // 16 % 4
        down = jnp.where(r == 0, 0.0, rolled(v, 1))
        up = jnp.where(r == length - 1, 0.0, rolled(v, -1))
        return jnp.where(group == 0, down, jnp.where(group == 1, v, up))

    def lanes(ref, *pieces):
        return jnp.concatenate([ref[:, at : at + size] for at, size in pieces], axis=1)

    for q in range(planes):
        three = jnp.zeros((256, 128), F32)
        for g, v in enumerate((before, turned, after)):
            three = jnp.where(lane // 32 == g, pltpu.roll(v, ((g - q) * 32) % 128, 1), three)
        first = jnp.maximum(nn(three.astype(BF), b_in[...]), 0.0)
        rows_q = slice(q * 256, (q + 1) * 256)
        place(lhs.at[rows_q], 0, 512, first[:, :512], 256)
        apart = taps_apart(first[:, 512:], 256)
        lhs[rows_q, 1536:1664] = jnp.where(lane < 64, apart, 0.0).astype(BF)
        lhs[rows_q, 1664:] = jnp.where(lane < 64, 0.0, apart).astype(BF)
    halves = []
    for x in range(2):
        cells = [(ky * 512 + x * 256, 256) for ky in range(3)]
        halves.append(lanes(lhs, *cells, (1536 + x * 128, 128)))
    skip = jnp.maximum(nt(jnp.concatenate(halves, axis=0), b_mid[...]), 0.0)
    skip = jnp.concatenate([skip[: planes * 256], skip[planes * 256 :]], axis=1)
    place(wide, 0, 512, skip, 256)
    fine = nt(skip.astype(BF), b_pool[:256])
    for c in range(2):
        half[...] = fine[:, c * 128 : (c + 1) * 128]
        coarse[:, c * 128 : (c + 1) * 128] = 0.25 * (
            half[pl.ds(0, low_rows, stride=2), :] + half[pl.ds(1, low_rows, stride=2), :]
        )
    place(lhs.at[:low_rows], 0, 256, coarse[...], 128)
    low = jnp.maximum(nt(lhs[:low_rows, :768], b_low[...]), 0.0)
    place(lhs.at[:low_rows], 768, 256, low, 128)
    deep = jnp.maximum(nt(lhs[:low_rows, 768:1536], b_deep[...]), 0.0)
    for c in range(2):
        part = deep[:, c * 128 : (c + 1) * 128]
        half[pl.ds(0, low_rows, stride=2), :] = part
        half[pl.ds(1, low_rows, stride=2), :] = part
        raised[:, c * 128 : (c + 1) * 128] = half[...]
    place(wide, 1536, 256, raised[...], 256)
    wide[:, 2304:] = taps_apart(nt(lanes(wide, (640, 256), (1792, 256)), b_pool[256:]), 256).astype(BF)
    halves = []
    for x in range(2):
        cells = [(ky * 512 + x * 256, 256) for ky in range(3)]
        cells += [(1536 + ky * 256 + x * 128, 128) for ky in range(3)]
        bands = lanes(b_up, (0, 1152), (1152 + x * 128, 128))
        halves.append(jnp.maximum(nt(lanes(wide, *cells, (2304 + x * 128, 128)), bands), 0.0))
    joined = jnp.concatenate(halves, axis=1).astype(BF)
    total = jnp.zeros((256, 128), F32)
    for q in range(planes):
        total = total + nt(joined[q * 256 : (q + 1) * 256], b_last[2 * rim + q])
    vol[0:8] = jnp.zeros((8, 128), F32)
    vol[264:272] = jnp.zeros((8, 128), F32)
    vol[8:264] = total
    for z in range(NZ):
        window = vol[z * 32 : z * 32 + 48]
        if before_ref is not None:
            window = window + before_ref[z].astype(F32)
        out_ref[z] = window.astype(BF)


def volume_weights_kernel(w_ref, b_rest, b_mid, b_skip, b_rise):
    edge = [nn(w_ref[kxy, 72:88], lane_spread(16, 8, 0, 256)) for kxy in range(9)]
    spread = lane_spread(16, 8, 0, 128)
    w_mid, w_low, w_skip = (
        [nn(w_ref[kxy, at : at + 24], spread) for kxy in range(9)] for at in (0, 24, 48)
    )
    w_rise = [nn(w_ref[kxy, 48:72], lane_spread(16, 8, 8, 128)) for kxy in range(9)]
    xi = iota((32, 256), 0)
    xo = iota((32, 256), 1) // 8
    for ky in range(3):
        for kz in range(3):
            plain = jnp.zeros((32, 256), F32)
            mirror = jnp.zeros((32, 256), F32)
            for kx in range(3):
                tap = edge[kx * 3 + ky][kz : kz + 1]
                plain = jnp.where(xi == xo + (kx - 1), tap, plain)
                mirror = jnp.where(xi == (32 - kx) - xo, tap, mirror)
            at = kz * 32
            b_rest[ky, at : at + 32, :256] = plain.astype(BF)
            b_rest[ky, at : at + 32, 256:512] = mirror.astype(BF)
        b_rest[ky, 96:128, :512] = jnp.zeros((32, 512), BF)
    for ky in range(3):
        for kz in range(3):
            for w, b_ref in ((w_mid, b_mid), (w_skip, b_skip)):
                taps = [stacked(w[kx * 3 + ky], kz, 8) for kx in range(3)]
                for side, part in enumerate(band_parts(taps, 8)):
                    at = (kz * 3 + side) * 128
                    b_ref[ky, :, at : at + 128] = part
            taps = [stacked(w_low[kx * 3 + ky], kz, 8) for kx in range(3)]
            same_level(b_rest.at[ky], 512 + kz * 128, 1, taps, 8)
            taps = [stacked(w_rise[kx * 3 + ky], kz, 8) for kx in range(3)]
            from_coarse(b_rise, (ky,), kz * 128, 2, 1, taps, 8)
    w_out = edge[0][8:16].astype(BF)
    row_r = iota((128, 256), 0)
    cell = iota((128, 256), 1) // 8
    pick = (iota((128, 8), 1) == (iota((128, 8), 0) // 4) % 4 + 4 * lax.axis_index("rep"))
    w_rows = nn(pick.astype(F32).astype(BF), w_out)
    x_row = (row_r // 16) * 4 + row_r % 4
    b_rest[0, :, 896:] = jnp.where(cell == x_row, w_rows, 0.0).astype(BF)
    b_rest[1, :, 896:] = jnp.where(31 - cell == x_row, w_rows, 0.0).astype(BF)


def segment_kernel(v_ref, b_rest, b_mid, b_skip, b_rise, out_ref, vz, vl, h1l, pool, ql, rise, l4):
    at_i, at_z, at_c = (lax.axis_index(name) for name in ("i", "z", "c"))
    out_lane = iota((128, 512), 1)
    select = (
        (iota((128, 512), 0) == (out_lane // 128) * 32 + out_lane % 32) & (out_lane % 128 < 96)
    ).astype(F32).astype(BF)
    vz[...] = jnp.zeros(vz.shape, F32)
    for src in range(NZ):
        spread_v = nn(v_ref[src], select)
        for q in range(4):
            z_row = 8 + 2 * src + q
            if q >= 2:
                if src >= 5:
                    z_row = 2 * src + (q - 2) - 8
                elif src <= 2:
                    z_row = 24 + 2 * src + (q - 2)
                else:
                    continue
            vz[pl.ds(z_row, 48, stride=32), :] = spread_v[:, q * 128 : (q + 1) * 128]
    v = vz[...]
    lane = iota(v.shape, 1)
    v = jnp.where(lane < 32, rolled(v, 1), jnp.where(lane < 64, v, rolled(v, -1)))
    v = v.astype(BF).reshape(48, 32, 128)
    for ky in range(3):
        vl[:, :, ky * 128 : (ky + 1) * 128] = v[2 + ky : 44 + ky]

    z_base = 128 * at_c + 16 * at_i - 8
    y_base = 32 * at_z

    def inside(y_count, y_first, z_count, z_first, limit):
        z = iota((z_count, 128), 0) + z_first
        rows = ((z >= 0) & (z < limit)).astype(F32)
        return jnp.concatenate(
            [
                rows * jnp.where((y_first + y >= 0) & (y_first + y < limit), 1.0, 0.0)
                for y in range(y_count)
            ],
            axis=0,
        )

    def masked(v, mask):
        return jnp.maximum(v, 0.0) * jnp.concatenate([mask] * (v.shape[1] // 128), axis=1)

    part = 14
    for step in range(3):
        y0 = step * part
        n = part * 32
        h1 = nn(vl[y0 : y0 + part].reshape(n, 384), b_rest[:, :, :512].reshape(384, 512))
        mask = inside(part, y_base - 5 + y0, 32, z_base, 256)
        for copy in range(2):
            h = masked(h1[:, copy * 256 : (copy + 1) * 256], mask)
            for kz in range(3):
                moved = rolled(h, -(3 + kz)).reshape(part, 32, 256)[:, :24].reshape(part * 24, 256)
                rows = slice(y0 * 24, (y0 + part) * 24)
                h1l[copy, rows, kz * 256 : (kz + 1) * 256] = moved.astype(BF)

    pool_t = jnp.concatenate([pool_matrix(8, 0), pool_matrix(8, 1)], axis=1)
    logits = jnp.zeros((128, 512), F32)
    for copy in range(2):
        rows = jnp.concatenate([h1l[copy, ky * 24 : ky * 24 + 960] for ky in range(3)], axis=1)
        bands = jnp.concatenate([two_blocks(b_mid, ky) for ky in range(3)], axis=1)
        h2 = masked(nt(rows, bands), inside(40, y_base - 4, 24, z_base + 4, 256))
        fine = nt(h2.astype(BF), pool_t).reshape(20, 2, 24, 128)
        filled = [fine[:, 0] + fine[:, 1], jnp.zeros((20, 8, 128), F32)]
        pool[...] = jnp.concatenate(filled, axis=1).reshape(640, 128)
        for kz in range(3):
            moved = rolled(h2, -(3 + kz)).reshape(40, 24, 256)
            l4[copy, :, :, kz * 256 : (kz + 1) * 256] = moved[3:37, :16].astype(BF)
        q = 0.125 * (pool[pl.ds(0, 320, stride=2), :] + pool[pl.ds(1, 320, stride=2), :])
        for kz, steps in enumerate((1, 0, -1)):
            moved = rolled(q, steps) if steps else q
            ql[:, :, kz * 128 : (kz + 1) * 128] = moved.astype(BF).reshape(20, 16, 128)
        acc = jnp.zeros((288, 128), F32)
        for ky in range(3):
            acc = acc + nt(ql[ky : ky + 18].reshape(288, 384), b_rest[ky, :, 512:896])
        h3 = masked(
            acc, inside(18, 16 * at_z - 1, 16, 64 * at_c + 8 * at_i - 2, 128)
        )
        rise[pl.ds(0, 288, stride=2), :] = h3
        rise[pl.ds(1, 288, stride=2), :] = h3
        r = rise[...]
        for kz in range(3):
            moved = rolled(r, -(3 + kz)).reshape(18, 32, 128)[:, :16].astype(BF)
            for slot in range(34):
                l4[copy, slot, :, 768 + kz * 128 : 896 + kz * 128] = moved[(slot + 3) // 2 - 1]
        at_rows = [slice(ky, ky + 32) for ky in range(3)]
        rows = [l4[copy, at, :, :768].reshape(512, 768) for at in at_rows]
        rows += [l4[copy, at, :, 768:].reshape(512, 384) for at in at_rows]
        bands = [two_blocks(b_skip, ky) for ky in range(3)] + [b_rise[ky] for ky in range(3)]
        h4 = nt(jnp.concatenate(rows, axis=1), jnp.concatenate(bands, axis=1))
        h4 = jnp.maximum(h4, 0.0).astype(BF)
        logits = logits + nt(b_rest[copy, :, 896:], h4)
    out_ref[...] = (0.5 * logits).astype(BF).reshape(NI, 16, 512)


def arrange_kernel(parts_ref, out_ref):
    lane = iota((16, 128), 1) // 16
    for o in range(4):
        parts = [parts_ref[src, :, o * 128 : (o + 1) * 128].astype(F32) for src in range(NI)]
        for bit in (1, 2, 4):
            upper = (lane & bit) != 0
            for low in range(NI):
                if low & bit == 0:
                    first, second = parts[low], parts[low | bit]
                    parts[low] = jnp.where(upper, pltpu.roll(second, 16 * bit, 1), first)
                    parts[low | bit] = jnp.where(upper, second, pltpu.roll(first, 128 - 16 * bit, 1))
        for y in range(8):
            out_ref[pl.ds(o * 8 + y, 16, stride=32), :] = parts[y]


def call(kernel, out_shape, scratch, megabytes, *args):
    spec = pl.BlockSpec(memory_space=pltpu.VMEM)
    return pl.pallas_call(
        kernel,
        out_shape=out_shape,
        in_specs=[spec] * len(args),
        out_specs=jax.tree.map(lambda _: spec, out_shape),
        scratch_shapes=scratch,
        compiler_params=pltpu.CompilerParams(vmem_limit_bytes=megabytes * 1024 * 1024),
    )(*args)


def bf(*shape):
    return jax.ShapeDtypeStruct(shape, BF)


def table(lead, rows, width, *weights):
    total = 0
    for at, w in weights:
        size = w.shape
        total = total + jnp.pad(
            w, ((0, lead - size[0]), (at, rows - at - size[1]), (0, width - size[2]))
        )
    return total


def taps2(w):
    return w.transpose(2, 3, 0, 1).reshape(3, -1, w.shape[1])


def taps3(w):
    return w.transpose(2, 3, 4, 0, 1).reshape(9, -1, w.shape[1])


def rim_pairs():
    def index(i, z, c):
        return (i * NZ + z) * NC + c

    pairs = []
    for z in range(NZ):
        if z >= NZ - 3:
            step, edge, wrapped = 1, NI - 1, 0
        elif z <= 2:
            step, edge, wrapped = -1, 0, 1
        else:
            continue
        for i in range(NI):
            for c in range(NC):
                if i != edge:
                    pairs.append((index(i, z, c), index(i + step, z, c)))
                elif c == wrapped:
                    pairs.append((index(i, z, c), index((i + step) % NI, z, 1 - c)))
    return pairs


def denoise(rim, planes, before, weights):
    args = (planes, before) if rim else (planes,)
    count = 2
    vmem = pltpu.VMEM
    return call(
        functools.partial(denoise_kernel, rim),
        bf(NZ, 48, 128),
        [
            vmem((count * 256, 1792), BF),
            vmem((count * 256, 2560), BF),
            vmem((count * 128, 256), F32),
            vmem((count * 256, 128), F32),
            vmem((count * 256, 256), F32),
            vmem((272, 128), F32),
        ],
        24,
        *args,
        *weights,
    )


def per_device(
    noisy, w2_in, w2_mid, w2_low, w2_deep, w2_up, w2_out, w3_in, w3_mid, w3_low, w3_up, w3_out
):
    near = noisy.reshape(2, 32, 256)
    far = lax.ppermute(near, "c", [(0, 1), (1, 0)])
    kernels = ((0, w2_mid), (48, w2_low), (96, w2_deep), (144, w2_up))
    taps = [(at, taps2(w)) for at, w in kernels]
    taps += [(192, w2_in.transpose(1, 2, 3, 0)[0]), (195, w2_out[None])]
    weights = call(
        plane_weights_kernel,
        [
            bf(128, 640),
            bf(256, 896),
            bf(256, 768),
            bf(256, 768),
            bf(256, 1408),
            bf(512, 512),
            bf(4, 128, 512),
        ],
        [],
        16,
        table(3, 208, 32, *taps),
    )
    far, weights = lax.optimization_barrier((far, weights))
    second = lax.axis_index("c") == 1
    own = jnp.stack([jnp.where(second, far[1], near[0]), jnp.where(second, near[1], far[0])])
    rim = lax.ppermute(own, ("i", "z", "c"), rim_pairs())
    volume = denoise(0, own, None, weights)
    volume = denoise(1, rim, volume, weights)
    taps = [(at, taps3(w)) for at, w in ((0, w3_mid), (24, w3_low), (48, w3_up))]
    taps += [(72, w3_in.transpose(1, 2, 3, 4, 0).reshape(9, 3, 8)), (80, w3_out[None])]
    bands = call(volume_weights_kernel, [bf(3, 128, 1152), bf(3, 128, 1152), bf(3, 128, 1152), bf(3, 256, 384)], [], 16, table(9, 88, 16, *taps))
    window = lax.all_to_all(volume, "z", 0, 0, tiled=True)
    vmem = pltpu.VMEM
    logits = call(
        segment_kernel,
        bf(NI, 16, 512),
        [
            vmem((48 * 32, 128), F32),
            vmem((42, 32, 384), BF),
            vmem((2, 42 * 24, 768), BF),
            vmem((640, 128), F32),
            vmem((20, 16, 384), BF),
            vmem((576, 128), F32),
            vmem((2, 34, 16, 1152), BF),
        ],
        24,
        window,
        *bands,
    )
    parts = lax.all_to_all(logits, "i", 0, 0, tiled=True)
    out = call(arrange_kernel, jax.ShapeDtypeStruct((512, 128), F32), [], 4, parts)
    return out.reshape(1, 4, 4, 32, 128)


def solution(mesh):
    finer = Mesh(mesh.devices.reshape(2, NI, NZ, NC), ("rep", "i", "z", "c"))
    brick = ("i", "z", "c")
    placed = (P(None, brick, None, None),) + (P(),) * 11
    return jax.shard_map(
        per_device,
        mesh=finer,
        in_specs=placed,
        out_specs=P(brick, "rep", None, None, None),
        check_vma=False,
    )
```

```python
import functools

import jax
import jax.numpy as jnp
from jax import lax
from jax.experimental import pallas as pl
from jax.experimental.pallas import tpu as pltpu
from jax.sharding import Mesh
from jax.sharding import PartitionSpec as P

BF = jnp.bfloat16
F32 = jnp.float32
NI, NZ, NC = 8, 8, 2


def iota(shape, dim):
    return lax.broadcasted_iota(jnp.int32, shape, dim)


def nn(a, b):
    return lax.dot_general(a, b, (((1,), (0,)), ((), ())), preferred_element_type=F32)


def nt(a, b):
    return lax.dot_general(a, b, (((1,), (1,)), ((), ())), preferred_element_type=F32)


def lane_spread(rows, channels, first, lanes):
    return (iota((rows, lanes), 1) % channels + first == iota((rows, lanes), 0)).astype(
        F32
    ).astype(BF)


def stacked(taps, at, channels):
    return jnp.concatenate([taps[at * channels : (at + 1) * channels]] * (128 // channels), axis=0)


def band_parts(taps, channels):
    cells = 128 // channels
    gap = iota((128, 128), 1) // channels - iota((128, 128), 0) // channels
    zero = jnp.zeros((128, 128), F32)
    own = jnp.where(
        gap == 0, taps[1], jnp.where(gap == -1, taps[0], jnp.where(gap == 1, taps[2], zero))
    )
    later = jnp.where(gap == 1 - cells, taps[2], zero)
    earlier = jnp.where(gap == cells - 1, taps[0], zero)
    return [part.astype(BF) for part in (own, later, earlier)]


def same_level(ref, at, blocks, taps, channels):
    own, later, earlier = band_parts(taps, channels)
    for out in range(blocks):
        for inp in range(blocks):
            if inp == out:
                block = own
            elif inp == out + 1:
                block = later
            elif inp == out - 1:
                block = earlier
            else:
                block = jnp.zeros((128, 128), BF)
            ref[out * 128 : (out + 1) * 128, at + inp * 128 : at + (inp + 1) * 128] = block


def two_blocks(ref, ky):
    parts = [ref[ky, :, at * 128 : (at + 1) * 128] for at in range(9)]
    rows = [[], []]
    for own, later, earlier in (parts[0:3], parts[3:6], parts[6:9]):
        rows[0] += [own, later]
        rows[1] += [earlier, own]
    return jnp.concatenate([jnp.concatenate(row, axis=1) for row in rows], axis=0)


def from_coarse(ref, lead, at, out_blocks, in_blocks, taps, channels):
    cells = 128 // channels
    lane_cell = iota((128, 128), 1) // channels
    row_cell = iota((128, 128), 0) // channels
    zero = jnp.zeros((128, 128), F32)
    for out in range(out_blocks):
        for inp in range(in_blocks):
            total = zero
            for kx in range(3):
                meets = (row_cell + (out * cells + kx - 1)) >> 1 == lane_cell + inp * cells
                total = total + jnp.where(meets, taps[kx], zero)
            ref[lead + (pl.ds(out * 128, 128), pl.ds(at + inp * 128, 128))] = total.astype(BF)


def pool_matrix(channels, half):
    cells = 128 // channels
    lane, row = iota((128, 128), 1), iota((128, 128), 0)
    meets = ((lane // channels + half * cells) >> 1 == row // channels) & (
        lane % channels == row % channels
    )
    return meets.astype(F32).astype(BF)


def rolled(v, steps):
    return pltpu.roll(v, steps % v.shape[0], 0)


def edge_rows(w, first):
    group = iota((16, 128), 1) // 16
    total = jnp.zeros((16, 128), F32)
    for ky in range(3):
        total = jnp.where(group == first + ky, w[ky * 16 : ky * 16 + 16], total)
    return total


def plane_weights_kernel(w_ref, b_in, b_mid, b_low, b_deep, b_up, b_pool, b_last):
    edge = [nn(w_ref[kx, 192:208], lane_spread(32, 16, 0, 512)) for kx in range(3)]
    w_row = edge[0][3:4]
    xi = iota((32, 512), 0)
    xo = iota((32, 512), 1) // 16
    group = iota((32, 128), 1) // 16
    cell = jnp.where(group % 4 == 3, -9, jnp.where(group < 4, 16, 15))
    for ky in range(3):
        total = jnp.zeros((32, 512), F32)
        extra = jnp.zeros((32, 128), F32)
        for kx in range(3):
            tap = edge[kx][ky : ky + 1]
            total = jnp.where(xi == xo + (kx - 1), tap, total)
            extra = jnp.where(xi[:, :128] == cell + (kx - 1), tap[:, :128], extra)
        b_in[ky * 32 : (ky + 1) * 32, :512] = total.astype(BF)
        b_in[ky * 32 : (ky + 1) * 32, 512:] = extra.astype(BF)
    b_in[96:128] = jnp.zeros((32, 640), BF)
    spread = lane_spread(32, 16, 0, 128)
    w_mid, w_low, w_deep, w_skip = (
        [nn(w_ref[kx, at : at + 48], spread) for kx in range(3)] for at in (0, 48, 96, 144)
    )
    w_rise = [nn(w_ref[kx, 144:192], lane_spread(32, 16, 16, 128)) for kx in range(3)]
    for ky in range(3):
        for w, b_ref in ((w_mid, b_mid), (w_low, b_low), (w_deep, b_deep), (w_skip, b_up)):
            same_level(b_ref, ky * 256, 2, [stacked(w[kx], ky, 16) for kx in range(3)], 16)
        taps = [stacked(w_rise[kx], ky, 16) for kx in range(3)]
        from_coarse(b_up, (), 768 + ky * 128, 2, 1, taps, 16)
    b_mid[:, 768:] = jnp.zeros((256, 256), BF)
    b_mid[240:256, 768:896] = edge_rows(w_mid[2], 0).astype(BF)
    b_mid[0:16, 896:1024] = edge_rows(w_mid[0], 4).astype(BF)
    b_up[:, 1152:] = jnp.zeros((256, 256), BF)
    b_up[240:256, 1152:1280] = (edge_rows(w_skip[2], 0) + edge_rows(w_rise[2], 4)).astype(BF)
    b_up[0:16, 1280:1408] = (edge_rows(w_skip[0], 0) + edge_rows(w_rise[0], 4)).astype(BF)
    none = jnp.zeros((128, 128), BF)
    for out in range(2):
        for inp in range(4):
            b_pool[out * 128 : (out + 1) * 128, inp * 128 : (inp + 1) * 128] = (
                pool_matrix(16, inp % 2) if inp // 2 == out else none
            )
    o = iota((256, 512), 0)
    group = o % 128 // 16
    place = 128 - o // 128 * 16 + o % 16
    place = jnp.where(group < 4, place, place + 256)
    picks = (iota((256, 512), 1) == place) & (group % 4 < 3)
    b_pool[256:512] = picks.astype(F32).astype(BF)
    to_lane, cell = iota((128, 512), 0), iota((128, 512), 1) // 16
    for q in range(4):
        b_last[q] = jnp.where(to_lane == q * 32 + cell, w_row, 0.0).astype(BF)


def denoise_kernel(rim, planes_ref, *refs):
    before_ref = refs[0] if rim else None
    refs = refs[rim:]
    b_in, b_mid, b_low, b_deep, b_up, b_pool, b_last, out_ref = refs[:8]
    lhs, wide, coarse, half, raised, vol = refs[8:]
    planes = 2
    low_rows = planes * 128

    def place(ref, at, width, v, length):
        n = v.shape[0]
        row = iota(v.shape, 0) % length
        ref[:n, at : at + width] = jnp.where(row == 0, 0.0, rolled(v, 1)).astype(BF)
        ref[:n, at + width : at + 2 * width] = v.astype(BF)
        ref[:n, at + 2 * width : at + 3 * width] = jnp.where(
            row == length - 1, 0.0, rolled(v, -1)
        ).astype(BF)

    turned = planes_ref[...].astype(F32).reshape(64, 256)
    turned = jnp.concatenate([turned, jnp.zeros((64, 256), F32)], axis=0).T
    row = iota((256, 128), 0)
    lane = iota((256, 128), 1)
    before = jnp.where(row == 0, 0.0, rolled(turned, 1))
    after = jnp.where(row == 255, 0.0, rolled(turned, -1))
    def taps_apart(v, length):
        r, group = iota(v.shape, 0) % length, iota(v.shape, 1) // 16 % 4
        down = jnp.where(r == 0, 0.0, rolled(v, 1))
        up = jnp.where(r == length - 1, 0.0, rolled(v, -1))
        return jnp.where(group == 0, down, jnp.where(group == 1, v, up)).astype(BF)

    def lanes(ref, *pieces):
        return jnp.concatenate([ref[:, at : at + size] for at, size in pieces], axis=1)

    for q in range(planes):
        three = jnp.zeros((256, 128), F32)
        for g, v in enumerate((before, turned, after)):
            three = jnp.where(lane // 32 == g, pltpu.roll(v, ((g - q) * 32) % 128, 1), three)
        first = jnp.maximum(nn(three.astype(BF), b_in[...]), 0.0)
        rows_q = slice(q * 256, (q + 1) * 256)
        place(lhs.at[rows_q], 0, 512, first[:, :512], 256)
        lhs[rows_q, 1536:] = taps_apart(first[:, 512:], 256)
    halves = []
    for x in range(2):
        cells = [(ky * 512 + x * 256, 256) for ky in range(3)]
        bands = lanes(b_mid, (0, 768), (768 + x * 128, 128))
        halves.append(jnp.maximum(nt(lanes(lhs, *cells, (1536, 128)), bands), 0.0))
    skip = jnp.concatenate(halves, axis=1)
    place(wide, 0, 512, skip, 256)
    fine = nt(skip.astype(BF), b_pool[:256])
    for c in range(2):
        half[...] = fine[:, c * 128 : (c + 1) * 128]
        coarse[:, c * 128 : (c + 1) * 128] = 0.25 * (
            half[pl.ds(0, low_rows, stride=2), :] + half[pl.ds(1, low_rows, stride=2), :]
        )
    place(lhs.at[:low_rows], 0, 256, coarse[...], 128)
    low = jnp.maximum(nt(lhs[:low_rows, :768], b_low[...]), 0.0)
    place(lhs.at[:low_rows], 768, 256, low, 128)
    deep = jnp.maximum(nt(lhs[:low_rows, 768:1536], b_deep[...]), 0.0)
    for c in range(2):
        part = deep[:, c * 128 : (c + 1) * 128]
        half[pl.ds(0, low_rows, stride=2), :] = part
        half[pl.ds(1, low_rows, stride=2), :] = part
        raised[:, c * 128 : (c + 1) * 128] = half[...]
    place(wide, 1536, 256, raised[...], 256)
    wide[:, 2304:] = taps_apart(nt(lanes(wide, (640, 256), (1792, 256)), b_pool[256:]), 256)
    halves = []
    for x in range(2):
        cells = [(ky * 512 + x * 256, 256) for ky in range(3)]
        cells += [(1536 + ky * 256 + x * 128, 128) for ky in range(3)]
        bands = lanes(b_up, (0, 1152), (1152 + x * 128, 128))
        halves.append(jnp.maximum(nt(lanes(wide, *cells, (2304 + x * 128, 128)), bands), 0.0))
    joined = jnp.concatenate(halves, axis=1).astype(BF)
    total = jnp.zeros((256, 128), F32)
    for q in range(planes):
        total = total + nt(joined[q * 256 : (q + 1) * 256], b_last[2 * rim + q])
    vol[0:8] = jnp.zeros((8, 128), F32)
    vol[264:272] = jnp.zeros((8, 128), F32)
    vol[8:264] = total
    for z in range(NZ):
        window = vol[z * 32 : z * 32 + 48]
        if before_ref is not None:
            window = window + before_ref[z].astype(F32)
        out_ref[z] = window.astype(BF)


def volume_weights_kernel(w_ref, b_rest, b_mid, b_skip, b_rise):
    edge = [nn(w_ref[kxy, 72:88], lane_spread(16, 8, 0, 256)) for kxy in range(9)]
    spread = lane_spread(16, 8, 0, 128)
    w_mid, w_low, w_skip = (
        [nn(w_ref[kxy, at : at + 24], spread) for kxy in range(9)] for at in (0, 24, 48)
    )
    w_rise = [nn(w_ref[kxy, 48:72], lane_spread(16, 8, 8, 128)) for kxy in range(9)]
    xi = iota((32, 256), 0)
    xo = iota((32, 256), 1) // 8
    for ky in range(3):
        for kz in range(3):
            plain = jnp.zeros((32, 256), F32)
            mirror = jnp.zeros((32, 256), F32)
            for kx in range(3):
                tap = edge[kx * 3 + ky][kz : kz + 1]
                plain = jnp.where(xi == xo + (kx - 1), tap, plain)
                mirror = jnp.where(xi == (32 - kx) - xo, tap, mirror)
            at = kz * 32
            b_rest[ky, at : at + 32, :256] = plain.astype(BF)
            b_rest[ky, at : at + 32, 256:512] = mirror.astype(BF)
        b_rest[ky, 96:128, :512] = jnp.zeros((32, 512), BF)
    for ky in range(3):
        for kz in range(3):
            for w, b_ref in ((w_mid, b_mid), (w_skip, b_skip)):
                taps = [stacked(w[kx * 3 + ky], kz, 8) for kx in range(3)]
                for side, part in enumerate(band_parts(taps, 8)):
                    at = (kz * 3 + side) * 128
                    b_ref[ky, :, at : at + 128] = part
            taps = [stacked(w_low[kx * 3 + ky], kz, 8) for kx in range(3)]
            same_level(b_rest.at[ky], 512 + kz * 128, 1, taps, 8)
            taps = [stacked(w_rise[kx * 3 + ky], kz, 8) for kx in range(3)]
            from_coarse(b_rise, (ky,), kz * 128, 2, 1, taps, 8)
    w_out = edge[0][8:16].astype(BF)
    row_r = iota((128, 256), 0)
    cell = iota((128, 256), 1) // 8
    pick = (iota((128, 8), 1) == (iota((128, 8), 0) // 4) % 4 + 4 * lax.axis_index("rep"))
    w_rows = nn(pick.astype(F32).astype(BF), w_out)
    x_row = (row_r // 16) * 4 + row_r % 4
    b_rest[0, :, 896:] = jnp.where(cell == x_row, w_rows, 0.0).astype(BF)
    b_rest[1, :, 896:] = jnp.where(31 - cell == x_row, w_rows, 0.0).astype(BF)


def segment_kernel(v_ref, b_rest, b_mid, b_skip, b_rise, out_ref, vz, vl, h1l, pool, ql, rise, l4):
    at_i, at_z, at_c = (lax.axis_index(name) for name in ("i", "z", "c"))
    out_lane = iota((128, 512), 1)
    select = (
        (iota((128, 512), 0) == (out_lane // 128) * 32 + out_lane % 32) & (out_lane % 128 < 96)
    ).astype(F32).astype(BF)
    vz[...] = jnp.zeros(vz.shape, F32)
    for src in range(NZ):
        spread_v = nn(v_ref[src], select)
        for q in range(4):
            z_row = 8 + 2 * src + q
            if q >= 2:
                if src >= 5:
                    z_row = 2 * src + (q - 2) - 8
                elif src <= 2:
                    z_row = 24 + 2 * src + (q - 2)
                else:
                    continue
            vz[pl.ds(z_row, 48, stride=32), :] = spread_v[:, q * 128 : (q + 1) * 128]
    v = vz[...]
    lane = iota(v.shape, 1)
    v = jnp.where(lane < 32, rolled(v, 1), jnp.where(lane < 64, v, rolled(v, -1)))
    v = v.astype(BF).reshape(48, 32, 128)
    for ky in range(3):
        vl[:, :, ky * 128 : (ky + 1) * 128] = v[2 + ky : 44 + ky]

    z_base = 128 * at_c + 16 * at_i - 8
    y_base = 32 * at_z

    def inside(y_count, y_first, z_count, z_first, limit):
        z = iota((z_count, 128), 0) + z_first
        rows = ((z >= 0) & (z < limit)).astype(F32)
        return jnp.concatenate(
            [
                rows * jnp.where((y_first + y >= 0) & (y_first + y < limit), 1.0, 0.0)
                for y in range(y_count)
            ],
            axis=0,
        )

    def masked(v, mask):
        return jnp.maximum(v, 0.0) * jnp.concatenate([mask] * (v.shape[1] // 128), axis=1)

    part = 14
    for step in range(3):
        y0 = step * part
        n = part * 32
        h1 = nn(vl[y0 : y0 + part].reshape(n, 384), b_rest[:, :, :512].reshape(384, 512))
        mask = inside(part, y_base - 5 + y0, 32, z_base, 256)
        for copy in range(2):
            h = masked(h1[:, copy * 256 : (copy + 1) * 256], mask)
            for kz in range(3):
                moved = rolled(h, -(3 + kz)).reshape(part, 32, 256)[:, :24].reshape(part * 24, 256)
                rows = slice(y0 * 24, (y0 + part) * 24)
                h1l[copy, rows, kz * 256 : (kz + 1) * 256] = moved.astype(BF)

    pool_t = jnp.concatenate([pool_matrix(8, 0), pool_matrix(8, 1)], axis=1)
    logits = jnp.zeros((128, 512), F32)
    for copy in range(2):
        rows = jnp.concatenate([h1l[copy, ky * 24 : ky * 24 + 960] for ky in range(3)], axis=1)
        bands = jnp.concatenate([two_blocks(b_mid, ky) for ky in range(3)], axis=1)
        h2 = masked(nt(rows, bands), inside(40, y_base - 4, 24, z_base + 4, 256))
        fine = nt(h2.astype(BF), pool_t).reshape(20, 2, 24, 128)
        filled = [fine[:, 0] + fine[:, 1], jnp.zeros((20, 8, 128), F32)]
        pool[...] = jnp.concatenate(filled, axis=1).reshape(640, 128)
        for kz in range(3):
            moved = rolled(h2, -(3 + kz)).reshape(40, 24, 256)
            l4[copy, :, :, kz * 256 : (kz + 1) * 256] = moved[3:37, :16].astype(BF)
        q = 0.125 * (pool[pl.ds(0, 320, stride=2), :] + pool[pl.ds(1, 320, stride=2), :])
        for kz, steps in enumerate((1, 0, -1)):
            moved = rolled(q, steps) if steps else q
            ql[:, :, kz * 128 : (kz + 1) * 128] = moved.astype(BF).reshape(20, 16, 128)
        rows = jnp.concatenate([ql[ky : ky + 18].reshape(288, 384) for ky in range(3)], axis=1)
        acc = nt(rows, jnp.concatenate([b_rest[ky, :, 512:896] for ky in range(3)], axis=1))
        h3 = masked(
            acc, inside(18, 16 * at_z - 1, 16, 64 * at_c + 8 * at_i - 2, 128)
        )
        rise[pl.ds(0, 288, stride=2), :] = h3
        rise[pl.ds(1, 288, stride=2), :] = h3
        r = rise[...]
        for kz in range(3):
            moved = rolled(r, -(3 + kz)).reshape(18, 32, 128)[:, :16].astype(BF)
            for slot in range(34):
                l4[copy, slot, :, 768 + kz * 128 : 896 + kz * 128] = moved[(slot + 3) // 2 - 1]
        at_rows = [slice(ky, ky + 32) for ky in range(3)]
        rows = [l4[copy, at, :, :768].reshape(512, 768) for at in at_rows]
        rows += [l4[copy, at, :, 768:].reshape(512, 384) for at in at_rows]
        bands = [two_blocks(b_skip, ky) for ky in range(3)] + [b_rise[ky] for ky in range(3)]
        h4 = nt(jnp.concatenate(rows, axis=1), jnp.concatenate(bands, axis=1))
        h4 = jnp.maximum(h4, 0.0).astype(BF)
        logits = logits + nt(b_rest[copy, :, 896:], h4)
    out_ref[...] = (0.5 * logits).astype(BF).reshape(NI, 16, 512)


def arrange_kernel(parts_ref, out_ref):
    lane = iota((16, 128), 1) // 16
    for o in range(4):
        parts = [parts_ref[src, :, o * 128 : (o + 1) * 128].astype(F32) for src in range(NI)]
        for bit in (1, 2, 4):
            upper = (lane & bit) != 0
            for low in range(NI):
                if low & bit == 0:
                    first, second = parts[low], parts[low | bit]
                    parts[low] = jnp.where(upper, pltpu.roll(second, 16 * bit, 1), first)
                    parts[low | bit] = jnp.where(upper, second, pltpu.roll(first, 128 - 16 * bit, 1))
        for y in range(8):
            out_ref[pl.ds(o * 8 + y, 16, stride=32), :] = parts[y]


def call(kernel, out_shape, scratch, megabytes, *args):
    spec = pl.BlockSpec(memory_space=pltpu.VMEM)
    return pl.pallas_call(
        kernel,
        out_shape=out_shape,
        in_specs=[spec] * len(args),
        out_specs=jax.tree.map(lambda _: spec, out_shape),
        scratch_shapes=scratch,
        compiler_params=pltpu.CompilerParams(vmem_limit_bytes=megabytes * 1024 * 1024),
    )(*args)


def bf(*shape):
    return jax.ShapeDtypeStruct(shape, BF)


def table(lead, rows, width, *weights):
    total = 0
    for at, w in weights:
        size = w.shape
        total = total + jnp.pad(
            w, ((0, lead - size[0]), (at, rows - at - size[1]), (0, width - size[2]))
        )
    return total


def taps2(w):
    return w.transpose(2, 3, 0, 1).reshape(3, -1, w.shape[1])


def taps3(w):
    return w.transpose(2, 3, 4, 0, 1).reshape(9, -1, w.shape[1])


def rim_pairs():
    def index(i, z, c):
        return (i * NZ + z) * NC + c

    pairs = []
    for z in range(NZ):
        if z >= NZ - 3:
            step, edge, wrapped = 1, NI - 1, 0
        elif z <= 2:
            step, edge, wrapped = -1, 0, 1
        else:
            continue
        for i in range(NI):
            for c in range(NC):
                if i != edge:
                    pairs.append((index(i, z, c), index(i + step, z, c)))
                elif c == wrapped:
                    pairs.append((index(i, z, c), index((i + step) % NI, z, 1 - c)))
    return pairs


def denoise(rim, planes, before, weights):
    args = (planes, before) if rim else (planes,)
    count = 2
    vmem = pltpu.VMEM
    return call(
        functools.partial(denoise_kernel, rim),
        bf(NZ, 48, 128),
        [
            vmem((count * 256, 1664), BF),
            vmem((count * 256, 2560), BF),
            vmem((count * 128, 256), F32),
            vmem((count * 256, 128), F32),
            vmem((count * 256, 256), F32),
            vmem((272, 128), F32),
        ],
        24,
        *args,
        *weights,
    )


def per_device(
    noisy, w2_in, w2_mid, w2_low, w2_deep, w2_up, w2_out, w3_in, w3_mid, w3_low, w3_up, w3_out
):
    near = noisy.reshape(2, 32, 256)
    far = lax.ppermute(near, "c", [(0, 1), (1, 0)])
    kernels = ((0, w2_mid), (48, w2_low), (96, w2_deep), (144, w2_up))
    taps = [(at, taps2(w)) for at, w in kernels]
    taps += [(192, w2_in.transpose(1, 2, 3, 0)[0]), (195, w2_out[None])]
    weights = call(
        plane_weights_kernel,
        [
            bf(128, 640),
            bf(256, 1024),
            bf(256, 768),
            bf(256, 768),
            bf(256, 1408),
            bf(512, 512),
            bf(4, 128, 512),
        ],
        [],
        16,
        table(3, 208, 32, *taps),
    )
    far, weights = lax.optimization_barrier((far, weights))
    second = lax.axis_index("c") == 1
    own = jnp.stack([jnp.where(second, far[1], near[0]), jnp.where(second, near[1], far[0])])
    rim = lax.ppermute(own, ("i", "z", "c"), rim_pairs())
    volume = denoise(0, own, None, weights)
    volume = denoise(1, rim, volume, weights)
    taps = [(at, taps3(w)) for at, w in ((0, w3_mid), (24, w3_low), (48, w3_up))]
    taps += [(72, w3_in.transpose(1, 2, 3, 4, 0).reshape(9, 3, 8)), (80, w3_out[None])]
    bands = call(volume_weights_kernel, [bf(3, 128, 1152), bf(3, 128, 1152), bf(3, 128, 1152), bf(3, 256, 384)], [], 16, table(9, 88, 16, *taps))
    window = lax.all_to_all(volume, "z", 0, 0, tiled=True)
    vmem = pltpu.VMEM
    logits = call(
        segment_kernel,
        bf(NI, 16, 512),
        [
            vmem((48 * 32, 128), F32),
            vmem((42, 32, 384), BF),
            vmem((2, 42 * 24, 768), BF),
            vmem((640, 128), F32),
            vmem((20, 16, 384), BF),
            vmem((576, 128), F32),
            vmem((2, 34, 16, 1152), BF),
        ],
        24,
        window,
        *bands,
    )
    parts = lax.all_to_all(logits, "i", 0, 0, tiled=True)
    out = call(arrange_kernel, jax.ShapeDtypeStruct((512, 128), F32), [], 4, parts)
    return out.reshape(1, 4, 4, 32, 128)


def solution(mesh):
    finer = Mesh(mesh.devices.reshape(2, NI, NZ, NC), ("rep", "i", "z", "c"))
    brick = ("i", "z", "c")
    placed = (P(None, brick, None, None),) + (P(),) * 11
    return jax.shard_map(
        per_device,
        mesh=finer,
        in_specs=placed,
        out_specs=P(brick, "rep", None, None, None),
        check_vma=False,
    )
```
